32 devices in a mesh: branch: 2 (over y), trow: 2 (over x), tcol: 8 (over z, core).
Axes of the slice: x: 2, y: 2, z: 4, core: 2. Of those that a mesh axis runs over, the one named last changes fastest.
Arguments:
- latent: bfloat16 [2, 2, 16, 64, 1152], P('branch', None, 'trow', 'tcol'), may hold values from -6 to 6
- modulation: float32 [2, 3, 1152], replicated, may hold values from -2 to 2
- w_query: bfloat16 [2, 1152, 576], P('branch', None, 'tcol'), may hold values from -0.176776695 to 0.176776695
- w_keyval: bfloat16 [2, 1152, 1152], P('branch', None, 'tcol'), may hold values from -3.8301617 to 3.8301617
- w_out: bfloat16 [2, 576, 1152], P('branch', 'tcol'), may hold values from -0.25 to 0.25
- w_zero: bfloat16 [1152, 1152], P(None, 'tcol'), may hold values from -0.1875 to 0.1875
Outputs:
- hidden_out: bfloat16 [2, 2, 16, 64, 1152], P('branch', None, 'trow', 'tcol')
The draws below stay inside these ranges and needn't reach their ends.
All inputs are finite; a program needn't handle non-finite values.
Results may differ from the reference program's by a relative error of at most 0.0075.
Values may be sent and summed in bfloat16 or wider, within the bound.
No kernel may reach another device: no remote copies, remote signals or barrier semaphores. Data moves between devices by JAX's collectives and lax.ppermute only.
A program may use at most 128 MiB of HBM per device.

```python
import math
import jax
import jax.numpy as jnp
from jax import lax

D = 1152
HD = 72
HEADS = 8
WIN = 13
IMGS = 2
HW = 576
H = 16
W = 64


def clipped_normal(key, full_shape, bound_abs):
    return jnp.clip(jax.random.normal(key, full_shape, jnp.float32), -bound_abs, bound_abs)


def query_weights(key):
    return clipped_normal(jax.random.fold_in(key, 101), (2, D, HW), 5.0) / math.sqrt(D)


def draw_w_query(key, part):
    return query_weights(key).astype(jnp.bfloat16)


def draw_w_keyval(key, part):
    noise_part = clipped_normal(jax.random.fold_in(key, 102), (2, D, 2 * HW), 5.0) / math.sqrt(D)
    return noise_part.astype(jnp.bfloat16)


def draw_latent(key, part):
    fresh_draw = clipped_normal(jax.random.fold_in(key, 201), (2, IMGS, H, W, D), 6.0)
    return fresh_draw.astype(jnp.bfloat16)


def block_levels(stream_key, extent, shards, least, top_value):
    factor_of, own = 1.0, jax.random.fold_in(stream_key, 6)
    for dim, parts in shards:
        draws = jnp.exp(jax.random.uniform(jax.random.fold_in(own, dim), (parts,), jnp.float32, least / len(shards), top_value / len(shards)))
        factor_of = factor_of * jnp.repeat(draws, extent[dim] // parts).reshape([-1 if axis == dim else 1 for axis in range(len(extent))])
    return factor_of


def scatter_about(own_key, shape, scale, most, cuts=(), held_as=jnp.bfloat16):
    drawn = scale * jax.random.normal(own_key, shape, jnp.float32)
    if cuts:
        drawn = drawn * block_levels(own_key, shape, cuts, -0.22, 0.18)
    return jnp.clip(drawn, -most, most).astype(held_as)


def setup_inputs(seed: int = 0) -> dict:
    arg_keys = jax.random.split(jax.random.key(seed), 7)
    return {
        "latent": draw_latent(jax.random.fold_in(arg_keys[6], 71), 0),
        "modulation": scatter_about(arg_keys[1], (2, 3, D), 0.5, 2.0, (), jnp.float32),
        "w_query": draw_w_query(jax.random.fold_in(arg_keys[6], 71), 0),
        "w_keyval": draw_w_keyval(jax.random.fold_in(arg_keys[6], 71), 0),
        "w_out": scatter_about(arg_keys[4], (2, HW, D), HW ** -0.5, 0.25, ((0, 2), (1, 8))),
        "w_zero": scatter_about(arg_keys[5], (D, D), D ** -0.5, 0.1875, ((1, 8),)),
    }


def modulate(hidden, shift_scale):
    average = lax.optimization_barrier(jnp.mean(hidden, axis=-1, keepdims=True))
    centred = hidden - average
    variance = lax.optimization_barrier(jnp.mean(centred * centred, axis=-1, keepdims=True))
    return (centred * lax.rsqrt(variance + 1e-06) * (1.0 + shift_scale[1]) + shift_scale[0]).astype(jnp.bfloat16)

def neighbor_attention(queries, key_values):
    radius = WIN // 2
    scaling = 1.0 / math.sqrt(HD)
    query_all = queries.astype(jnp.float32).reshape(IMGS, H, W, HEADS, HD)
    key_part = key_values[..., :HW].reshape(IMGS, H, W, HEADS, HD)
    value_part = key_values[..., HW:].reshape(IMGS, H, W, HEADS, HD)
    row_starts = jnp.clip(jnp.arange(H) - radius, 0, H - WIN).astype(jnp.int32)
    col_starts = jnp.clip(jnp.arange(W) - radius, 0, W - WIN).astype(jnp.int32)

    def shifted(source, offset):
        row_offset = (offset // WIN).astype(jnp.int32)
        col_offset = (offset % WIN).astype(jnp.int32)
        picked = jnp.take(source, row_starts + row_offset, axis=1)
        picked = jnp.take(picked, col_starts + col_offset, axis=2)
        return picked.astype(jnp.float32)

    def scores_at(offset):
        return lax.optimization_barrier(jnp.sum(query_all * shifted(key_part, offset), axis=-1)) * scaling

    def first_pass(offset, carry):
        running_max, totals = carry
        current = scores_at(offset)
        new_max = jnp.maximum(running_max, current)
        totals = totals * jnp.exp(running_max - new_max) + jnp.exp(current - new_max)
        return (new_max, totals)
    start_max = jnp.full((IMGS, H, W, HEADS), -1e+30, jnp.float32)
    start_total = jnp.zeros((IMGS, H, W, HEADS), jnp.float32)
    highest, totals = lax.fori_loop(0, WIN * WIN, first_pass, (start_max, start_total))

    def second_pass(offset, accumulated):
        weights = (jnp.exp(scores_at(offset) - highest) / totals).astype(jnp.bfloat16).astype(jnp.float32)
        return accumulated + weights[..., None] * shifted(value_part, offset)
    accumulated = lax.fori_loop(0, WIN * WIN, second_pass, jnp.zeros((IMGS, H, W, HEADS, HD), jnp.float32))
    return accumulated.reshape(IMGS, H, W, HW).astype(jnp.bfloat16)

def run_copy(hidden, shift_scale, weight_q, weight_kv, weight_o):
    flattened = modulate(hidden, shift_scale).reshape(-1, D)
    queries = jnp.dot(flattened, weight_q, preferred_element_type=jnp.float32).astype(jnp.bfloat16)
    key_values = jnp.dot(flattened, weight_kv, preferred_element_type=jnp.float32).astype(jnp.bfloat16)
    attended = neighbor_attention(queries.reshape(IMGS, H, W, HW), key_values.reshape(IMGS, H, W, 2 * HW))
    projected = jnp.dot(attended.reshape(-1, HW), weight_o, preferred_element_type=jnp.float32)
    return (hidden + shift_scale[2] * projected.reshape(hidden.shape)).astype(jnp.bfloat16)

def reference(latent, modulation, w_query, w_keyval, w_out, w_zero):
    base_rows = latent[0].astype(jnp.float32)
    control_in = base_rows + latent[1].astype(jnp.float32)
    control_out = run_copy(control_in, modulation[1], w_query[1], w_keyval[1], w_out[1])
    residual = jnp.dot(control_out.reshape(-1, D), w_zero, preferred_element_type=jnp.float32).astype(jnp.bfloat16)
    base_in = base_rows + residual.reshape(base_rows.shape).astype(jnp.float32)
    base_out = run_copy(base_in, modulation[0], w_query[0], w_keyval[0], w_out[0])
    return jnp.stack([base_out, control_out])
```

```python
import functools
import math

import jax
import jax.numpy as jnp
from jax import lax
from jax.experimental import pallas as pl
from jax.experimental.pallas import tpu as pltpu
from jax.sharding import PartitionSpec as P

D = 1152
HD = 72
HEADS = 8
WIN = 13
HW = 576


def padded(block, sides, width):
    for axis, dim in sides:
        count = lax.axis_size(axis)
        forward = [(i, i + 1) for i in range(count - 1)]
        backward = [(target, source) for source, target in forward]
        low = lax.ppermute(
            lax.slice_in_dim(block, block.shape[dim] - width, None, axis=dim), axis, forward
        )
        high = lax.ppermute(lax.slice_in_dim(block, 0, width, axis=dim), axis, backward)
        block = jnp.concatenate([low, block, high], axis=dim)
    return block


def shifted(block, axis, distance):
    devices = range(lax.axis_size(axis))
    route = [(i - distance, i) for i in devices if i - distance in devices]
    return lax.ppermute(block, axis, route)


def modulate(hidden, shift_scale):
    average = jnp.mean(hidden, axis=-1, keepdims=True)
    centred = hidden - average
    variance = jnp.mean(centred * centred, axis=-1, keepdims=True)
    return (centred * lax.rsqrt(variance + 1e-06) * (1.0 + shift_scale[1]) + shift_scale[0]).astype(
        jnp.bfloat16
    )


def block_mask(row_first, col_first, total_rows, total_cols, key_count):
    query_edge = 8
    radius = WIN // 2
    key_side = query_edge + 2 * radius
    offsets = jnp.arange(query_edge)
    reaches = jnp.arange(key_side)
    row_starts = jnp.clip(row_first + offsets - radius, 0, total_rows - WIN)
    key_rows = row_first - radius + reaches
    row_inside = (key_rows[None, :] >= row_starts[:, None]) & (
        key_rows[None, :] < row_starts[:, None] + WIN
    )
    col_starts = jnp.clip(col_first + offsets - radius, 0, total_cols - WIN)
    key_cols = col_first - radius + reaches
    col_inside = (key_cols[None, :] >= col_starts[:, None]) & (
        key_cols[None, :] < col_starts[:, None] + WIN
    )
    joined = row_inside[:, None, :, None] & col_inside[None, :, None, :]
    joined = joined.reshape(query_edge * query_edge, key_side * key_side)
    filler = jnp.zeros((query_edge * query_edge, key_count - key_side * key_side), dtype=jnp.bool_)
    return jnp.concatenate([joined, filler], axis=1)


def edge_keys(key_values):
    radius = WIN // 2
    return padded(key_values, (("trow", 1), ("tcol", 2)), radius)


def attend_tile(queries, extended, row_anchor, col_anchor, total_rows, total_cols):
    images, tile_rows, tile_cols = (queries.shape[0], queries.shape[1], queries.shape[2])
    query_edge = 8
    radius = WIN // 2
    key_side = query_edge + 2 * radius
    key_count = (key_side * key_side + 127) // 128 * 128
    across = tile_cols // query_edge
    block_count = tile_rows // query_edge * across
    scaling = 1.0 / math.sqrt(HD)

    def one_block(position):
        row_block = position // across * query_edge
        col_block = position % across * query_edge
        query_block = queries
        query_block = query_block.reshape(images, query_edge * query_edge, HEADS, HD)
        key_block = extended
        key_block = key_block.reshape(images, key_side * key_side, 2 * HW)
        key_block = jnp.pad(key_block, ((0, 0), (0, key_count - key_side * key_side), (0, 0)))
        key_heads = key_block[..., :HW].reshape(images, key_count, HEADS, HD)
        value_heads = key_block[..., HW:].reshape(images, key_count, HEADS, HD)
        allowed = block_mask(
            row_anchor + row_block, col_anchor + col_block, total_rows, total_cols, key_count
        )
        scores = (
            jnp.einsum(
                "iqhd,ikhd->ihqk", query_block, key_heads, preferred_element_type=jnp.float32
            )
            * scaling
        )
        scores = jnp.where(allowed[None, None], scores, -1e30)
        highest = jnp.max(scores, axis=-1, keepdims=True)
        raised = jnp.exp(scores - highest)
        totals = jnp.sum(raised, axis=-1, keepdims=True)
        weights = (raised / totals).astype(jnp.bfloat16)
        blended = jnp.einsum(
            "ihqk,ikhd->iqhd", weights, value_heads, preferred_element_type=jnp.float32
        )
        return blended.astype(jnp.bfloat16).reshape(images, query_edge, query_edge, HW)

    result = lax.map(one_block, jnp.arange(block_count))
    result = result.reshape(tile_rows // query_edge, across, images, query_edge, query_edge, HW)
    return result.transpose(2, 0, 3, 1, 4, 5).reshape(images, tile_rows, tile_cols, HW)


def run_block(active, hidden, shift_scale, weight_q, weight_kv, weight_o):
    images, tile_rows, tile_cols = (hidden.shape[0], hidden.shape[1], hidden.shape[2])
    tokens = images * tile_rows * tile_cols

    def project():
        flattened = modulate(hidden, shift_scale).reshape(tokens, D)
        queries = jnp.dot(flattened, weight_q, preferred_element_type=jnp.float32).astype(
            jnp.bfloat16
        )
        key_values = jnp.dot(flattened, weight_kv, preferred_element_type=jnp.float32).astype(
            jnp.bfloat16
        )
        return (queries, key_values)

    def nothing():
        return (jnp.zeros((tokens, HW), jnp.bfloat16), jnp.zeros((tokens, 2 * HW), jnp.bfloat16))

    queries, key_values = lax.cond(active, project, nothing)
    extended = edge_keys(key_values.reshape(images, tile_rows, tile_cols, 2 * HW))
    row_anchor = lax.axis_index("trow") * tile_rows
    col_anchor = lax.axis_index("tcol") * tile_cols
    total_rows = tile_rows * lax.axis_size("trow")
    total_cols = tile_cols * lax.axis_size("tcol")

    def finish():
        attended = attend_tile(
            queries.reshape(images, tile_rows, tile_cols, HW),
            extended,
            row_anchor,
            col_anchor,
            total_rows,
            total_cols,
        )
        projected = jnp.dot(
            attended.reshape(tokens, HW), weight_o, preferred_element_type=jnp.float32
        )
        return (hidden + shift_scale[2] * projected.reshape(hidden.shape)).astype(jnp.bfloat16)

    def vacant():
        return jnp.zeros(hidden.shape, jnp.bfloat16)

    return lax.cond(active, finish, vacant)


def zero_project(control_out, weight_z):
    flattened = control_out.reshape(-1, D)
    return (
        jnp.dot(flattened, weight_z, preferred_element_type=jnp.float32)
        .astype(jnp.bfloat16)
        .reshape(control_out.shape)
    )


def on_device(latent, modulation, w_query, w_keyval, w_out, w_zero):
    sources = (w_query, w_keyval, w_out)
    weight_q, weight_kv, weight_o, weight_z = (
        lax.all_gather(sources[0], "tcol", axis=2, tiled=True),
        lax.all_gather(sources[1], "tcol", axis=2, tiled=True),
        lax.all_gather(sources[2], "tcol", axis=1, tiled=True),
        lax.all_gather(w_zero, "tcol", axis=1, tiled=True),
    )
    branch_index = lax.axis_index("branch")
    is_control = branch_index == 1
    own_copy = latent[0]
    shift_scale = lax.dynamic_index_in_dim(modulation, branch_index, 0, keepdims=False)
    received = shifted(own_copy, "branch", 1)
    control_in = own_copy.astype(jnp.float32) + received.astype(jnp.float32)
    control_out = run_block(
        is_control, control_in, shift_scale, weight_q[0], weight_kv[0], weight_o[0]
    )

    def with_projection():
        return zero_project(control_out, weight_z)

    def without_projection():
        return jnp.zeros(control_out.shape, jnp.bfloat16)

    residual = lax.cond(is_control, with_projection, without_projection)
    returned = shifted(residual, "branch", -1)
    base_in = own_copy.astype(jnp.float32) + returned.astype(jnp.float32)
    base_out = run_block(
        jnp.logical_not(is_control), base_in, shift_scale, weight_q[0], weight_kv[0], weight_o[0]
    )
    return jnp.where(is_control, control_out, base_out)[None]


AXES = ("branch", "trow", "tcol")
SLOT = 80
ORDER = (0, 3, 1, 2)


def routes(sizes, move):
    found = []
    for b in range(sizes[0]):
        for r in range(sizes[1]):
            for t in range(sizes[2]):
                target = move(b, r, t)
                if target is not None:
                    found.append((place_of(sizes, b, r, t), place_of(sizes, *target)))
    return found


def place_of(sizes, b, r, t):
    return (b * sizes[1] + r) * sizes[2] + t


def send(block, sizes, move):
    return lax.ppermute(block, AXES, routes(sizes, move))


def after(block, *earlier):
    return lax.optimization_barrier((block,) + earlier)[0]


def kernel_call(body, outs, args, scratch=(), copies=0, stay=False, micros=0):
    def space(a):
        if a.dtype == jnp.int32:
            return pltpu.SMEM
        return pltpu.VMEM if a.dtype == jnp.float32 else pl.ANY

    buffers = [pltpu.VMEM(shape, kind) for shape, kind in scratch]
    return pl.pallas_call(
        body,
        out_shape=[jax.ShapeDtypeStruct(shape, kind) for shape, kind in outs],
        in_specs=[pl.BlockSpec(memory_space=space(a)) for a in args],
        out_specs=[pl.BlockSpec(memory_space=pl.ANY if stay else pltpu.VMEM) for _ in outs],
        scratch_shapes=buffers + [pltpu.SemaphoreType.DMA((copies,))],
        compiler_params=pltpu.CompilerParams(vmem_limit_bytes=32 * 1024 * 1024),
        cost_estimate=pl.CostEstimate(
            flops=0, bytes_accessed=1 + 3_700_000 * micros, transcendentals=0
        ),
    )(*args)


def begin(copies, done, first=0):
    started = []
    for n, (source, target) in enumerate(copies):
        copy = pltpu.make_async_copy(source, target, done.at[first + n])
        copy.start()
        started.append(copy)
    return started


def finish(started):
    for copy in started:
        copy.wait()


def dot_rows(left, right):
    return lax.dot_general(left, right, (((1,), (1,)), ((), ())), preferred_element_type=jnp.float32)


def rows_at(start, count):
    return pl.ds(pl.multiple_of(start, 16), count)


def stack_kernel(*refs):
    *pieces, stacked, done = refs
    finish(begin([(piece, stacked.at[n]) for n, piece in enumerate(pieces)], done))


def norm_kernel(total_rows, total_cols, spot, own, far, mod, normed, bias, total, first, second, done):
    copies = [(own, first), (far, second)]
    started = begin(copies, done)
    radius = WIN // 2
    query = lax.broadcasted_iota(jnp.int32, bias.shape, 0)
    key = lax.broadcasted_iota(jnp.int32, bias.shape, 1)
    base = spot[4]
    row_start = jnp.clip((query >> 3) - radius, 0, total_rows - WIN)
    col_start = jnp.clip(base + (query & 7) - radius, 0, total_cols - WIN)
    key_row = (key & 127) >> 3
    outward = 2 * spot[3] - 1
    key_col = base + (1 - (key >> 7)) * outward * 8 + (key & 7)
    inside = (
        (key_row >= row_start)
        & (key_row < row_start + WIN)
        & (key_col >= col_start)
        & (key_col < col_start + WIN)
    )
    bias[...] = jnp.where(inside, 0.0, -1e30)
    finish(started)
    for image in range(own.shape[0]):
        hidden = first[image].astype(jnp.float32) + second[image].astype(jnp.float32)
        total[image] = hidden
        normed[image] = modulate(hidden, mod)


def in_order(origin):
    return (origin % 2) * 2 + origin // 2


def arrange_keyvals(link, stacks, weight):
    for at in range(2):
        for step in range(4):
            origin = link ^ ORDER[step]
            slot = (1 - origin // 2) * 4 + at * 2 + origin % 2
            weight[rows_at(slot * SLOT, SLOT), :] = stacks[at, step, :SLOT]


def arrange_heads(link, stack, first_row, weight):
    for step in range(4):
        start = first_row + in_order(link ^ ORDER[step]) * SLOT
        weight[rows_at(start, SLOT), :] = stack[step]


def arrange_queries(link, stacks, row, weight):
    start = weight.shape[0] - 4 * SLOT
    weight[8 * SLOT : start, :] = jnp.zeros((start - 8 * SLOT, weight.shape[1]), weight.dtype)
    arrange_heads(link, stacks.at[row, :, SLOT:], start, weight)


def project_kernel(spot, normed, normed_other, mine, other, keyval, query, stacks, weight, both, done):
    row, link, core = (spot[1], spot[2], spot[3])
    copies = [(mine, stacks.at[core]), (other, stacks.at[1 - core])]
    for image in range(normed.shape[0]):
        copies.append((normed.at[image], both.at[image, row]))
        copies.append((normed_other.at[image], both.at[image, 1 - row]))
    finish(begin(copies, done))
    arrange_keyvals(link, stacks, weight)
    arrange_queries(link, stacks, row, weight)
    tokens = both[...].reshape(-1, both.shape[3])
    projected = dot_rows(tokens, weight[...]).astype(keyval.dtype)
    keyval[...] = projected[:, : keyval.shape[1]]
    query[...] = projected[:, keyval.shape[1] :]


def attend_kernel(spot, queries, outer, here, inner, bias, out, query_rows, keyvals, done):
    scaling = 1.0 / math.sqrt(HD)
    tokens = bias.shape[0]
    images = out.shape[0] // tokens
    copies = [(queries, query_rows)]
    copies += [(part, keyvals.at[index]) for index, part in enumerate((outer, here, inner))]
    finish(begin(copies, done))
    key_lanes = queries.shape[1]
    first_key = here.shape[1] - key_lanes
    heads = out.shape[1] // SLOT
    pad = key_lanes - heads * SLOT
    value_lanes = (out.shape[1] + 127) // 128 * 128
    query_lane = lax.broadcasted_iota(jnp.int32, (tokens, key_lanes), 1) - pad
    value_lane = lax.broadcasted_iota(jnp.int32, (tokens, value_lanes), 1)

    def within(lane, head):
        return (lane >= head * SLOT) & (lane < (head + 1) * SLOT)

    for image in range(images):
        rows = slice(image * tokens, (image + 1) * tokens)
        keys = jnp.concatenate([keyvals[n, rows, first_key:] for n in range(3)], axis=0)
        values = jnp.concatenate([keyvals[n, rows, :value_lanes] for n in range(3)], axis=0)
        query = query_rows[rows, :].astype(jnp.float32)
        split = [jnp.where(within(query_lane, head), query, 0.0) for head in range(heads)]
        scores = dot_rows(jnp.concatenate(split, axis=0).astype(jnp.bfloat16), keys)
        raised, sums = ([], [])
        for head in range(heads):
            part = scores[head * tokens : (head + 1) * tokens] * scaling + bias[...]
            part = jnp.exp(part - jnp.max(part, axis=-1, keepdims=True))
            sums.append(jnp.sum(part, axis=-1, keepdims=True))
            raised.append(part.astype(jnp.bfloat16))
        blended = jnp.dot(
            jnp.concatenate(raised, axis=0), values, preferred_element_type=jnp.float32
        )
        total = jnp.zeros((tokens, value_lanes), jnp.float32)
        for head in range(heads):
            part = blended[head * tokens : (head + 1) * tokens] / sums[head]
            total = jnp.where(within(value_lane, head), part, total)
        out[rows, :] = total[:, : out.shape[1]].astype(out.dtype)


def prepare_kernel(
    spot, first, first_other, zero_side, zero_corner, second, second_other, w_zero, weight,
    stacks, zeros, keyval_stacks, done,
):
    row, link, core = (spot[1], spot[2], spot[3])
    copies = [(first, stacks.at[core]), (first_other, stacks.at[1 - core])]
    copies += [(zero_side, zeros.at[core]), (zero_corner, zeros.at[1 - core])]
    copies += [(second, keyval_stacks.at[core]), (second_other, keyval_stacks.at[1 - core])]
    started = begin(copies, done)
    finish(started)
    shard = w_zero.shape[0] // 8
    for at in range(2):
        for step in range(4):
            start = (2 * (link ^ ORDER[step]) + at) * shard
            mine = start + row * (shard - SLOT)
            w_zero[rows_at(mine, SLOT), :] = stacks[at, step, :SLOT]
            other = start + (1 - row) * (shard - SLOT)
            w_zero[rows_at(other, SLOT), :] = zeros[at, step]
    arrange_keyvals(link, keyval_stacks, weight)
    arrange_queries(link, stacks, row, weight)


def middle_kernel(
    spot, own, far, side, corner, near, cross, out_mine, out_other, zero_rows, projections,
    mod, mod_base, base_in, keyval, query,
    base_rows, more_rows, heads, outs, w_out, w_zero, weight, both, done,
):
    row, link, core = (spot[1], spot[2], spot[3])
    images, tokens, _ = own.shape
    tile = images * tokens
    width = heads.shape[2]
    copies = []
    for image in range(images):
        for part, slot in ((0, row), (1, 1 - row)):
            rows = slice(part * tile + image * tokens, part * tile + (image + 1) * tokens)
            for index, ref in enumerate((near, cross)):
                copies.append((ref.at[image, slot], heads.at[index, rows]))
    copies += [(out_mine, outs.at[core]), (out_other, outs.at[1 - core])]
    copies += [(own, base_rows.at[0]), (side, base_rows.at[1])]
    copies += [(far, more_rows.at[0]), (corner, more_rows.at[1])]
    early = begin(copies, done)
    late = begin([(zero_rows, w_zero), (projections, weight)], done, len(early))
    finish(early)
    for at in range(2):
        arrange_heads(link, outs.at[at], at * width, w_out)
    projected = jnp.dot(
        heads[0], w_out[rows_at(row * width, width), :], preferred_element_type=jnp.float32
    )
    projected += jnp.dot(
        heads[1], w_out[rows_at((1 - row) * width, width), :], preferred_element_type=jnp.float32
    )

    def flat(ref):
        return ref[...].reshape(2 * tile, ref.shape[3]).astype(jnp.float32)

    base = flat(base_rows)
    out = (base + flat(more_rows) + mod[2] * projected).astype(jnp.bfloat16)
    finish(late)
    residual = dot_rows(out, w_zero[...]).astype(jnp.bfloat16)
    base = base + residual.astype(jnp.float32)
    result = modulate(base, mod_base)
    for image in range(images):
        rows = slice(image * tokens, (image + 1) * tokens)
        base_in[image] = base[rows]
        both[image, row] = result[rows]
        both[image, 1 - row] = result[tile + image * tokens : tile + (image + 1) * tokens]
    rows = both[...].reshape(2 * tile, both.shape[3])
    projected = dot_rows(rows, weight[...]).astype(keyval.dtype)
    keyval[...] = projected[:, : keyval.shape[1]]
    query[...] = projected[:, keyval.shape[1] :]


def final_kernel(spot, attended, side, mine, other, base, mod, out, near, far, outs, w_out, done):
    row, link = (spot[1], spot[2])
    images = out.shape[0]
    width = near.shape[2]
    copies = [(side, far)]
    copies += [(attended.at[image, row], near.at[image]) for image in range(images)]
    copies += [(mine, outs.at[1 - row]), (other, outs.at[row])]
    finish(begin(copies, done))
    for at in range(2):
        arrange_heads(link, outs.at[at], at * width, w_out)

    def flat(ref):
        return jnp.concatenate([ref[i] for i in range(images)], axis=0)

    projected = jnp.dot(
        flat(near), w_out[rows_at(row * width, width), :], preferred_element_type=jnp.float32
    )
    projected += jnp.dot(
        flat(far), w_out[rows_at((1 - row) * width, width), :], preferred_element_type=jnp.float32
    )
    tokens = out.shape[1]
    for image in range(images):
        rows = slice(image * tokens, (image + 1) * tokens)
        out[image] = (base[image] + mod[2] * projected[rows]).astype(out.dtype)


def paired_rows(sizes, latent, modulation, w_query, w_keyval, w_out, w_zero):
    branch = lax.axis_index("branch")
    row = lax.axis_index("trow")
    column = lax.axis_index("tcol")
    core = column % 2
    is_control = branch == 1
    is_query = core == row
    _, images, tile_rows, tile_cols, _ = latent.shape
    tile = tile_rows * tile_cols
    tokens = images * 2 * tile
    half = HEADS // 2 * SLOT
    lanes = half + half % 128
    spot = jnp.stack([branch, row, column // 2, core, column * tile_cols]).astype(jnp.int32)
    own = latent.reshape(images, tile, D)

    def everyone(b, r, t):
        return True

    def base_only(b, r, t):
        return b == 0

    def control_only(b, r, t):
        return b == 1

    def swap_cores(block, joins=everyone):
        return send(block, sizes, lambda b, r, t: (b, r, t ^ 1) if joins(b, r, t) else None)

    def swap_rows(block, joins=everyone):
        return send(block, sizes, lambda b, r, t: (b, 1 - r, t) if joins(b, r, t) else None)

    def swap_links(block, distance, joins=everyone):
        return send(
            block, sizes, lambda b, r, t: (b, r, t ^ (2 * distance)) if joins(b, r, t) else None
        )

    def padded_rows(block):
        return jnp.pad(block, ((0, SLOT - HD), (0, 0)))

    def stacked(pieces):
        shape = (len(pieces),) + pieces[0].shape
        out = [(shape, jnp.bfloat16)]
        (stack,) = kernel_call(stack_kernel, out, pieces, copies=len(pieces), stay=True)
        return stack.reshape((-1,) + shape[-2:])

    def joined(block, other):
        return jnp.concatenate([block, other], axis=0)

    keyval_piece = padded_rows(lax.dynamic_slice_in_dim(w_keyval[0].T, row * HD, HD, axis=0))
    zero_piece = lax.dynamic_slice_in_dim(
        w_zero.T, row * (w_zero.shape[1] - SLOT), SLOT, axis=0
    )
    query_or_out = padded_rows(jnp.where(is_query, w_query[0].T, w_out[0]))

    piece = joined(jnp.where(is_control, keyval_piece, zero_piece), query_or_out)
    first = [piece, swap_links(piece, ORDER[1]), swap_links(piece, ORDER[2])]
    started = after(own, piece)
    far = send(started, sizes, lambda b, r, t: (1 - b, r, t))
    corner = send(started, sizes, lambda b, r, t: (0, 1 - r, t) if b == 1 else None)
    tile_shape = (images, tile, D)
    normed, bias, hidden = kernel_call(
        functools.partial(norm_kernel, 2 * tile_rows, sizes[2] * tile_cols),
        [
            (tile_shape, jnp.bfloat16),
            ((2 * tile, 6 * tile), jnp.float32),
            (tile_shape, jnp.float32),
        ],
        (spot, own, far, modulation[1]),
        scratch=[(tile_shape, jnp.bfloat16), (tile_shape, jnp.bfloat16)],
        copies=2,
    )
    side = swap_rows(jnp.where(is_control, normed, own))
    side, corner, *first = lax.optimization_barrier((side, corner, *first))
    first.append(swap_links(first[1], ORDER[2]))
    first = stacked(first)
    first_other = swap_cores(first)
    zero_side = swap_rows(first[:, :SLOT], base_only)
    head_stack = jnp.where(is_query, first_other[:, SLOT:], first[:, SLOT:])

    def to_base(b, r, t):
        if b == 0:
            return None
        return (0, 1 - r, t ^ 1) if t % 2 == r else (0, r, t)

    out_mine = send(head_stack, sizes, to_base)
    projections = [((tokens, 2 * half), jnp.bfloat16), ((tokens, lanes), jnp.bfloat16)]
    stacks = ((2, 4, 2 * SLOT, D), jnp.bfloat16)
    half_stacks = ((2, 4, SLOT, D), jnp.bfloat16)
    projection_scratch = [
        ((2 * half + lanes, D), jnp.bfloat16),
        ((images, 2, tile, D), jnp.bfloat16),
    ]

    def neighborhood(keyval, query, joins):
        def across(b, r, t):
            target = t + 1 if t % 2 else t - 1
            return (b, r, target) if joins(b, r, t) and 0 <= target < sizes[2] else None

        outer = send(keyval, sizes, across)
        inner = swap_cores(keyval, joins)
        (attended,) = kernel_call(
            attend_kernel, [((tokens, half), jnp.bfloat16)],
            (spot, query, outer, keyval, inner, bias),
            scratch=[((tokens, lanes), jnp.bfloat16), ((3, tokens, 2 * half), jnp.bfloat16)],
            copies=4, micros=8,
        )
        return attended.reshape(images, 2, tile, half)

    def finished(attended, other_stack, base, mod, joins):
        theirs = lax.dynamic_index_in_dim(attended, 1 - row, 1, keepdims=False)
        (out,) = kernel_call(
            final_kernel, [(tile_shape, jnp.bfloat16)],
            (spot, attended, swap_rows(theirs, joins), head_stack, other_stack, base, mod),
            scratch=[
                ((images, tile, half), jnp.bfloat16),
                ((images, tile, half), jnp.bfloat16),
                half_stacks,
                ((2 * half, D), jnp.bfloat16),
            ],
            copies=3 + images,
        )
        return out

    def empty(*outs):
        return tuple(jnp.zeros(shape, kind) for shape, kind in outs)

    head_shape = ((images, 2, tile, half), jnp.bfloat16)
    stack_shape = ((4, SLOT, D), jnp.bfloat16)
    piece_shape = ((SLOT, D), jnp.bfloat16)

    def control_attention():
        keyval, query = kernel_call(
            project_kernel, projections, (spot, normed, side, first, first_other),
            scratch=[stacks] + projection_scratch, copies=2 + 2 * images, micros=5,
        )
        return (neighborhood(keyval, query, control_only),) + empty(piece_shape, piece_shape)

    def base_weights():
        one = swap_links(keyval_piece, ORDER[1], base_only)
        two = swap_links(keyval_piece, ORDER[2], base_only)
        return empty(head_shape) + (one, two)

    attended, one, two = lax.cond(is_control, control_attention, base_weights)
    near = send(attended, sizes, lambda b, r, t: (0, r, t) if b == 1 else None)
    cross = send(attended, sizes, lambda b, r, t: (0, 1 - r, t) if b == 1 else None)
    prepared = [((D, D), jnp.bfloat16), ((2 * half + lanes, D), jnp.bfloat16), stack_shape]

    def control_finish():
        other = swap_rows(head_stack, control_only)
        out = finished(after(attended, other), other, hidden, modulation[1], control_only)
        return empty(*prepared) + (out,)

    def base_prepare():
        three = swap_links(one, ORDER[2], base_only)
        out_other = swap_cores(after(out_mine, three), base_only)
        zero_corner = swap_cores(after(zero_side, out_other), base_only)
        second = stacked([keyval_piece, one, two, three])
        second_other = swap_cores(after(second, zero_corner), base_only)
        zero_rows, projection_rows = kernel_call(
            prepare_kernel, prepared[:2],
            (spot, first, first_other, zero_side, zero_corner, second, second_other),
            scratch=[stacks, half_stacks, half_stacks], copies=6,
        )
        return (zero_rows, projection_rows, out_other) + empty((tile_shape, jnp.bfloat16))

    zero_rows, projection_rows, out_other, control = lax.cond(
        is_control, control_finish, base_prepare
    )

    def base_finish():
        other = swap_rows(head_stack, base_only)
        base_in, keyval, query = kernel_call(
            middle_kernel,
            [(tile_shape, jnp.float32)] + projections,
            (
                spot, own, far, side, corner, near, cross, out_mine, out_other, zero_rows,
                projection_rows, modulation[1], modulation[0],
            ),
            scratch=[
                ((2, images, tile, D), jnp.bfloat16),
                ((2, images, tile, D), jnp.bfloat16),
                ((2, 2 * images * tile, half), jnp.bfloat16),
                half_stacks,
                ((2 * half, D), jnp.bfloat16),
                ((D, D), jnp.bfloat16),
            ]
            + projection_scratch,
            copies=4 * images + 8, micros=8,
        )
        attended = neighborhood(keyval, query, base_only)
        return finished(attended, other, base_in, modulation[0], base_only)

    out = lax.cond(is_control, lambda: control, base_finish)
    return out.reshape(latent.shape)


def solution(mesh):
    placed = (
        P("branch", None, "trow", "tcol", None),
        P(),
        P("branch", None, "tcol"),
        P("branch", None, "tcol"),
        P("branch", "tcol", None),
        P(None, "tcol"),
    )
    sizes = (mesh.shape["branch"], mesh.shape["trow"], mesh.shape["tcol"])
    body = on_device
    if sizes == (2, 2, HEADS):
        body = functools.partial(paired_rows, sizes)
    return jax.shard_map(
        body,
        mesh=mesh,
        in_specs=placed,
        out_specs=P("branch", None, "trow", "tcol", None),
        check_vma=False,
    )
```

```python
import functools
import math

import jax
import jax.numpy as jnp
from jax import lax
from jax.experimental import pallas as pl
from jax.experimental.pallas import tpu as pltpu
from jax.sharding import PartitionSpec as P

D = 1152
HD = 72
HEADS = 8
WIN = 13
HW = 576


def padded(block, sides, width):
    for axis, dim in sides:
        count = lax.axis_size(axis)
        forward = [(i, i + 1) for i in range(count - 1)]
        backward = [(target, source) for source, target in forward]
        low = lax.ppermute(
            lax.slice_in_dim(block, block.shape[dim] - width, None, axis=dim), axis, forward
        )
        high = lax.ppermute(lax.slice_in_dim(block, 0, width, axis=dim), axis, backward)
        block = jnp.concatenate([low, block, high], axis=dim)
    return block


def shifted(block, axis, distance):
    devices = range(lax.axis_size(axis))
    route = [(i - distance, i) for i in devices if i - distance in devices]
    return lax.ppermute(block, axis, route)


def modulate(hidden, shift_scale):
    average = jnp.mean(hidden, axis=-1, keepdims=True)
    centred = hidden - average
    variance = jnp.mean(centred * centred, axis=-1, keepdims=True)
    return (centred * lax.rsqrt(variance + 1e-06) * (1.0 + shift_scale[1]) + shift_scale[0]).astype(
        jnp.bfloat16
    )


def block_mask(row_first, col_first, total_rows, total_cols, key_count):
    query_edge = 8
    radius = WIN // 2
    key_side = query_edge + 2 * radius
    offsets = jnp.arange(query_edge)
    reaches = jnp.arange(key_side)
    row_starts = jnp.clip(row_first + offsets - radius, 0, total_rows - WIN)
    key_rows = row_first - radius + reaches
    row_inside = (key_rows[None, :] >= row_starts[:, None]) & (
        key_rows[None, :] < row_starts[:, None] + WIN
    )
    col_starts = jnp.clip(col_first + offsets - radius, 0, total_cols - WIN)
    key_cols = col_first - radius + reaches
    col_inside = (key_cols[None, :] >= col_starts[:, None]) & (
        key_cols[None, :] < col_starts[:, None] + WIN
    )
    joined = row_inside[:, None, :, None] & col_inside[None, :, None, :]
    joined = joined.reshape(query_edge * query_edge, key_side * key_side)
    filler = jnp.zeros((query_edge * query_edge, key_count - key_side * key_side), dtype=jnp.bool_)
    return jnp.concatenate([joined, filler], axis=1)


def edge_keys(key_values):
    radius = WIN // 2
    return padded(key_values, (("trow", 1), ("tcol", 2)), radius)


def attend_tile(queries, extended, row_anchor, col_anchor, total_rows, total_cols):
    images, tile_rows, tile_cols = (queries.shape[0], queries.shape[1], queries.shape[2])
    query_edge = 8
    radius = WIN // 2
    key_side = query_edge + 2 * radius
    key_count = (key_side * key_side + 127) // 128 * 128
    across = tile_cols // query_edge
    block_count = tile_rows // query_edge * across
    scaling = 1.0 / math.sqrt(HD)

    def one_block(position):
        row_block = position // across * query_edge
        col_block = position % across * query_edge
        query_block = queries
        query_block = query_block.reshape(images, query_edge * query_edge, HEADS, HD)
        key_block = extended
        key_block = key_block.reshape(images, key_side * key_side, 2 * HW)
        key_block = jnp.pad(key_block, ((0, 0), (0, key_count - key_side * key_side), (0, 0)))
        key_heads = key_block[..., :HW].reshape(images, key_count, HEADS, HD)
        value_heads = key_block[..., HW:].reshape(images, key_count, HEADS, HD)
        allowed = block_mask(
            row_anchor + row_block, col_anchor + col_block, total_rows, total_cols, key_count
        )
        scores = (
            jnp.einsum(
                "iqhd,ikhd->ihqk", query_block, key_heads, preferred_element_type=jnp.float32
            )
            * scaling
        )
        scores = jnp.where(allowed[None, None], scores, -1e30)
        highest = jnp.max(scores, axis=-1, keepdims=True)
        raised = jnp.exp(scores - highest)
        totals = jnp.sum(raised, axis=-1, keepdims=True)
        weights = (raised / totals).astype(jnp.bfloat16)
        blended = jnp.einsum(
            "ihqk,ikhd->iqhd", weights, value_heads, preferred_element_type=jnp.float32
        )
        return blended.astype(jnp.bfloat16).reshape(images, query_edge, query_edge, HW)

    result = lax.map(one_block, jnp.arange(block_count))
    result = result.reshape(tile_rows // query_edge, across, images, query_edge, query_edge, HW)
    return result.transpose(2, 0, 3, 1, 4, 5).reshape(images, tile_rows, tile_cols, HW)


def run_block(active, hidden, shift_scale, weight_q, weight_kv, weight_o):
    images, tile_rows, tile_cols = (hidden.shape[0], hidden.shape[1], hidden.shape[2])
    tokens = images * tile_rows * tile_cols

    def project():
        flattened = modulate(hidden, shift_scale).reshape(tokens, D)
        queries = jnp.dot(flattened, weight_q, preferred_element_type=jnp.float32).astype(
            jnp.bfloat16
        )
        key_values = jnp.dot(flattened, weight_kv, preferred_element_type=jnp.float32).astype(
            jnp.bfloat16
        )
        return (queries, key_values)

    def nothing():
        return (jnp.zeros((tokens, HW), jnp.bfloat16), jnp.zeros((tokens, 2 * HW), jnp.bfloat16))

    queries, key_values = lax.cond(active, project, nothing)
    extended = edge_keys(key_values.reshape(images, tile_rows, tile_cols, 2 * HW))
    row_anchor = lax.axis_index("trow") * tile_rows
    col_anchor = lax.axis_index("tcol") * tile_cols
    total_rows = tile_rows * lax.axis_size("trow")
    total_cols = tile_cols * lax.axis_size("tcol")

    def finish():
        attended = attend_tile(
            queries.reshape(images, tile_rows, tile_cols, HW),
            extended,
            row_anchor,
            col_anchor,
            total_rows,
            total_cols,
        )
        projected = jnp.dot(
            attended.reshape(tokens, HW), weight_o, preferred_element_type=jnp.float32
        )
        return (hidden + shift_scale[2] * projected.reshape(hidden.shape)).astype(jnp.bfloat16)

    def vacant():
        return jnp.zeros(hidden.shape, jnp.bfloat16)

    return lax.cond(active, finish, vacant)


def zero_project(control_out, weight_z):
    flattened = control_out.reshape(-1, D)
    return (
        jnp.dot(flattened, weight_z, preferred_element_type=jnp.float32)
        .astype(jnp.bfloat16)
        .reshape(control_out.shape)
    )


def on_device(latent, modulation, w_query, w_keyval, w_out, w_zero):
    sources = (w_query, w_keyval, w_out)
    weight_q, weight_kv, weight_o, weight_z = (
        lax.all_gather(sources[0], "tcol", axis=2, tiled=True),
        lax.all_gather(sources[1], "tcol", axis=2, tiled=True),
        lax.all_gather(sources[2], "tcol", axis=1, tiled=True),
        lax.all_gather(w_zero, "tcol", axis=1, tiled=True),
    )
    branch_index = lax.axis_index("branch")
    is_control = branch_index == 1
    own_copy = latent[0]
    shift_scale = lax.dynamic_index_in_dim(modulation, branch_index, 0, keepdims=False)
    received = shifted(own_copy, "branch", 1)
    control_in = own_copy.astype(jnp.float32) + received.astype(jnp.float32)
    control_out = run_block(
        is_control, control_in, shift_scale, weight_q[0], weight_kv[0], weight_o[0]
    )

    def with_projection():
        return zero_project(control_out, weight_z)

    def without_projection():
        return jnp.zeros(control_out.shape, jnp.bfloat16)

    residual = lax.cond(is_control, with_projection, without_projection)
    returned = shifted(residual, "branch", -1)
    base_in = own_copy.astype(jnp.float32) + returned.astype(jnp.float32)
    base_out = run_block(
        jnp.logical_not(is_control), base_in, shift_scale, weight_q[0], weight_kv[0], weight_o[0]
    )
    return jnp.where(is_control, control_out, base_out)[None]


AXES = ("branch", "trow", "tcol")
SLOT = 80
SHARED = 64
ORDER = (0, 3, 1, 2)


def routes(sizes, move):
    found = []
    for b in range(sizes[0]):
        for r in range(sizes[1]):
            for t in range(sizes[2]):
                target = move(b, r, t)
                if target is not None:
                    found.append((place_of(sizes, b, r, t), place_of(sizes, *target)))
    return found


def place_of(sizes, b, r, t):
    return (b * sizes[1] + r) * sizes[2] + t


def send(block, sizes, move):
    return lax.ppermute(block, AXES, routes(sizes, move))


def after(block, *earlier):
    return lax.optimization_barrier((block,) + earlier)[0]


def kernel_call(body, outs, args, scratch=(), copies=0, stay=False, micros=0):
    def space(a):
        if a.dtype == jnp.int32:
            return pltpu.SMEM
        return pltpu.VMEM if a.dtype == jnp.float32 else pl.ANY

    buffers = [pltpu.VMEM(shape, kind) for shape, kind in scratch]
    return pl.pallas_call(
        body,
        out_shape=[jax.ShapeDtypeStruct(shape, kind) for shape, kind in outs],
        in_specs=[pl.BlockSpec(memory_space=space(a)) for a in args],
        out_specs=[pl.BlockSpec(memory_space=pl.ANY if stay else pltpu.VMEM) for _ in outs],
        scratch_shapes=buffers + [pltpu.SemaphoreType.DMA((copies,))],
        compiler_params=pltpu.CompilerParams(vmem_limit_bytes=32 * 1024 * 1024),
        cost_estimate=pl.CostEstimate(
            flops=0, bytes_accessed=1 + 3_700_000 * micros, transcendentals=0
        ),
    )(*args)


def begin(copies, done, first=0):
    started = []
    for n, (source, target) in enumerate(copies):
        copy = pltpu.make_async_copy(source, target, done.at[first + n])
        copy.start()
        started.append(copy)
    return started


def finish(started):
    for copy in started:
        copy.wait()


def dot_rows(left, right):
    return lax.dot_general(left, right, (((1,), (1,)), ((), ())), preferred_element_type=jnp.float32)


def rows_at(start, count):
    return pl.ds(pl.multiple_of(start, 16), count)


def stack_kernel(*refs):
    *pieces, stacked, done = refs
    finish(begin([(piece, stacked.at[n]) for n, piece in enumerate(pieces)], done))


def norm_kernel(spot, own, far, mod, normed, first, second, done):
    finish(begin([(own, first), (far, second)], done))
    for image in range(own.shape[0]):
        hidden = first[image].astype(jnp.float32) + second[image].astype(jnp.float32)
        normed[image] = modulate(hidden, mod)


def bias_kernel(total_rows, total_cols, spot, bias, done):
    radius = WIN // 2
    query = lax.broadcasted_iota(jnp.int32, bias.shape, 0)
    key = lax.broadcasted_iota(jnp.int32, bias.shape, 1)
    base = spot[4]
    row_start = jnp.clip((query >> 3) - radius, 0, total_rows - WIN)
    col_start = jnp.clip(base + (query & 7) - radius, 0, total_cols - WIN)
    key_row = (key & 127) >> 3
    outward = 2 * spot[3] - 1
    key_col = base + (1 - (key >> 7)) * outward * 8 + (key & 7)
    inside = (
        (key_row >= row_start)
        & (key_row < row_start + WIN)
        & (key_col >= col_start)
        & (key_col < col_start + WIN)
    )
    bias[...] = jnp.where(inside, 0.0, -1e30)


def unset_kernel(spot, out, done):
    pass


def in_order(origin):
    return (origin % 2) * 2 + origin // 2


def arrange_keyvals(link, stacks, weight):
    for at in range(2):
        for step in range(4):
            origin = link ^ ORDER[step]
            slot = (1 - origin // 2) * 4 + at * 2 + origin % 2
            weight[rows_at(slot * SLOT, SLOT), :] = stacks[at, step, :SLOT]


def arrange_heads(link, stack, first_row, weight):
    for step in range(4):
        start = first_row + in_order(link ^ ORDER[step]) * SLOT
        weight[rows_at(start, SLOT), :] = stack[step]


def clear_rows(weight, start, stop):
    weight[start:stop, :] = jnp.zeros((stop - start, weight.shape[1]), weight.dtype)


def project_kernel(spot, normed, normed_other, mine, other, keyval, query, stacks, weight, both, done):
    row, link, core = (spot[1], spot[2], spot[3])
    copies = [(mine, stacks.at[core]), (other, stacks.at[1 - core])]
    for image in range(normed.shape[0]):
        copies.append((normed.at[image], both.at[image, row]))
        copies.append((normed_other.at[image], both.at[image, 1 - row]))
    finish(begin(copies, done))
    arrange_keyvals(link, stacks, weight)
    start = weight.shape[0] - 4 * SLOT
    clear_rows(weight, 8 * SLOT, start)
    arrange_heads(link, stacks.at[row, :, SLOT : 2 * SLOT], start, weight)
    tokens = both[...].reshape(-1, both.shape[3])
    projected = dot_rows(tokens, weight[...]).astype(keyval.dtype)
    keyval[...] = projected[:, : keyval.shape[1]]
    query[...] = projected[:, keyval.shape[1] :]


def attend_kernel(spot, queries, outer, here, inner, bias, out, query_rows, keyvals, done):
    scaling = 1.0 / math.sqrt(HD)
    tokens = bias.shape[0]
    images = out.shape[0] // tokens
    copies = [(queries, query_rows)]
    copies += [(part, keyvals.at[index]) for index, part in enumerate((outer, here, inner))]
    finish(begin(copies, done))
    key_lanes = queries.shape[1]
    first_key = here.shape[1] - key_lanes
    heads = out.shape[1] // SLOT
    pad = key_lanes - heads * SLOT
    value_lanes = (out.shape[1] + 127) // 128 * 128
    query_lane = lax.broadcasted_iota(jnp.int32, (tokens, key_lanes), 1) - pad
    value_lane = lax.broadcasted_iota(jnp.int32, (tokens, value_lanes), 1)

    def within(lane, head):
        return (lane >= head * SLOT) & (lane < (head + 1) * SLOT)

    for image in range(images):
        rows = slice(image * tokens, (image + 1) * tokens)
        keys = jnp.concatenate([keyvals[n, rows, first_key:] for n in range(3)], axis=0)
        values = jnp.concatenate([keyvals[n, rows, :value_lanes] for n in range(3)], axis=0)
        query = query_rows[rows, :].astype(jnp.float32)
        split = [jnp.where(within(query_lane, head), query, 0.0) for head in range(heads)]
        scores = dot_rows(jnp.concatenate(split, axis=0).astype(jnp.bfloat16), keys)
        raised, sums = ([], [])
        for head in range(heads):
            part = scores[head * tokens : (head + 1) * tokens] * scaling + bias[...]
            part = jnp.exp(part - jnp.max(part, axis=-1, keepdims=True))
            sums.append(jnp.sum(part, axis=-1, keepdims=True))
            raised.append(part.astype(jnp.bfloat16))
        blended = jnp.dot(
            jnp.concatenate(raised, axis=0), values, preferred_element_type=jnp.float32
        )
        total = jnp.zeros((tokens, value_lanes), jnp.float32)
        for head in range(heads):
            part = blended[head * tokens : (head + 1) * tokens] / sums[head]
            total = jnp.where(within(value_lane, head), part, total)
        out[rows, :] = total[:, : out.shape[1]].astype(out.dtype)


def head_rows_kernel(index, spot, mine, other, out, outs, done):
    at = spot[index]
    copies = [(mine, outs.at[1 - at]), (other, outs.at[at])]
    finish(begin(copies, done))
    for part in range(2):
        arrange_heads(spot[2], outs.at[part], part * 4 * SLOT, out)


def middle_kernel(
    spot, own, far, side, corner, near, cross, out_mine, out_other, first, first_other,
    zero_side, zero_corner, mod, mod_base, residue, keyval, query,
    base_rows, more_rows, heads, outs, w_out, stacks, zeros, w_zero, weight, both, done,
):
    row, link, core = (spot[1], spot[2], spot[3])
    images, tokens, _ = own.shape
    tile = images * tokens
    width = heads.shape[2]
    copies = []
    for image in range(images):
        for part, slot in ((0, row), (1, 1 - row)):
            rows = slice(part * tile + image * tokens, part * tile + (image + 1) * tokens)
            for index, ref in enumerate((near, cross)):
                copies.append((ref.at[image, slot], heads.at[index, rows]))
    copies += [(out_mine, outs.at[core]), (out_other, outs.at[1 - core])]
    copies += [(own, base_rows.at[0]), (side, base_rows.at[1])]
    copies += [(far, more_rows.at[0]), (corner, more_rows.at[1])]
    early = begin(copies, done)
    copies = [(first, stacks.at[core]), (first_other, stacks.at[1 - core])]
    copies += [(zero_side, zeros.at[core]), (zero_corner, zeros.at[1 - core])]
    late = begin(copies, done, len(early))
    finish(early)
    for at in range(2):
        arrange_heads(link, outs.at[at], at * width, w_out)
    projected = jnp.dot(
        heads[0], w_out[rows_at(row * width, width), :], preferred_element_type=jnp.float32
    )
    projected += jnp.dot(
        heads[1], w_out[rows_at((1 - row) * width, width), :], preferred_element_type=jnp.float32
    )

    def flat(ref):
        return ref[...].reshape(2 * tile, ref.shape[3]).astype(jnp.float32)

    base = flat(base_rows)
    out = (base + flat(more_rows) + mod[2] * projected).astype(jnp.bfloat16)
    finish(late)
    shard = w_zero.shape[0] // 8
    kept = shard - SHARED
    for at in range(2):
        for step in range(4):
            start = (2 * (link ^ ORDER[step]) + at) * shard
            w_zero[rows_at(start + row * SHARED, kept), :] = stacks[at, step, SLOT : 2 * SLOT]
            w_zero[rows_at(start + (1 - row) * kept, SHARED), :] = zeros[at, step]
    arrange_keyvals(link, stacks, weight)
    start = weight.shape[0] - 4 * SLOT
    clear_rows(weight, 8 * SLOT, start)
    arrange_heads(link, stacks.at[row, :, 2 * SLOT :], start, weight)
    residual = dot_rows(out, w_zero[...]).astype(jnp.bfloat16)
    base = base + residual.astype(jnp.float32)
    result = modulate(base, mod_base)
    for image in range(images):
        rows = slice(image * tokens, (image + 1) * tokens)
        residue[image] = residual[rows]
        both[image, row] = result[rows]
        both[image, 1 - row] = result[tile + image * tokens : tile + (image + 1) * tokens]
    rows = both[...].reshape(2 * tile, both.shape[3])
    projected = dot_rows(rows, weight[...]).astype(keyval.dtype)
    keyval[...] = projected[:, : keyval.shape[1]]
    query[...] = projected[:, keyval.shape[1] :]


def final_kernel(
    spot, attended, side, head_rows, own, more, mod, out, near, far, w_out, first, second, done
):
    row = spot[1]
    images = out.shape[0]
    width = near.shape[2]
    copies = [(head_rows, w_out), (own, first), (more, second), (side, far)]
    copies += [(attended.at[image, row], near.at[image]) for image in range(images)]
    finish(begin(copies, done))

    def flat(ref):
        return jnp.concatenate([ref[i] for i in range(images)], axis=0)

    projected = jnp.dot(
        flat(near), w_out[rows_at(row * width, width), :], preferred_element_type=jnp.float32
    )
    projected += jnp.dot(
        flat(far), w_out[rows_at((1 - row) * width, width), :], preferred_element_type=jnp.float32
    )
    tokens = out.shape[1]
    for image in range(images):
        rows = slice(image * tokens, (image + 1) * tokens)
        base = first[image].astype(jnp.float32) + second[image].astype(jnp.float32)
        out[image] = (base + mod[2] * projected[rows]).astype(out.dtype)


def paired_rows(sizes, latent, modulation, w_query, w_keyval, w_out, w_zero):
    branch = lax.axis_index("branch")
    row = lax.axis_index("trow")
    column = lax.axis_index("tcol")
    core = column % 2
    is_control = branch == 1
    is_query = core == row
    _, images, tile_rows, tile_cols, _ = latent.shape
    tile = tile_rows * tile_cols
    tokens = images * 2 * tile
    half = HEADS // 2 * SLOT
    lanes = half + half % 128
    spot = jnp.stack([branch, row, column // 2, core, column * tile_cols]).astype(jnp.int32)
    own = latent.reshape(images, tile, D)

    def everyone(b, r, t):
        return True

    def base_only(b, r, t):
        return b == 0

    def control_only(b, r, t):
        return b == 1

    def swap_cores(block, joins=everyone):
        return send(block, sizes, lambda b, r, t: (b, r, t ^ 1) if joins(b, r, t) else None)

    def swap_rows(block, joins=everyone):
        return send(block, sizes, lambda b, r, t: (b, 1 - r, t) if joins(b, r, t) else None)

    def swap_links(block, distance, joins=everyone):
        return send(
            block, sizes, lambda b, r, t: (b, r, t ^ (2 * distance)) if joins(b, r, t) else None
        )

    def padded_rows(block):
        return jnp.pad(block, ((0, SLOT - HD), (0, 0)))

    def stacked(pieces):
        shape = (len(pieces),) + pieces[0].shape
        out = [(shape, jnp.bfloat16)]
        (stack,) = kernel_call(stack_kernel, out, pieces, copies=len(pieces), stay=True)
        return stack.reshape((-1,) + shape[-2:])

    def joined(block, other):
        return jnp.concatenate([block, other], axis=0)

    def unset(*outs):
        return tuple(kernel_call(unset_kernel, [out], (spot,), copies=1, stay=True)[0] for out in outs)

    tile_shape = (images, tile, D)
    head_shape = ((images, 2, tile, half), jnp.bfloat16)
    half_head_shape = ((images, tile, half), jnp.bfloat16)
    stack_shape = ((4, SLOT, D), jnp.bfloat16)
    shared_shape = ((4, SHARED, D), jnp.bfloat16)
    rows_shape = ((2 * half, D), jnp.bfloat16)
    projections = [((tokens, 2 * half), jnp.bfloat16), ((tokens, lanes), jnp.bfloat16)]
    shard = w_zero.shape[1]
    triple_shape = ((4, 3 * SLOT, D), jnp.bfloat16)
    stacks = ((2,) + triple_shape[0], jnp.bfloat16)
    shared_stacks = ((2, 4, SHARED, D), jnp.bfloat16)
    half_stacks = ((2, 4, SLOT, D), jnp.bfloat16)
    both_shape = ((images, 2, tile, D), jnp.bfloat16)

    keyval_piece = padded_rows(lax.dynamic_slice_in_dim(w_keyval[0].T, row * HD, HD, axis=0))
    zero_piece = lax.dynamic_slice_in_dim(w_zero.T, row * SHARED, shard - SHARED, axis=0)
    query_or_out = padded_rows(jnp.where(is_query, w_query[0].T, w_out[0]))

    out_piece = padded_rows(w_out[0])
    piece = jnp.concatenate(
        [
            keyval_piece,
            jnp.where(is_control, query_or_out, zero_piece),
            jnp.where(is_control, out_piece, query_or_out),
        ],
        axis=0,
    )
    first = [piece, swap_links(piece, ORDER[1]), swap_links(piece, ORDER[2])]
    started = after(own, piece)
    far = send(started, sizes, lambda b, r, t: (1 - b, r, t))
    corner = send(started, sizes, lambda b, r, t: (0, 1 - r, t) if b == 1 else None)
    (normed,) = kernel_call(
        norm_kernel, [(tile_shape, jnp.bfloat16)], (spot, own, far, modulation[1]),
        scratch=[(tile_shape, jnp.bfloat16), (tile_shape, jnp.bfloat16)], copies=2,
    )
    side = swap_rows(jnp.where(is_control, normed, own))
    side, corner, *first = lax.optimization_barrier((side, corner, *first))
    first.append(swap_links(first[1], ORDER[2]))
    first = stacked(first)
    first_other = swap_cores(first)
    head_stack = jnp.where(is_query, first[:, 2 * SLOT :], first[:, SLOT : 2 * SLOT])
    out_mine = send(head_stack, sizes, lambda b, r, t: (0, r, t) if b == 1 else None)

    def halos(keyval, joins):
        def across(b, r, t):
            target = t + 1 if t % 2 else t - 1
            return (b, r, target) if joins(b, r, t) and 0 <= target < sizes[2] else None

        return send(keyval, sizes, across), swap_cores(keyval, joins)

    def neighborhood(query, keyval, outer, inner):
        (bias,) = kernel_call(
            functools.partial(bias_kernel, 2 * tile_rows, sizes[2] * tile_cols),
            [((2 * tile, 6 * tile), jnp.float32)], (spot,), copies=1,
        )
        (attended,) = kernel_call(
            attend_kernel, [((tokens, half), jnp.bfloat16)],
            (spot, query, outer, keyval, inner, bias),
            scratch=[((tokens, lanes), jnp.bfloat16), ((3, tokens, 2 * half), jnp.bfloat16)],
            copies=4, micros=8,
        )
        return attended.reshape(images, 2, tile, half)

    def their_heads(attended, joins):
        theirs = lax.dynamic_index_in_dim(attended, 1 - row, 1, keepdims=False)
        return swap_rows(theirs, joins)

    def head_rows(index, mine, other):
        (rows,) = kernel_call(
            functools.partial(head_rows_kernel, index), [rows_shape], (spot, mine, other),
            scratch=[half_stacks], copies=2,
        )
        return rows

    def finished(attended, side_heads, rows, more, mod):
        (out,) = kernel_call(
            final_kernel, [(tile_shape, jnp.bfloat16)],
            (spot, attended, side_heads, rows, own, more, mod),
            scratch=[half_head_shape, half_head_shape, rows_shape]
            + [(tile_shape, jnp.bfloat16), (tile_shape, jnp.bfloat16)],
            copies=4 + images,
        )
        return out

    def control_attention():
        keyval, query = kernel_call(
            project_kernel, projections, (spot, normed, side, first, first_other),
            scratch=[stacks, ((2 * half + lanes, D), jnp.bfloat16), both_shape],
            copies=2 + 2 * images, micros=5,
        )
        attended = neighborhood(query, keyval, *halos(keyval, control_only))
        return attended

    attended = lax.cond(is_control, control_attention, lambda: unset(head_shape)[0])
    near = send(attended, sizes, lambda b, r, t: (0, r, t) if b == 1 else None)
    cross = send(attended, sizes, lambda b, r, t: (0, 1 - r, t) if b == 1 else None)

    def base_exchange():
        shared = lax.dynamic_slice_in_dim(
            after(first, attended), SLOT + row * (SLOT - SHARED), SHARED, axis=1
        )
        third = jnp.where(
            is_query, first_other[:, 2 * SLOT :], after(first, attended)[:, 2 * SLOT :]
        )
        return swap_rows(shared, base_only), third

    zero_side, third = lax.cond(
        is_control, lambda: unset(shared_shape, stack_shape), base_exchange
    )

    def control_finish():
        rows = head_rows(3, swap_cores(head_stack, control_only), head_stack)
        side_heads = their_heads(attended, control_only)
        out = finished(attended, side_heads, rows, far, modulation[1])
        return unset(shared_shape, stack_shape) + (out,)

    def base_prepare():
        zero_corner = swap_cores(zero_side, base_only)
        out_other = swap_cores(out_mine, base_only)
        return (zero_corner, out_other) + unset((tile_shape, jnp.bfloat16))

    zero_corner, out_other, control = lax.cond(
        is_control, control_finish, base_prepare
    )

    def base_finish():
        other = swap_rows(third, base_only)
        residue, keyval, query = kernel_call(
            middle_kernel,
            [(tile_shape, jnp.bfloat16)] + projections,
            (
                spot, own, far, side, corner, near, cross, out_mine, out_other, first, first_other,
                zero_side, zero_corner, modulation[1], modulation[0],
            ),
            scratch=[
                ((2, images, tile, D), jnp.bfloat16),
                ((2, images, tile, D), jnp.bfloat16),
                ((2, 2 * images * tile, half), jnp.bfloat16),
                half_stacks,
                rows_shape,
                stacks,
                shared_stacks,
                ((D, D), jnp.bfloat16),
                ((2 * half + lanes, D), jnp.bfloat16),
                both_shape,
            ],
            copies=4 * images + 10, micros=8,
        )
        outer, inner = halos(keyval, base_only)
        attended = neighborhood(query, keyval, outer, inner)
        side_heads = their_heads(attended, base_only)
        return finished(attended, side_heads, head_rows(1, third, other), residue, modulation[0])

    out = lax.cond(is_control, lambda: control, base_finish)
    return out.reshape(latent.shape)


def solution(mesh):
    placed = (
        P("branch", None, "trow", "tcol", None),
        P(),
        P("branch", None, "tcol"),
        P("branch", None, "tcol"),
        P("branch", "tcol", None),
        P(None, "tcol"),
    )
    sizes = (mesh.shape["branch"], mesh.shape["trow"], mesh.shape["tcol"])
    body = on_device
    if sizes == (2, 2, HEADS):
        body = functools.partial(paired_rows, sizes)
    return jax.shard_map(
        body,
        mesh=mesh,
        in_specs=placed,
        out_specs=P("branch", None, "trow", "tcol", None),
        check_vma=False,
    )
```

```python
import functools
import math

import jax
import jax.numpy as jnp
from jax import lax
from jax.experimental import pallas as pl
from jax.experimental.pallas import tpu as pltpu
from jax.sharding import PartitionSpec as P

D = 1152
HD = 72
HEADS = 8
WIN = 13
HW = 576


def padded(block, sides, width):
    for axis, dim in sides:
        count = lax.axis_size(axis)
        forward = [(i, i + 1) for i in range(count - 1)]
        backward = [(target, source) for source, target in forward]
        low = lax.ppermute(
            lax.slice_in_dim(block, block.shape[dim] - width, None, axis=dim), axis, forward
        )
        high = lax.ppermute(lax.slice_in_dim(block, 0, width, axis=dim), axis, backward)
        block = jnp.concatenate([low, block, high], axis=dim)
    return block


def shifted(block, axis, distance):
    devices = range(lax.axis_size(axis))
    route = [(i - distance, i) for i in devices if i - distance in devices]
    return lax.ppermute(block, axis, route)


def modulate(hidden, shift_scale):
    average = jnp.mean(hidden, axis=-1, keepdims=True)
    centred = hidden - average
    variance = jnp.mean(centred * centred, axis=-1, keepdims=True)
    return (centred * lax.rsqrt(variance + 1e-06) * (1.0 + shift_scale[1]) + shift_scale[0]).astype(
        jnp.bfloat16
    )


def block_mask(row_first, col_first, total_rows, total_cols, key_count):
    query_edge = 8
    radius = WIN // 2
    key_side = query_edge + 2 * radius
    offsets = jnp.arange(query_edge)
    reaches = jnp.arange(key_side)
    row_starts = jnp.clip(row_first + offsets - radius, 0, total_rows - WIN)
    key_rows = row_first - radius + reaches
    row_inside = (key_rows[None, :] >= row_starts[:, None]) & (
        key_rows[None, :] < row_starts[:, None] + WIN
    )
    col_starts = jnp.clip(col_first + offsets - radius, 0, total_cols - WIN)
    key_cols = col_first - radius + reaches
    col_inside = (key_cols[None, :] >= col_starts[:, None]) & (
        key_cols[None, :] < col_starts[:, None] + WIN
    )
    joined = row_inside[:, None, :, None] & col_inside[None, :, None, :]
    joined = joined.reshape(query_edge * query_edge, key_side * key_side)
    filler = jnp.zeros((query_edge * query_edge, key_count - key_side * key_side), dtype=jnp.bool_)
    return jnp.concatenate([joined, filler], axis=1)


def edge_keys(key_values):
    radius = WIN // 2
    return padded(key_values, (("trow", 1), ("tcol", 2)), radius)


def attend_tile(queries, extended, row_anchor, col_anchor, total_rows, total_cols):
    images, tile_rows, tile_cols = (queries.shape[0], queries.shape[1], queries.shape[2])
    query_edge = 8
    radius = WIN // 2
    key_side = query_edge + 2 * radius
    key_count = (key_side * key_side + 127) // 128 * 128
    across = tile_cols // query_edge
    block_count = tile_rows // query_edge * across
    scaling = 1.0 / math.sqrt(HD)

    def one_block(position):
        row_block = position // across * query_edge
        col_block = position % across * query_edge
        query_block = queries
        query_block = query_block.reshape(images, query_edge * query_edge, HEADS, HD)
        key_block = extended
        key_block = key_block.reshape(images, key_side * key_side, 2 * HW)
        key_block = jnp.pad(key_block, ((0, 0), (0, key_count - key_side * key_side), (0, 0)))
        key_heads = key_block[..., :HW].reshape(images, key_count, HEADS, HD)
        value_heads = key_block[..., HW:].reshape(images, key_count, HEADS, HD)
        allowed = block_mask(
            row_anchor + row_block, col_anchor + col_block, total_rows, total_cols, key_count
        )
        scores = (
            jnp.einsum(
                "iqhd,ikhd->ihqk", query_block, key_heads, preferred_element_type=jnp.float32
            )
            * scaling
        )
        scores = jnp.where(allowed[None, None], scores, -1e30)
        highest = jnp.max(scores, axis=-1, keepdims=True)
        raised = jnp.exp(scores - highest)
        totals = jnp.sum(raised, axis=-1, keepdims=True)
        weights = (raised / totals).astype(jnp.bfloat16)
        blended = jnp.einsum(
            "ihqk,ikhd->iqhd", weights, value_heads, preferred_element_type=jnp.float32
        )
        return blended.astype(jnp.bfloat16).reshape(images, query_edge, query_edge, HW)

    result = lax.map(one_block, jnp.arange(block_count))
    result = result.reshape(tile_rows // query_edge, across, images, query_edge, query_edge, HW)
    return result.transpose(2, 0, 3, 1, 4, 5).reshape(images, tile_rows, tile_cols, HW)


def run_block(active, hidden, shift_scale, weight_q, weight_kv, weight_o):
    images, tile_rows, tile_cols = (hidden.shape[0], hidden.shape[1], hidden.shape[2])
    tokens = images * tile_rows * tile_cols

    def project():
        flattened = modulate(hidden, shift_scale).reshape(tokens, D)
        queries = jnp.dot(flattened, weight_q, preferred_element_type=jnp.float32).astype(
            jnp.bfloat16
        )
        key_values = jnp.dot(flattened, weight_kv, preferred_element_type=jnp.float32).astype(
            jnp.bfloat16
        )
        return (queries, key_values)

    def nothing():
        return (jnp.zeros((tokens, HW), jnp.bfloat16), jnp.zeros((tokens, 2 * HW), jnp.bfloat16))

    queries, key_values = lax.cond(active, project, nothing)
    extended = edge_keys(key_values.reshape(images, tile_rows, tile_cols, 2 * HW))
    row_anchor = lax.axis_index("trow") * tile_rows
    col_anchor = lax.axis_index("tcol") * tile_cols
    total_rows = tile_rows * lax.axis_size("trow")
    total_cols = tile_cols * lax.axis_size("tcol")

    def finish():
        attended = attend_tile(
            queries.reshape(images, tile_rows, tile_cols, HW),
            extended,
            row_anchor,
            col_anchor,
            total_rows,
            total_cols,
        )
        projected = jnp.dot(
            attended.reshape(tokens, HW), weight_o, preferred_element_type=jnp.float32
        )
        return (hidden + shift_scale[2] * projected.reshape(hidden.shape)).astype(jnp.bfloat16)

    def vacant():
        return jnp.zeros(hidden.shape, jnp.bfloat16)

    return lax.cond(active, finish, vacant)


def zero_project(control_out, weight_z):
    flattened = control_out.reshape(-1, D)
    return (
        jnp.dot(flattened, weight_z, preferred_element_type=jnp.float32)
        .astype(jnp.bfloat16)
        .reshape(control_out.shape)
    )


def on_device(latent, modulation, w_query, w_keyval, w_out, w_zero):
    sources = (w_query, w_keyval, w_out)
    weight_q, weight_kv, weight_o, weight_z = (
        lax.all_gather(sources[0], "tcol", axis=2, tiled=True),
        lax.all_gather(sources[1], "tcol", axis=2, tiled=True),
        lax.all_gather(sources[2], "tcol", axis=1, tiled=True),
        lax.all_gather(w_zero, "tcol", axis=1, tiled=True),
    )
    branch_index = lax.axis_index("branch")
    is_control = branch_index == 1
    own_copy = latent[0]
    shift_scale = lax.dynamic_index_in_dim(modulation, branch_index, 0, keepdims=False)
    received = shifted(own_copy, "branch", 1)
    control_in = own_copy.astype(jnp.float32) + received.astype(jnp.float32)
    control_out = run_block(
        is_control, control_in, shift_scale, weight_q[0], weight_kv[0], weight_o[0]
    )

    def with_projection():
        return zero_project(control_out, weight_z)

    def without_projection():
        return jnp.zeros(control_out.shape, jnp.bfloat16)

    residual = lax.cond(is_control, with_projection, without_projection)
    returned = shifted(residual, "branch", -1)
    base_in = own_copy.astype(jnp.float32) + returned.astype(jnp.float32)
    base_out = run_block(
        jnp.logical_not(is_control), base_in, shift_scale, weight_q[0], weight_kv[0], weight_o[0]
    )
    return jnp.where(is_control, control_out, base_out)[None]


AXES = ("branch", "trow", "tcol")
SLOT = 80
SHARED = 64
ORDER = (0, 3, 1, 2)


def routes(sizes, move):
    found = []
    for b in range(sizes[0]):
        for r in range(sizes[1]):
            for t in range(sizes[2]):
                target = move(b, r, t)
                if target is not None:
                    found.append((place_of(sizes, b, r, t), place_of(sizes, *target)))
    return found


def place_of(sizes, b, r, t):
    return (b * sizes[1] + r) * sizes[2] + t


def send(block, sizes, move):
    return lax.ppermute(block, AXES, routes(sizes, move))


def after(block, *earlier):
    return lax.optimization_barrier((block,) + earlier)[0]


def kernel_call(body, outs, args, scratch=(), copies=0, stay=False, micros=0, near=False):
    def space(a):
        if a.dtype == jnp.int32:
            return pltpu.SMEM
        return pltpu.VMEM if near or a.dtype == jnp.float32 else pl.ANY

    buffers = [pltpu.VMEM(shape, kind) for shape, kind in scratch]
    return pl.pallas_call(
        body,
        out_shape=[jax.ShapeDtypeStruct(shape, kind) for shape, kind in outs],
        in_specs=[pl.BlockSpec(memory_space=space(a)) for a in args],
        out_specs=[pl.BlockSpec(memory_space=pl.ANY if stay else pltpu.VMEM) for _ in outs],
        scratch_shapes=buffers + ([pltpu.SemaphoreType.DMA((copies,))] if copies else []),
        compiler_params=pltpu.CompilerParams(vmem_limit_bytes=32 * 1024 * 1024),
        cost_estimate=pl.CostEstimate(
            flops=0, bytes_accessed=1 + 3_700_000 * micros, transcendentals=0
        ),
    )(*args)


def begin(copies, done, first=0):
    started = []
    for n, (source, target) in enumerate(copies):
        copy = pltpu.make_async_copy(source, target, done.at[first + n])
        copy.start()
        started.append(copy)
    return started


def finish(started):
    for copy in started:
        copy.wait()


def dot_rows(left, right):
    return lax.dot_general(left, right, (((1,), (1,)), ((), ())), preferred_element_type=jnp.float32)


def rows_at(start, count):
    return pl.ds(pl.multiple_of(start, 16), count)


def stack_kernel(spot, one, two, three, four, stacked, heads, shared, done):
    pieces = (one, two, three, four)
    started = begin([(piece, stacked.at[n]) for n, piece in enumerate(pieces)], done)

    def part(first, target):
        rows = slice(first, first + target.shape[1])
        finish(begin([(piece.at[rows], target.at[n]) for n, piece in enumerate(pieces)], done, 4))

    is_control = spot[0] == 1
    is_query = spot[3] == spot[1]
    low = spot[1] == 0
    pl.when(is_control & is_query)(lambda: part(2 * SLOT, heads))
    pl.when(is_control & jnp.logical_not(is_query))(lambda: part(SLOT, heads))
    pl.when(jnp.logical_not(is_control) & low)(lambda: part(SLOT, shared))
    pl.when(jnp.logical_not(is_control | low))(lambda: part(2 * SLOT - SHARED, shared))
    finish(started)


def norm_kernel(spot, own, far, mod, normed, first, second, done):
    finish(begin([(own, first), (far, second)], done))
    for image in range(own.shape[0]):
        hidden = first[image].astype(jnp.float32) + second[image].astype(jnp.float32)
        normed[image] = modulate(hidden, mod)


def bias_kernel(total_rows, total_cols, spot, bias, done):
    radius = WIN // 2
    query = lax.broadcasted_iota(jnp.int32, bias.shape, 0)
    key = lax.broadcasted_iota(jnp.int32, bias.shape, 1)
    base = spot[4]
    row_start = jnp.clip((query >> 3) - radius, 0, total_rows - WIN)
    col_start = jnp.clip(base + (query & 7) - radius, 0, total_cols - WIN)
    key_row = (key & 127) >> 3
    outward = 2 * spot[3] - 1
    key_col = base + (1 - (key >> 7)) * outward * 8 + (key & 7)
    inside = (
        (key_row >= row_start)
        & (key_row < row_start + WIN)
        & (key_col >= col_start)
        & (key_col < col_start + WIN)
    )
    bias[...] = jnp.where(inside, 0.0, -1e30)


def unset_kernel(spot, out, done):
    pass


def in_order(origin):
    return (origin % 2) * 2 + origin // 2


def arrange_keyvals(link, core, mine, other, weight):
    for block, at in ((mine, core), (other, 1 - core)):
        for step in range(4):
            origin = link ^ ORDER[step]
            slot = (1 - origin // 2) * 4 + at * 2 + origin % 2
            weight[rows_at(slot * SLOT, SLOT), :] = block[step, :SLOT]


def arrange_heads(link, stack, first_row, weight):
    for step in range(4):
        start = first_row + in_order(link ^ ORDER[step]) * SLOT
        weight[rows_at(start, SLOT), :] = stack[step]


def clear_rows(weight, start, stop):
    weight[start:stop, :] = jnp.zeros((stop - start, weight.shape[1]), weight.dtype)


def arrange_queries(spot, mine, other, part, weight):
    start = weight.shape[0] - 4 * SLOT
    clear_rows(weight, 8 * SLOT, start)
    rows = slice(part * SLOT, (part + 1) * SLOT)
    own = spot[3] == spot[1]
    pl.when(own)(lambda: arrange_heads(spot[2], mine.at[:, rows], start, weight))
    pl.when(jnp.logical_not(own))(lambda: arrange_heads(spot[2], other.at[:, rows], start, weight))


def project_kernel(spot, normed, normed_other, mine, other, keyval, query, weight, both):
    row, link, core = (spot[1], spot[2], spot[3])
    arrange_keyvals(link, core, mine, other, weight)
    arrange_queries(spot, mine, other, 1, weight)
    both[:, row] = normed[...]
    both[:, 1 - row] = normed_other[...]
    tokens = both[...].reshape(-1, both.shape[3])
    projected = dot_rows(tokens, weight[...]).astype(keyval.dtype)
    keyval[...] = projected[:, : keyval.shape[1]]
    query[...] = projected[:, keyval.shape[1] :]


def attend_kernel(spot, queries, outer, here, inner, bias, out, query_rows, keyvals, done):
    scaling = math.log2(math.e) / math.sqrt(HD)
    tokens = bias.shape[0]
    images = out.shape[0] // tokens
    copies = [(queries, query_rows)]
    copies += [(part, keyvals.at[index]) for index, part in enumerate((outer, here, inner))]
    finish(begin(copies, done))
    key_lanes = queries.shape[1]
    first_key = here.shape[1] - key_lanes
    heads = out.shape[1] // SLOT
    pad = key_lanes - heads * SLOT
    value_lanes = (out.shape[1] + 127) // 128 * 128
    query_lane = lax.broadcasted_iota(jnp.int32, (tokens, key_lanes), 1) - pad
    value_lane = lax.broadcasted_iota(jnp.int32, (tokens, value_lanes), 1)

    def within(lane, head):
        return (lane >= head * SLOT) & (lane < (head + 1) * SLOT)

    for image in range(images):
        rows = slice(image * tokens, (image + 1) * tokens)
        keys = jnp.concatenate([keyvals[n, rows, first_key:] for n in range(3)], axis=0)
        values = jnp.concatenate([keyvals[n, rows, :value_lanes] for n in range(3)], axis=0)
        query = query_rows[rows, :].astype(jnp.float32)
        split = [jnp.where(within(query_lane, head), query, 0.0) for head in range(heads)]
        scores = dot_rows(jnp.concatenate(split, axis=0).astype(jnp.bfloat16), keys)
        raised, sums = ([], [])
        for head in range(heads):
            part = scores[head * tokens : (head + 1) * tokens] * scaling + bias[...]
            part = jnp.exp2(part - jnp.max(part, axis=-1, keepdims=True))
            sums.append(1.0 / jnp.sum(part, axis=-1, keepdims=True))
            raised.append(part.astype(jnp.bfloat16))
        blended = jnp.dot(
            jnp.concatenate(raised, axis=0), values, preferred_element_type=jnp.float32
        )
        total = jnp.zeros((tokens, value_lanes), jnp.float32)
        for head in range(heads):
            part = blended[head * tokens : (head + 1) * tokens] * sums[head]
            total = jnp.where(within(value_lane, head), part, total)
        out[rows, :] = total[:, : out.shape[1]].astype(out.dtype)


def head_rows_kernel(index, spot, mine, other, out, outs, done):
    at = spot[index]
    copies = [(mine, outs.at[1 - at]), (other, outs.at[at])]
    finish(begin(copies, done))
    for part in range(2):
        arrange_heads(spot[2], outs.at[part], part * 4 * SLOT, out)


def middle_kernel(
    spot, own, far, side, corner, near, cross, out_mine, out_other, first, first_other,
    zero_side, zero_corner, mod, mod_base, residue, keyval, query,
    w_out, w_zero, weight, both,
):
    row, link, core = (spot[1], spot[2], spot[3])
    images, tokens, _ = own.shape
    tile = images * tokens
    width = near.shape[3]
    for block, at in ((out_mine, core), (out_other, 1 - core)):
        arrange_heads(link, block, at * width, w_out)
    shard = w_zero.shape[0] // 8
    kept = shard - SHARED
    for block, part, at in (
        (first, zero_side, core),
        (first_other, zero_corner, 1 - core),
    ):
        for step in range(4):
            start = (2 * (link ^ ORDER[step]) + at) * shard
            w_zero[rows_at(start + row * SHARED, kept), :] = block[step, SLOT : 2 * SLOT]
            w_zero[rows_at(start + (1 - row) * kept, SHARED), :] = part[step]
    arrange_keyvals(link, core, first, first_other, weight)
    arrange_queries(spot, first, first_other, 2, weight)

    def ordered(ref):
        return jnp.concatenate([ref[i, s] for s in (row, 1 - row) for i in range(images)], axis=0)

    def stacked(one, two):
        parts = [ref[i] for ref in (one, two) for i in range(images)]
        return jnp.concatenate(parts, axis=0).astype(jnp.float32)

    projected = jnp.dot(
        ordered(near), w_out[rows_at(row * width, width), :], preferred_element_type=jnp.float32
    )
    projected += jnp.dot(
        ordered(cross),
        w_out[rows_at((1 - row) * width, width), :],
        preferred_element_type=jnp.float32,
    )
    base = stacked(own, side)
    out = (base + stacked(far, corner) + mod[2] * projected).astype(jnp.bfloat16)
    residual = dot_rows(out, w_zero[...]).astype(jnp.bfloat16)
    base = base + residual.astype(jnp.float32)
    result = modulate(base, mod_base)
    for image in range(images):
        rows = slice(image * tokens, (image + 1) * tokens)
        residue[image] = residual[rows]
        both[image, row] = result[rows]
        both[image, 1 - row] = result[tile + image * tokens : tile + (image + 1) * tokens]
    rows = both[...].reshape(2 * tile, both.shape[3])
    projected = dot_rows(rows, weight[...]).astype(keyval.dtype)
    keyval[...] = projected[:, : keyval.shape[1]]
    query[...] = projected[:, keyval.shape[1] :]


def final_kernel(
    spot, attended, side, head_rows, own, more, mod, out, near, far, w_out, first, second, done
):
    row = spot[1]
    images = out.shape[0]
    width = near.shape[2]
    copies = [(head_rows, w_out), (own, first), (more, second), (side, far)]
    copies += [(attended.at[image, row], near.at[image]) for image in range(images)]
    finish(begin(copies, done))

    def flat(ref):
        return jnp.concatenate([ref[i] for i in range(images)], axis=0)

    projected = jnp.dot(
        flat(near), w_out[rows_at(row * width, width), :], preferred_element_type=jnp.float32
    )
    projected += jnp.dot(
        flat(far), w_out[rows_at((1 - row) * width, width), :], preferred_element_type=jnp.float32
    )
    tokens = out.shape[1]
    for image in range(images):
        rows = slice(image * tokens, (image + 1) * tokens)
        base = first[image].astype(jnp.float32) + second[image].astype(jnp.float32)
        out[image] = (base + mod[2] * projected[rows]).astype(out.dtype)


def paired_rows(sizes, latent, modulation, w_query, w_keyval, w_out, w_zero):
    branch = lax.axis_index("branch")
    row = lax.axis_index("trow")
    column = lax.axis_index("tcol")
    core = column % 2
    is_control = branch == 1
    is_query = core == row
    _, images, tile_rows, tile_cols, _ = latent.shape
    tile = tile_rows * tile_cols
    tokens = images * 2 * tile
    half = HEADS // 2 * SLOT
    lanes = half + half % 128
    spot = jnp.stack([branch, row, column // 2, core, column * tile_cols]).astype(jnp.int32)
    own = latent.reshape(images, tile, D)

    def everyone(b, r, t):
        return True

    def base_only(b, r, t):
        return b == 0

    def control_only(b, r, t):
        return b == 1

    def swap_cores(block, joins=everyone):
        return send(block, sizes, lambda b, r, t: (b, r, t ^ 1) if joins(b, r, t) else None)

    def swap_rows(block, joins=everyone):
        return send(block, sizes, lambda b, r, t: (b, 1 - r, t) if joins(b, r, t) else None)

    def swap_links(block, distance, joins=everyone):
        return send(
            block, sizes, lambda b, r, t: (b, r, t ^ (2 * distance)) if joins(b, r, t) else None
        )

    def padded_rows(block):
        return jnp.pad(block, ((0, SLOT - HD), (0, 0)))

    def joined(block, other):
        return jnp.concatenate([block, other], axis=0)

    def unset(*outs):
        return tuple(kernel_call(unset_kernel, [out], (spot,), copies=1, stay=True)[0] for out in outs)

    tile_shape = (images, tile, D)
    head_shape = ((images, 2, tile, half), jnp.bfloat16)
    half_head_shape = ((images, tile, half), jnp.bfloat16)
    stack_shape = ((4, SLOT, D), jnp.bfloat16)
    shared_shape = ((4, SHARED, D), jnp.bfloat16)
    rows_shape = ((2 * half, D), jnp.bfloat16)
    projections = [((tokens, 2 * half), jnp.bfloat16), ((tokens, lanes), jnp.bfloat16)]
    shard = w_zero.shape[1]
    triple_shape = ((4, 3 * SLOT, D), jnp.bfloat16)
    half_stacks = ((2, 4, SLOT, D), jnp.bfloat16)
    both_shape = ((images, 2, tile, D), jnp.bfloat16)

    keyval_piece = padded_rows(lax.dynamic_slice_in_dim(w_keyval[0].T, row * HD, HD, axis=0))
    zero_piece = lax.dynamic_slice_in_dim(w_zero.T, row * SHARED, shard - SHARED, axis=0)
    query_or_out = padded_rows(jnp.where(is_query, w_query[0].T, w_out[0]))

    out_piece = padded_rows(w_out[0])
    piece = jnp.concatenate(
        [
            keyval_piece,
            jnp.where(is_control, query_or_out, zero_piece),
            jnp.where(is_control, out_piece, query_or_out),
        ],
        axis=0,
    )
    first = [piece, swap_links(piece, ORDER[1]), swap_links(piece, ORDER[2])]
    started = after(own, piece)
    far = send(started, sizes, lambda b, r, t: (1 - b, r, t))
    corner = send(started, sizes, lambda b, r, t: (0, 1 - r, t) if b == 1 else None)
    (normed,) = kernel_call(
        norm_kernel, [(tile_shape, jnp.bfloat16)], (spot, own, far, modulation[1]),
        scratch=[(tile_shape, jnp.bfloat16), (tile_shape, jnp.bfloat16)], copies=2,
    )
    (bias,) = kernel_call(
        functools.partial(bias_kernel, 2 * tile_rows, sizes[2] * tile_cols),
        [((2 * tile, 6 * tile), jnp.float32)], (spot,), copies=1,
    )
    side = swap_rows(jnp.where(is_control, normed, own))
    side, corner, bias, *first = lax.optimization_barrier((side, corner, bias, *first))
    first.append(swap_links(first[1], ORDER[2]))
    first, head_stack, shared = kernel_call(
        stack_kernel, [triple_shape, stack_shape, shared_shape], (spot, *first),
        copies=8, stay=True,
    )
    first_other = swap_cores(first)
    out_mine = send(head_stack, sizes, lambda b, r, t: (0, r, t) if b == 1 else None)
    zero_side = swap_rows(shared, base_only)

    def halos(keyval, joins):
        def across(b, r, t):
            target = t + 1 if t % 2 else t - 1
            return (b, r, target) if joins(b, r, t) and 0 <= target < sizes[2] else None

        return send(keyval, sizes, across), swap_cores(keyval, joins)

    def neighborhood(query, keyval, outer, inner):
        (attended,) = kernel_call(
            attend_kernel, [((tokens, half), jnp.bfloat16)],
            (spot, query, outer, keyval, inner, bias),
            scratch=[((tokens, lanes), jnp.bfloat16), ((3, tokens, 2 * half), jnp.bfloat16)],
            copies=4, micros=8,
        )
        return attended.reshape(images, 2, tile, half)

    def their_heads(attended, joins):
        theirs = lax.dynamic_index_in_dim(attended, 1 - row, 1, keepdims=False)
        return swap_rows(theirs, joins)

    def head_rows(index, mine, other):
        (rows,) = kernel_call(
            functools.partial(head_rows_kernel, index), [rows_shape], (spot, mine, other),
            scratch=[half_stacks], copies=2,
        )
        return rows

    def finished(attended, side_heads, rows, more, mod):
        (out,) = kernel_call(
            final_kernel, [(tile_shape, jnp.bfloat16)],
            (spot, attended, side_heads, rows, own, more, mod),
            scratch=[half_head_shape, half_head_shape, rows_shape]
            + [(tile_shape, jnp.bfloat16), (tile_shape, jnp.bfloat16)],
            copies=4 + images,
        )
        return out

    def control_attention():
        keyval, query = kernel_call(
            project_kernel, projections, (spot, normed, side, first, first_other),
            scratch=[((2 * half + lanes, D), jnp.bfloat16), both_shape], micros=5, near=True,
        )
        attended = neighborhood(query, keyval, *halos(keyval, control_only))
        return attended

    attended = lax.cond(is_control, control_attention, lambda: unset(head_shape)[0])
    near = send(attended, sizes, lambda b, r, t: (0, r, t) if b == 1 else None)
    cross = send(attended, sizes, lambda b, r, t: (0, 1 - r, t) if b == 1 else None)

    def control_finish():
        rows = head_rows(3, swap_cores(head_stack, control_only), head_stack)
        side_heads = their_heads(attended, control_only)
        out = finished(attended, side_heads, rows, far, modulation[1])
        return unset(shared_shape, stack_shape, stack_shape) + (out,)

    def base_prepare():
        third = jnp.where(
            is_query, first_other[:, 2 * SLOT :], after(first, attended)[:, 2 * SLOT :]
        )
        zero_corner = swap_cores(zero_side, base_only)
        out_other = swap_cores(out_mine, base_only)
        return (zero_corner, out_other, third) + unset((tile_shape, jnp.bfloat16))

    zero_corner, out_other, third, control = lax.cond(
        is_control, control_finish, base_prepare
    )

    def base_finish():
        other = swap_rows(third, base_only)
        residue, keyval, query = kernel_call(
            middle_kernel,
            [(tile_shape, jnp.bfloat16)] + projections,
            (
                spot, own, far, side, corner, near, cross, out_mine, out_other, first, first_other,
                zero_side, zero_corner, modulation[1], modulation[0],
            ),
            scratch=[
                rows_shape,
                ((D, D), jnp.bfloat16),
                ((2 * half + lanes, D), jnp.bfloat16),
                both_shape,
            ],
            micros=8, near=True,
        )
        outer, inner = halos(keyval, base_only)
        attended = neighborhood(query, keyval, outer, inner)
        side_heads = their_heads(attended, base_only)
        return finished(attended, side_heads, head_rows(1, third, other), residue, modulation[0])

    out = lax.cond(is_control, lambda: control, base_finish)
    return out.reshape(latent.shape)


def solution(mesh):
    placed = (
        P("branch", None, "trow", "tcol", None),
        P(),
        P("branch", None, "tcol"),
        P("branch", None, "tcol"),
        P("branch", "tcol", None),
        P(None, "tcol"),
    )
    sizes = (mesh.shape["branch"], mesh.shape["trow"], mesh.shape["tcol"])
    body = on_device
    if sizes == (2, 2, HEADS):
        body = functools.partial(paired_rows, sizes)
    return jax.shard_map(
        body,
        mesh=mesh,
        in_specs=placed,
        out_specs=P("branch", None, "trow", "tcol", None),
        check_vma=False,
    )
```

```python
import functools
import math

import jax
import jax.numpy as jnp
from jax import lax
from jax.experimental import pallas as pl
from jax.experimental.pallas import tpu as pltpu
from jax.sharding import PartitionSpec as P

D = 1152
HD = 72
HEADS = 8
WIN = 13
HW = 576


def padded(block, sides, width):
    for axis, dim in sides:
        count = lax.axis_size(axis)
        forward = [(i, i + 1) for i in range(count - 1)]
        backward = [(target, source) for source, target in forward]
        low = lax.ppermute(
            lax.slice_in_dim(block, block.shape[dim] - width, None, axis=dim), axis, forward
        )
        high = lax.ppermute(lax.slice_in_dim(block, 0, width, axis=dim), axis, backward)
        block = jnp.concatenate([low, block, high], axis=dim)
    return block


def shifted(block, axis, distance):
    devices = range(lax.axis_size(axis))
    route = [(i - distance, i) for i in devices if i - distance in devices]
    return lax.ppermute(block, axis, route)


def modulate(hidden, shift_scale):
    average = jnp.mean(hidden, axis=-1, keepdims=True)
    centred = hidden - average
    variance = jnp.mean(centred * centred, axis=-1, keepdims=True)
    return (centred * lax.rsqrt(variance + 1e-06) * (1.0 + shift_scale[1]) + shift_scale[0]).astype(
        jnp.bfloat16
    )


def block_mask(row_first, col_first, total_rows, total_cols, key_count):
    query_edge = 8
    radius = WIN // 2
    key_side = query_edge + 2 * radius
    offsets = jnp.arange(query_edge)
    reaches = jnp.arange(key_side)
    row_starts = jnp.clip(row_first + offsets - radius, 0, total_rows - WIN)
    key_rows = row_first - radius + reaches
    row_inside = (key_rows[None, :] >= row_starts[:, None]) & (
        key_rows[None, :] < row_starts[:, None] + WIN
    )
    col_starts = jnp.clip(col_first + offsets - radius, 0, total_cols - WIN)
    key_cols = col_first - radius + reaches
    col_inside = (key_cols[None, :] >= col_starts[:, None]) & (
        key_cols[None, :] < col_starts[:, None] + WIN
    )
    joined = row_inside[:, None, :, None] & col_inside[None, :, None, :]
    joined = joined.reshape(query_edge * query_edge, key_side * key_side)
    filler = jnp.zeros((query_edge * query_edge, key_count - key_side * key_side), dtype=jnp.bool_)
    return jnp.concatenate([joined, filler], axis=1)


def edge_keys(key_values):
    radius = WIN // 2
    return padded(key_values, (("trow", 1), ("tcol", 2)), radius)


def attend_tile(queries, extended, row_anchor, col_anchor, total_rows, total_cols):
    images, tile_rows, tile_cols = (queries.shape[0], queries.shape[1], queries.shape[2])
    query_edge = 8
    radius = WIN // 2
    key_side = query_edge + 2 * radius
    key_count = (key_side * key_side + 127) // 128 * 128
    across = tile_cols // query_edge
    block_count = tile_rows // query_edge * across
    scaling = 1.0 / math.sqrt(HD)

    def one_block(position):
        row_block = position // across * query_edge
        col_block = position % across * query_edge
        query_block = queries
        query_block = query_block.reshape(images, query_edge * query_edge, HEADS, HD)
        key_block = extended
        key_block = key_block.reshape(images, key_side * key_side, 2 * HW)
        key_block = jnp.pad(key_block, ((0, 0), (0, key_count - key_side * key_side), (0, 0)))
        key_heads = key_block[..., :HW].reshape(images, key_count, HEADS, HD)
        value_heads = key_block[..., HW:].reshape(images, key_count, HEADS, HD)
        allowed = block_mask(
            row_anchor + row_block, col_anchor + col_block, total_rows, total_cols, key_count
        )
        scores = (
            jnp.einsum(
                "iqhd,ikhd->ihqk", query_block, key_heads, preferred_element_type=jnp.float32
            )
            * scaling
        )
        scores = jnp.where(allowed[None, None], scores, -1e30)
        highest = jnp.max(scores, axis=-1, keepdims=True)
        raised = jnp.exp(scores - highest)
        totals = jnp.sum(raised, axis=-1, keepdims=True)
        weights = (raised / totals).astype(jnp.bfloat16)
        blended = jnp.einsum(
            "ihqk,ikhd->iqhd", weights, value_heads, preferred_element_type=jnp.float32
        )
        return blended.astype(jnp.bfloat16).reshape(images, query_edge, query_edge, HW)

    result = lax.map(one_block, jnp.arange(block_count))
    result = result.reshape(tile_rows // query_edge, across, images, query_edge, query_edge, HW)
    return result.transpose(2, 0, 3, 1, 4, 5).reshape(images, tile_rows, tile_cols, HW)


def run_block(active, hidden, shift_scale, weight_q, weight_kv, weight_o):
    images, tile_rows, tile_cols = (hidden.shape[0], hidden.shape[1], hidden.shape[2])
    tokens = images * tile_rows * tile_cols

    def project():
        flattened = modulate(hidden, shift_scale).reshape(tokens, D)
        queries = jnp.dot(flattened, weight_q, preferred_element_type=jnp.float32).astype(
            jnp.bfloat16
        )
        key_values = jnp.dot(flattened, weight_kv, preferred_element_type=jnp.float32).astype(
            jnp.bfloat16
        )
        return (queries, key_values)

    def nothing():
        return (jnp.zeros((tokens, HW), jnp.bfloat16), jnp.zeros((tokens, 2 * HW), jnp.bfloat16))

    queries, key_values = lax.cond(active, project, nothing)
    extended = edge_keys(key_values.reshape(images, tile_rows, tile_cols, 2 * HW))
    row_anchor = lax.axis_index("trow") * tile_rows
    col_anchor = lax.axis_index("tcol") * tile_cols
    total_rows = tile_rows * lax.axis_size("trow")
    total_cols = tile_cols * lax.axis_size("tcol")

    def finish():
        attended = attend_tile(
            queries.reshape(images, tile_rows, tile_cols, HW),
            extended,
            row_anchor,
            col_anchor,
            total_rows,
            total_cols,
        )
        projected = jnp.dot(
            attended.reshape(tokens, HW), weight_o, preferred_element_type=jnp.float32
        )
        return (hidden + shift_scale[2] * projected.reshape(hidden.shape)).astype(jnp.bfloat16)

    def vacant():
        return jnp.zeros(hidden.shape, jnp.bfloat16)

    return lax.cond(active, finish, vacant)


def zero_project(control_out, weight_z):
    flattened = control_out.reshape(-1, D)
    return (
        jnp.dot(flattened, weight_z, preferred_element_type=jnp.float32)
        .astype(jnp.bfloat16)
        .reshape(control_out.shape)
    )


def on_device(latent, modulation, w_query, w_keyval, w_out, w_zero):
    sources = (w_query, w_keyval, w_out)
    weight_q, weight_kv, weight_o, weight_z = (
        lax.all_gather(sources[0], "tcol", axis=2, tiled=True),
        lax.all_gather(sources[1], "tcol", axis=2, tiled=True),
        lax.all_gather(sources[2], "tcol", axis=1, tiled=True),
        lax.all_gather(w_zero, "tcol", axis=1, tiled=True),
    )
    branch_index = lax.axis_index("branch")
    is_control = branch_index == 1
    own_copy = latent[0]
    shift_scale = lax.dynamic_index_in_dim(modulation, branch_index, 0, keepdims=False)
    received = shifted(own_copy, "branch", 1)
    control_in = own_copy.astype(jnp.float32) + received.astype(jnp.float32)
    control_out = run_block(
        is_control, control_in, shift_scale, weight_q[0], weight_kv[0], weight_o[0]
    )

    def with_projection():
        return zero_project(control_out, weight_z)

    def without_projection():
        return jnp.zeros(control_out.shape, jnp.bfloat16)

    residual = lax.cond(is_control, with_projection, without_projection)
    returned = shifted(residual, "branch", -1)
    base_in = own_copy.astype(jnp.float32) + returned.astype(jnp.float32)
    base_out = run_block(
        jnp.logical_not(is_control), base_in, shift_scale, weight_q[0], weight_kv[0], weight_o[0]
    )
    return jnp.where(is_control, control_out, base_out)[None]


AXES = ("branch", "trow", "tcol")
SLOT = 80
SHARED = 64
ORDER = (0, 3, 1, 2)


def routes(sizes, move):
    found = []
    for b in range(sizes[0]):
        for r in range(sizes[1]):
            for t in range(sizes[2]):
                target = move(b, r, t)
                if target is not None:
                    found.append((place_of(sizes, b, r, t), place_of(sizes, *target)))
    return found


def place_of(sizes, b, r, t):
    return (b * sizes[1] + r) * sizes[2] + t


def send(block, sizes, move):
    return lax.ppermute(block, AXES, routes(sizes, move))


def after(block, *earlier):
    return lax.optimization_barrier((block,) + earlier)[0]


def kernel_call(body, outs, args, scratch=(), copies=0, stay=False, micros=0, near=False, room=16):
    def space(a):
        if a.dtype == jnp.int32:
            return pltpu.SMEM
        return pltpu.VMEM if near or a.dtype == jnp.float32 else pl.ANY

    buffers = [pltpu.VMEM(shape, kind) for shape, kind in scratch]
    return pl.pallas_call(
        body,
        out_shape=[jax.ShapeDtypeStruct(shape, kind) for shape, kind in outs],
        in_specs=[pl.BlockSpec(memory_space=space(a)) for a in args],
        out_specs=[pl.BlockSpec(memory_space=pl.ANY if stay else pltpu.VMEM) for _ in outs],
        scratch_shapes=buffers + ([pltpu.SemaphoreType.DMA((copies,))] if copies else []),
        compiler_params=pltpu.CompilerParams(vmem_limit_bytes=room * 1024 * 1024),
        cost_estimate=pl.CostEstimate(
            flops=0, bytes_accessed=1 + 3_700_000 * micros, transcendentals=0
        ),
    )(*args)


def begin(copies, done, first=0):
    started = []
    for n, (source, target) in enumerate(copies):
        copy = pltpu.make_async_copy(source, target, done.at[first + n])
        copy.start()
        started.append(copy)
    return started


def finish(started):
    for copy in started:
        copy.wait()


def dot_rows(left, right):
    return lax.dot_general(left, right, (((1,), (1,)), ((), ())), preferred_element_type=jnp.float32)


def rows_at(start, count):
    return pl.ds(pl.multiple_of(start, 16), count)


def stack_kernel(spot, one, two, three, four, stacked, heads, shared, done):
    pieces = (one, two, three, four)
    started = begin([(piece, stacked.at[n]) for n, piece in enumerate(pieces)], done)

    def part(first, target):
        rows = slice(first, first + target.shape[1])
        finish(begin([(piece.at[rows], target.at[n]) for n, piece in enumerate(pieces)], done, 4))

    is_control = spot[0] == 1
    is_query = spot[3] == spot[1]
    low = spot[1] == 0
    pl.when(is_control & is_query)(lambda: part(2 * SLOT, heads))
    pl.when(is_control & jnp.logical_not(is_query))(lambda: part(SLOT, heads))
    pl.when(jnp.logical_not(is_control) & low)(lambda: part(SLOT, shared))
    pl.when(jnp.logical_not(is_control | low))(lambda: part(2 * SLOT - SHARED, shared))
    finish(started)


def norm_kernel(spot, own, far, mod, normed):
    for image in range(own.shape[0]):
        hidden = own[image].astype(jnp.float32) + far[image].astype(jnp.float32)
        normed[image] = modulate(hidden, mod)


def bias_kernel(total_rows, total_cols, spot, bias, done):
    radius = WIN // 2
    query = lax.broadcasted_iota(jnp.int32, bias.shape, 0)
    key = lax.broadcasted_iota(jnp.int32, bias.shape, 1)
    base = spot[4]
    row_start = jnp.clip((query >> 3) - radius, 0, total_rows - WIN)
    col_start = jnp.clip(base + (query & 7) - radius, 0, total_cols - WIN)
    key_row = (key & 127) >> 3
    outward = 2 * spot[3] - 1
    key_col = base + (1 - (key >> 7)) * outward * 8 + (key & 7)
    inside = (
        (key_row >= row_start)
        & (key_row < row_start + WIN)
        & (key_col >= col_start)
        & (key_col < col_start + WIN)
    )
    bias[...] = jnp.where(inside, 0.0, -1e30)


def unset_kernel(spot, out, done):
    pass


def in_order(origin):
    return (origin % 2) * 2 + origin // 2


def arrange_keyvals(link, core, mine, other, weight):
    for block, at in ((mine, core), (other, 1 - core)):
        for step in range(4):
            origin = link ^ ORDER[step]
            slot = (1 - origin // 2) * 4 + at * 2 + origin % 2
            weight[rows_at(slot * SLOT, SLOT), :] = block[step, :SLOT]


def arrange_heads(link, stack, first_row, weight):
    for step in range(4):
        start = first_row + in_order(link ^ ORDER[step]) * SLOT
        weight[rows_at(start, SLOT), :] = stack[step]


def clear_rows(weight, start, stop):
    weight[start:stop, :] = jnp.zeros((stop - start, weight.shape[1]), weight.dtype)


def arrange_queries(spot, mine, other, part, weight):
    start = weight.shape[0] - 4 * SLOT
    clear_rows(weight, 8 * SLOT, start)
    rows = slice(part * SLOT, (part + 1) * SLOT)
    own = spot[3] == spot[1]
    pl.when(own)(lambda: arrange_heads(spot[2], mine.at[:, rows], start, weight))
    pl.when(jnp.logical_not(own))(lambda: arrange_heads(spot[2], other.at[:, rows], start, weight))


def project_kernel(spot, normed, normed_other, mine, other, keyval, query, weight, both):
    row, link, core = (spot[1], spot[2], spot[3])
    arrange_keyvals(link, core, mine, other, weight)
    arrange_queries(spot, mine, other, 1, weight)
    both[:, row] = normed[...]
    both[:, 1 - row] = normed_other[...]
    tokens = both[...].reshape(-1, both.shape[3])
    projected = dot_rows(tokens, weight[...]).astype(keyval.dtype)
    keyval[...] = projected[:, : keyval.shape[1]]
    query[...] = projected[:, keyval.shape[1] :]


def attend_kernel(spot, queries, outer, here, inner, bias, out):
    scaling = math.log2(math.e) / math.sqrt(HD)
    tokens = bias.shape[0]
    images = out.shape[0] // tokens
    parts = (outer, here, inner)
    key_lanes = queries.shape[1]
    first_key = here.shape[1] - key_lanes
    heads = out.shape[1] // SLOT
    pad = key_lanes - heads * SLOT
    value_lanes = (out.shape[1] + 127) // 128 * 128
    query_lane = lax.broadcasted_iota(jnp.int32, (tokens, key_lanes), 1) - pad
    value_lane = lax.broadcasted_iota(jnp.int32, (tokens, value_lanes), 1)

    def within(lane, head):
        return (lane >= head * SLOT) & (lane < (head + 1) * SLOT)

    for image in range(images):
        rows = slice(image * tokens, (image + 1) * tokens)
        keys = jnp.concatenate([part[rows, first_key:] for part in parts], axis=0)
        values = jnp.concatenate([part[rows, :value_lanes] for part in parts], axis=0)
        query = queries[rows, :].astype(jnp.float32)
        split = [jnp.where(within(query_lane, head), query, 0.0) for head in range(heads)]
        scores = dot_rows(jnp.concatenate(split, axis=0).astype(jnp.bfloat16), keys)
        raised, sums = ([], [])
        for head in range(heads):
            part = scores[head * tokens : (head + 1) * tokens] * scaling + bias[...]
            part = jnp.exp2(part - jnp.max(part, axis=-1, keepdims=True))
            sums.append(1.0 / jnp.sum(part, axis=-1, keepdims=True))
            raised.append(part.astype(jnp.bfloat16))
        blended = jnp.dot(
            jnp.concatenate(raised, axis=0), values, preferred_element_type=jnp.float32
        )
        total = jnp.zeros((tokens, value_lanes), jnp.float32)
        for head in range(heads):
            part = blended[head * tokens : (head + 1) * tokens] * sums[head]
            total = jnp.where(within(value_lane, head), part, total)
        out[rows, :] = total[:, : out.shape[1]].astype(out.dtype)


def head_rows_kernel(index, spot, mine, other, out, outs, done):
    at = spot[index]
    copies = [(mine, outs.at[1 - at]), (other, outs.at[at])]
    finish(begin(copies, done))
    for part in range(2):
        arrange_heads(spot[2], outs.at[part], part * 4 * SLOT, out)


def middle_kernel(
    spot, own, far, side, corner, near, cross, out_mine, out_other, first, first_other,
    zero_side, zero_corner, mod, mod_base, residue, keyval, query,
    w_out, w_zero, weight, both,
):
    row, link, core = (spot[1], spot[2], spot[3])
    images, tokens, _ = own.shape
    tile = images * tokens
    width = near.shape[3]
    for block, at in ((out_mine, core), (out_other, 1 - core)):
        arrange_heads(link, block, at * width, w_out)
    shard = w_zero.shape[0] // 8
    kept = shard - SHARED
    for block, part, at in (
        (first, zero_side, core),
        (first_other, zero_corner, 1 - core),
    ):
        for step in range(4):
            start = (2 * (link ^ ORDER[step]) + at) * shard
            w_zero[rows_at(start + row * SHARED, kept), :] = block[step, SLOT : 2 * SLOT]
            w_zero[rows_at(start + (1 - row) * kept, SHARED), :] = part[step]
    arrange_keyvals(link, core, first, first_other, weight)
    arrange_queries(spot, first, first_other, 2, weight)

    def ordered(ref):
        return jnp.concatenate([ref[i, s] for s in (row, 1 - row) for i in range(images)], axis=0)

    def stacked(one, two):
        parts = [ref[i] for ref in (one, two) for i in range(images)]
        return jnp.concatenate(parts, axis=0).astype(jnp.float32)

    projected = jnp.dot(
        ordered(near), w_out[rows_at(row * width, width), :], preferred_element_type=jnp.float32
    )
    projected += jnp.dot(
        ordered(cross),
        w_out[rows_at((1 - row) * width, width), :],
        preferred_element_type=jnp.float32,
    )
    base = stacked(own, side)
    out = (base + stacked(far, corner) + mod[2] * projected).astype(jnp.bfloat16)
    residual = dot_rows(out, w_zero[...]).astype(jnp.bfloat16)
    base = base + residual.astype(jnp.float32)
    result = modulate(base, mod_base)
    for image in range(images):
        rows = slice(image * tokens, (image + 1) * tokens)
        residue[image] = residual[rows]
        both[image, row] = result[rows]
        both[image, 1 - row] = result[tile + image * tokens : tile + (image + 1) * tokens]
    rows = both[...].reshape(2 * tile, both.shape[3])
    projected = dot_rows(rows, weight[...]).astype(keyval.dtype)
    keyval[...] = projected[:, : keyval.shape[1]]
    query[...] = projected[:, keyval.shape[1] :]


def final_kernel(spot, attended, side, head_rows, own, more, mod, out, result, done):
    row = spot[1]
    images = out.shape[0]
    width = side.shape[2]
    near = jnp.concatenate([attended[i, row] for i in range(images)], axis=0)
    far = jnp.concatenate([side[i] for i in range(images)], axis=0)
    projected = jnp.dot(
        near, head_rows[rows_at(row * width, width), :], preferred_element_type=jnp.float32
    )
    projected += jnp.dot(
        far, head_rows[rows_at((1 - row) * width, width), :], preferred_element_type=jnp.float32
    )
    tokens = out.shape[1]
    for image in range(images):
        rows = slice(image * tokens, (image + 1) * tokens)
        base = own[image].astype(jnp.float32) + more[image].astype(jnp.float32)
        result[image] = (base + mod[2] * projected[rows]).astype(out.dtype)
    finish(begin([(result, out)], done))


def paired_rows(sizes, latent, modulation, w_query, w_keyval, w_out, w_zero):
    branch = lax.axis_index("branch")
    row = lax.axis_index("trow")
    column = lax.axis_index("tcol")
    core = column % 2
    is_control = branch == 1
    is_query = core == row
    _, images, tile_rows, tile_cols, _ = latent.shape
    tile = tile_rows * tile_cols
    tokens = images * 2 * tile
    half = HEADS // 2 * SLOT
    lanes = half + half % 128
    spot = jnp.stack([branch, row, column // 2, core, column * tile_cols]).astype(jnp.int32)
    own = latent.reshape(images, tile, D)

    def everyone(b, r, t):
        return True

    def base_only(b, r, t):
        return b == 0

    def control_only(b, r, t):
        return b == 1

    def swap_cores(block, joins=everyone):
        return send(block, sizes, lambda b, r, t: (b, r, t ^ 1) if joins(b, r, t) else None)

    def swap_rows(block, joins=everyone):
        return send(block, sizes, lambda b, r, t: (b, 1 - r, t) if joins(b, r, t) else None)

    def swap_links(block, distance, joins=everyone):
        return send(
            block, sizes, lambda b, r, t: (b, r, t ^ (2 * distance)) if joins(b, r, t) else None
        )

    def padded_rows(block):
        return jnp.pad(block, ((0, SLOT - HD), (0, 0)))

    def joined(block, other):
        return jnp.concatenate([block, other], axis=0)

    def unset(*outs):
        return tuple(kernel_call(unset_kernel, [out], (spot,), copies=1, stay=True)[0] for out in outs)

    tile_shape = (images, tile, D)
    head_shape = ((images, 2, tile, half), jnp.bfloat16)
    stack_shape = ((4, SLOT, D), jnp.bfloat16)
    shared_shape = ((4, SHARED, D), jnp.bfloat16)
    rows_shape = ((2 * half, D), jnp.bfloat16)
    projections = [((tokens, 2 * half), jnp.bfloat16), ((tokens, lanes), jnp.bfloat16)]
    shard = w_zero.shape[1]
    triple_shape = ((4, 3 * SLOT, D), jnp.bfloat16)
    half_stacks = ((2, 4, SLOT, D), jnp.bfloat16)
    both_shape = ((images, 2, tile, D), jnp.bfloat16)

    keyval_piece = padded_rows(lax.dynamic_slice_in_dim(w_keyval[0].T, row * HD, HD, axis=0))
    zero_piece = lax.dynamic_slice_in_dim(w_zero.T, row * SHARED, shard - SHARED, axis=0)
    query_or_out = padded_rows(jnp.where(is_query, w_query[0].T, w_out[0]))

    out_piece = padded_rows(w_out[0])
    piece = jnp.concatenate(
        [
            keyval_piece,
            jnp.where(is_control, query_or_out, zero_piece),
            jnp.where(is_control, out_piece, query_or_out),
        ],
        axis=0,
    )
    first = [piece, swap_links(piece, ORDER[1]), swap_links(piece, ORDER[2])]
    started = after(own, piece)
    far = send(started, sizes, lambda b, r, t: (1 - b, r, t))
    corner = send(started, sizes, lambda b, r, t: (0, 1 - r, t) if b == 1 else None)
    (normed,) = kernel_call(
        norm_kernel, [(tile_shape, jnp.bfloat16)], (spot, own, far, modulation[1]),
        near=True,
    )
    (bias,) = kernel_call(
        functools.partial(bias_kernel, 2 * tile_rows, sizes[2] * tile_cols),
        [((2 * tile, 6 * tile), jnp.float32)], (spot,), copies=1,
    )
    side = swap_rows(jnp.where(is_control, normed, own))
    side, corner, bias, *first = lax.optimization_barrier((side, corner, bias, *first))
    first.append(swap_links(first[1], ORDER[2]))
    first, head_stack, shared = kernel_call(
        stack_kernel, [triple_shape, stack_shape, shared_shape], (spot, *first),
        copies=8, stay=True,
    )
    first_other = swap_cores(first)
    out_mine = send(head_stack, sizes, lambda b, r, t: (0, r, t) if b == 1 else None)
    zero_side = swap_rows(shared, base_only)

    def halos(keyval, joins):
        def across(b, r, t):
            target = t + 1 if t % 2 else t - 1
            return (b, r, target) if joins(b, r, t) and 0 <= target < sizes[2] else None

        return send(keyval, sizes, across), swap_cores(keyval, joins)

    def neighborhood(query, keyval, outer, inner):
        (attended,) = kernel_call(
            attend_kernel, [((tokens, half), jnp.bfloat16)],
            (spot, query, outer, keyval, inner, bias),
            micros=8, near=True,
        )
        return attended.reshape(images, 2, tile, half)

    def their_heads(attended, joins):
        theirs = lax.dynamic_index_in_dim(attended, 1 - row, 1, keepdims=False)
        return swap_rows(theirs, joins)

    def head_rows(index, mine, other):
        (rows,) = kernel_call(
            functools.partial(head_rows_kernel, index), [rows_shape], (spot, mine, other),
            scratch=[half_stacks], copies=2,
        )
        return rows

    def finished(attended, side_heads, rows, more, mod):
        (out,) = kernel_call(
            final_kernel, [(tile_shape, jnp.bfloat16)],
            (spot, attended, side_heads, rows, own, more, mod),
            scratch=[(tile_shape, jnp.bfloat16)], copies=1, near=True, stay=True,
        )
        return out

    def control_attention():
        keyval, query = kernel_call(
            project_kernel, projections, (spot, normed, side, first, first_other),
            scratch=[((2 * half + lanes, D), jnp.bfloat16), both_shape], micros=5, near=True, room=24,
        )
        attended = neighborhood(query, keyval, *halos(keyval, control_only))
        return attended

    attended = lax.cond(is_control, control_attention, lambda: unset(head_shape)[0])
    near = send(attended, sizes, lambda b, r, t: (0, r, t) if b == 1 else None)
    cross = send(attended, sizes, lambda b, r, t: (0, 1 - r, t) if b == 1 else None)

    def control_finish():
        rows = head_rows(3, swap_cores(head_stack, control_only), head_stack)
        side_heads = their_heads(attended, control_only)
        out = finished(attended, side_heads, rows, far, modulation[1])
        return unset(shared_shape, stack_shape, stack_shape) + (out,)

    def base_prepare():
        third = jnp.where(
            is_query, first_other[:, 2 * SLOT :], after(first, attended)[:, 2 * SLOT :]
        )
        zero_corner = swap_cores(zero_side, base_only)
        out_other = swap_cores(out_mine, base_only)
        return (zero_corner, out_other, third) + unset((tile_shape, jnp.bfloat16))

    zero_corner, out_other, third, control = lax.cond(
        is_control, control_finish, base_prepare
    )

    def base_finish():
        other = swap_rows(third, base_only)
        residue, keyval, query = kernel_call(
            middle_kernel,
            [(tile_shape, jnp.bfloat16)] + projections,
            (
                spot, own, far, side, corner, near, cross, out_mine, out_other, first, first_other,
                zero_side, zero_corner, modulation[1], modulation[0],
            ),
            scratch=[
                rows_shape,
                ((D, D), jnp.bfloat16),
                ((2 * half + lanes, D), jnp.bfloat16),
                both_shape,
            ],
            micros=8, near=True, room=32,
        )
        outer, inner = halos(keyval, base_only)
        attended = neighborhood(query, keyval, outer, inner)
        side_heads = their_heads(attended, base_only)
        return finished(attended, side_heads, head_rows(1, third, other), residue, modulation[0])

    out = lax.cond(is_control, lambda: control, base_finish)
    return out.reshape(latent.shape)


def solution(mesh):
    placed = (
        P("branch", None, "trow", "tcol", None),
        P(),
        P("branch", None, "tcol"),
        P("branch", None, "tcol"),
        P("branch", "tcol", None),
        P(None, "tcol"),
    )
    sizes = (mesh.shape["branch"], mesh.shape["trow"], mesh.shape["tcol"])
    body = on_device
    if sizes == (2, 2, HEADS):
        body = functools.partial(paired_rows, sizes)
    return jax.shard_map(
        body,
        mesh=mesh,
        in_specs=placed,
        out_specs=P("branch", None, "trow", "tcol", None),
        check_vma=False,
    )
```

```python
import functools
import math

import jax
import jax.numpy as jnp
from jax import lax
from jax.experimental import pallas as pl
from jax.experimental.pallas import tpu as pltpu
from jax.sharding import PartitionSpec as P

D = 1152
HD = 72
HEADS = 8
WIN = 13
HW = 576


def padded(block, sides, width):
    for axis, dim in sides:
        count = lax.axis_size(axis)
        forward = [(i, i + 1) for i in range(count - 1)]
        backward = [(target, source) for source, target in forward]
        low = lax.ppermute(
            lax.slice_in_dim(block, block.shape[dim] - width, None, axis=dim), axis, forward
        )
        high = lax.ppermute(lax.slice_in_dim(block, 0, width, axis=dim), axis, backward)
        block = jnp.concatenate([low, block, high], axis=dim)
    return block


def shifted(block, axis, distance):
    devices = range(lax.axis_size(axis))
    route = [(i - distance, i) for i in devices if i - distance in devices]
    return lax.ppermute(block, axis, route)


def modulate(hidden, shift_scale):
    average = jnp.mean(hidden, axis=-1, keepdims=True)
    centred = hidden - average
    variance = jnp.mean(centred * centred, axis=-1, keepdims=True)
    return (centred * lax.rsqrt(variance + 1e-06) * (1.0 + shift_scale[1]) + shift_scale[0]).astype(
        jnp.bfloat16
    )


def block_mask(row_first, col_first, total_rows, total_cols, key_count):
    query_edge = 8
    radius = WIN // 2
    key_side = query_edge + 2 * radius
    offsets = jnp.arange(query_edge)
    reaches = jnp.arange(key_side)
    row_starts = jnp.clip(row_first + offsets - radius, 0, total_rows - WIN)
    key_rows = row_first - radius + reaches
    row_inside = (key_rows[None, :] >= row_starts[:, None]) & (
        key_rows[None, :] < row_starts[:, None] + WIN
    )
    col_starts = jnp.clip(col_first + offsets - radius, 0, total_cols - WIN)
    key_cols = col_first - radius + reaches
    col_inside = (key_cols[None, :] >= col_starts[:, None]) & (
        key_cols[None, :] < col_starts[:, None] + WIN
    )
    joined = row_inside[:, None, :, None] & col_inside[None, :, None, :]
    joined = joined.reshape(query_edge * query_edge, key_side * key_side)
    filler = jnp.zeros((query_edge * query_edge, key_count - key_side * key_side), dtype=jnp.bool_)
    return jnp.concatenate([joined, filler], axis=1)


def edge_keys(key_values):
    radius = WIN // 2
    return padded(key_values, (("trow", 1), ("tcol", 2)), radius)


def attend_tile(queries, extended, row_anchor, col_anchor, total_rows, total_cols):
    images, tile_rows, tile_cols = (queries.shape[0], queries.shape[1], queries.shape[2])
    query_edge = 8
    radius = WIN // 2
    key_side = query_edge + 2 * radius
    key_count = (key_side * key_side + 127) // 128 * 128
    across = tile_cols // query_edge
    block_count = tile_rows // query_edge * across
    scaling = 1.0 / math.sqrt(HD)

    def one_block(position):
        row_block = position // across * query_edge
        col_block = position % across * query_edge
        query_block = queries
        query_block = query_block.reshape(images, query_edge * query_edge, HEADS, HD)
        key_block = extended
        key_block = key_block.reshape(images, key_side * key_side, 2 * HW)
        key_block = jnp.pad(key_block, ((0, 0), (0, key_count - key_side * key_side), (0, 0)))
        key_heads = key_block[..., :HW].reshape(images, key_count, HEADS, HD)
        value_heads = key_block[..., HW:].reshape(images, key_count, HEADS, HD)
        allowed = block_mask(
            row_anchor + row_block, col_anchor + col_block, total_rows, total_cols, key_count
        )
        scores = (
            jnp.einsum(
                "iqhd,ikhd->ihqk", query_block, key_heads, preferred_element_type=jnp.float32
            )
            * scaling
        )
        scores = jnp.where(allowed[None, None], scores, -1e30)
        highest = jnp.max(scores, axis=-1, keepdims=True)
        raised = jnp.exp(scores - highest)
        totals = jnp.sum(raised, axis=-1, keepdims=True)
        weights = (raised / totals).astype(jnp.bfloat16)
        blended = jnp.einsum(
            "ihqk,ikhd->iqhd", weights, value_heads, preferred_element_type=jnp.float32
        )
        return blended.astype(jnp.bfloat16).reshape(images, query_edge, query_edge, HW)

    result = lax.map(one_block, jnp.arange(block_count))
    result = result.reshape(tile_rows // query_edge, across, images, query_edge, query_edge, HW)
    return result.transpose(2, 0, 3, 1, 4, 5).reshape(images, tile_rows, tile_cols, HW)


def run_block(active, hidden, shift_scale, weight_q, weight_kv, weight_o):
    images, tile_rows, tile_cols = (hidden.shape[0], hidden.shape[1], hidden.shape[2])
    tokens = images * tile_rows * tile_cols

    def project():
        flattened = modulate(hidden, shift_scale).reshape(tokens, D)
        queries = jnp.dot(flattened, weight_q, preferred_element_type=jnp.float32).astype(
            jnp.bfloat16
        )
        key_values = jnp.dot(flattened, weight_kv, preferred_element_type=jnp.float32).astype(
            jnp.bfloat16
        )
        return (queries, key_values)

    def nothing():
        return (jnp.zeros((tokens, HW), jnp.bfloat16), jnp.zeros((tokens, 2 * HW), jnp.bfloat16))

    queries, key_values = lax.cond(active, project, nothing)
    extended = edge_keys(key_values.reshape(images, tile_rows, tile_cols, 2 * HW))
    row_anchor = lax.axis_index("trow") * tile_rows
    col_anchor = lax.axis_index("tcol") * tile_cols
    total_rows = tile_rows * lax.axis_size("trow")
    total_cols = tile_cols * lax.axis_size("tcol")

    def finish():
        attended = attend_tile(
            queries.reshape(images, tile_rows, tile_cols, HW),
            extended,
            row_anchor,
            col_anchor,
            total_rows,
            total_cols,
        )
        projected = jnp.dot(
            attended.reshape(tokens, HW), weight_o, preferred_element_type=jnp.float32
        )
        return (hidden + shift_scale[2] * projected.reshape(hidden.shape)).astype(jnp.bfloat16)

    def vacant():
        return jnp.zeros(hidden.shape, jnp.bfloat16)

    return lax.cond(active, finish, vacant)


def zero_project(control_out, weight_z):
    flattened = control_out.reshape(-1, D)
    return (
        jnp.dot(flattened, weight_z, preferred_element_type=jnp.float32)
        .astype(jnp.bfloat16)
        .reshape(control_out.shape)
    )


def on_device(latent, modulation, w_query, w_keyval, w_out, w_zero):
    sources = (w_query, w_keyval, w_out)
    weight_q, weight_kv, weight_o, weight_z = (
        lax.all_gather(sources[0], "tcol", axis=2, tiled=True),
        lax.all_gather(sources[1], "tcol", axis=2, tiled=True),
        lax.all_gather(sources[2], "tcol", axis=1, tiled=True),
        lax.all_gather(w_zero, "tcol", axis=1, tiled=True),
    )
    branch_index = lax.axis_index("branch")
    is_control = branch_index == 1
    own_copy = latent[0]
    shift_scale = lax.dynamic_index_in_dim(modulation, branch_index, 0, keepdims=False)
    received = shifted(own_copy, "branch", 1)
    control_in = own_copy.astype(jnp.float32) + received.astype(jnp.float32)
    control_out = run_block(
        is_control, control_in, shift_scale, weight_q[0], weight_kv[0], weight_o[0]
    )

    def with_projection():
        return zero_project(control_out, weight_z)

    def without_projection():
        return jnp.zeros(control_out.shape, jnp.bfloat16)

    residual = lax.cond(is_control, with_projection, without_projection)
    returned = shifted(residual, "branch", -1)
    base_in = own_copy.astype(jnp.float32) + returned.astype(jnp.float32)
    base_out = run_block(
        jnp.logical_not(is_control), base_in, shift_scale, weight_q[0], weight_kv[0], weight_o[0]
    )
    return jnp.where(is_control, control_out, base_out)[None]


AXES = ("branch", "trow", "tcol")
SLOT = 80
SHARED = 64
ORDER = (0, 3, 1, 2)


def routes(sizes, move):
    found = []
    for b in range(sizes[0]):
        for r in range(sizes[1]):
            for t in range(sizes[2]):
                target = move(b, r, t)
                if target is not None:
                    found.append((place_of(sizes, b, r, t), place_of(sizes, *target)))
    return found


def place_of(sizes, b, r, t):
    return (b * sizes[1] + r) * sizes[2] + t


def send(block, sizes, move):
    return lax.ppermute(block, AXES, routes(sizes, move))


def after(block, *earlier):
    return lax.optimization_barrier((block,) + earlier)[0]


def kernel_call(body, outs, args, scratch=(), copies=0, stay=False, micros=0, near=False, room=16):
    def space(a):
        if a.dtype == jnp.int32:
            return pltpu.SMEM
        return pltpu.VMEM if near or a.dtype == jnp.float32 else pl.ANY

    buffers = [pltpu.VMEM(shape, kind) for shape, kind in scratch]
    return pl.pallas_call(
        body,
        out_shape=[jax.ShapeDtypeStruct(shape, kind) for shape, kind in outs],
        in_specs=[pl.BlockSpec(memory_space=space(a)) for a in args],
        out_specs=[pl.BlockSpec(memory_space=pl.ANY if stay else pltpu.VMEM) for _ in outs],
        scratch_shapes=buffers + ([pltpu.SemaphoreType.DMA((copies,))] if copies else []),
        compiler_params=pltpu.CompilerParams(vmem_limit_bytes=room * 1024 * 1024),
        cost_estimate=pl.CostEstimate(
            flops=0, bytes_accessed=1 + 3_700_000 * micros, transcendentals=0
        ),
    )(*args)


def begin(copies, done, first=0):
    started = []
    for n, (source, target) in enumerate(copies):
        copy = pltpu.make_async_copy(source, target, done.at[first + n])
        copy.start()
        started.append(copy)
    return started


def finish(started):
    for copy in started:
        copy.wait()


def dot_rows(left, right):
    return lax.dot_general(left, right, (((1,), (1,)), ((), ())), preferred_element_type=jnp.float32)


def rows_at(start, count):
    return pl.ds(pl.multiple_of(start, 16), count)


def stack_kernel(spot, one, two, three, four, stacked, heads, shared, done):
    pieces = (one, two, three, four)
    started = begin([(piece, stacked.at[n]) for n, piece in enumerate(pieces)], done)

    def part(first, target):
        rows = slice(first, first + target.shape[1])
        finish(begin([(piece.at[rows], target.at[n]) for n, piece in enumerate(pieces)], done, 4))

    is_control = spot[0] == 1
    is_query = spot[3] == spot[1]
    low = spot[1] == 0
    pl.when(is_control & is_query)(lambda: part(2 * SLOT, heads))
    pl.when(is_control & jnp.logical_not(is_query))(lambda: part(SLOT, heads))
    pl.when(jnp.logical_not(is_control) & low)(lambda: part(SLOT, shared))
    pl.when(jnp.logical_not(is_control | low))(lambda: part(2 * SLOT - SHARED, shared))
    finish(started)


def norm_kernel(spot, own, far, mod, normed):
    for image in range(own.shape[0]):
        hidden = own[image].astype(jnp.float32) + far[image].astype(jnp.float32)
        normed[image] = modulate(hidden, mod)


def bias_kernel(total_rows, total_cols, spot, bias, done):
    radius = WIN // 2
    query = lax.broadcasted_iota(jnp.int32, bias.shape, 0)
    key = lax.broadcasted_iota(jnp.int32, bias.shape, 1)
    base = spot[4]
    row_start = jnp.clip((query >> 3) - radius, 0, total_rows - WIN)
    col_start = jnp.clip(base + (query & 7) - radius, 0, total_cols - WIN)
    key_row = (key & 127) >> 3
    outward = 2 * spot[3] - 1
    key_col = base + (1 - (key >> 7)) * outward * 8 + (key & 7)
    inside = (
        (key_row >= row_start)
        & (key_row < row_start + WIN)
        & (key_col >= col_start)
        & (key_col < col_start + WIN)
    )
    bias[...] = jnp.where(inside, 0.0, -1e30)


def unset_kernel(spot, out, done):
    pass


def in_order(origin):
    return (origin % 2) * 2 + origin // 2


def arrange_keyvals(link, core, mine, other, weight):
    for block, at in ((mine, core), (other, 1 - core)):
        for step in range(4):
            origin = link ^ ORDER[step]
            slot = (1 - origin // 2) * 4 + at * 2 + origin % 2
            weight[rows_at(slot * SLOT, SLOT), :] = block[step, :SLOT]


def arrange_heads(link, stack, first_row, weight):
    for step in range(4):
        start = first_row + in_order(link ^ ORDER[step]) * SLOT
        weight[rows_at(start, SLOT), :] = stack[step]


def clear_rows(weight, start, stop):
    weight[start:stop, :] = jnp.zeros((stop - start, weight.shape[1]), weight.dtype)


def arrange_queries(spot, mine, other, part, weight):
    start = weight.shape[0] - 4 * SLOT
    clear_rows(weight, 8 * SLOT, start)
    rows = slice(part * SLOT, (part + 1) * SLOT)
    own = spot[3] == spot[1]
    pl.when(own)(lambda: arrange_heads(spot[2], mine.at[:, rows], start, weight))
    pl.when(jnp.logical_not(own))(lambda: arrange_heads(spot[2], other.at[:, rows], start, weight))


def project_kernel(spot, normed, normed_other, mine, other, keyval, query, weight, both):
    row, link, core = (spot[1], spot[2], spot[3])
    arrange_keyvals(link, core, mine, other, weight)
    arrange_queries(spot, mine, other, 1, weight)
    both[:, row] = normed[...]
    both[:, 1 - row] = normed_other[...]
    tokens = both[...].reshape(-1, both.shape[3])
    projected = dot_rows(tokens, weight[...]).astype(keyval.dtype)
    keyval[...] = projected[:, : keyval.shape[1]]
    query[...] = projected[:, keyval.shape[1] :]


def attend_kernel(spot, queries, outer, here, inner, bias, out):
    scaling = math.log2(math.e) / math.sqrt(HD)
    tokens = bias.shape[0]
    images = queries.shape[0] // tokens
    parts = (outer, here, inner)
    key_lanes = queries.shape[1]
    first_key = here.shape[1] - key_lanes
    width = out.shape[1] // images
    heads = width // SLOT
    results = []
    pad = key_lanes - heads * SLOT
    value_lanes = (width + 127) // 128 * 128
    query_lane = lax.broadcasted_iota(jnp.int32, (tokens, key_lanes), 1) - pad
    value_lane = lax.broadcasted_iota(jnp.int32, (tokens, value_lanes), 1)

    def within(lane, head):
        return (lane >= head * SLOT) & (lane < (head + 1) * SLOT)

    for image in range(images):
        rows = slice(image * tokens, (image + 1) * tokens)
        keys = jnp.concatenate([part[rows, first_key:] for part in parts], axis=0)
        values = jnp.concatenate([part[rows, :value_lanes] for part in parts], axis=0)
        query = queries[rows, :].astype(jnp.float32)
        split = [jnp.where(within(query_lane, head), query, 0.0) for head in range(heads)]
        scores = dot_rows(jnp.concatenate(split, axis=0).astype(jnp.bfloat16), keys)
        raised, sums = ([], [])
        for head in range(heads):
            part = scores[head * tokens : (head + 1) * tokens] * scaling + bias[...]
            part = jnp.exp2(part - jnp.max(part, axis=-1, keepdims=True))
            sums.append(1.0 / jnp.sum(part, axis=-1, keepdims=True))
            raised.append(part.astype(jnp.bfloat16))
        blended = jnp.dot(
            jnp.concatenate(raised, axis=0), values, preferred_element_type=jnp.float32
        )
        total = jnp.zeros((tokens, value_lanes), jnp.float32)
        for head in range(heads):
            part = blended[head * tokens : (head + 1) * tokens] * sums[head]
            total = jnp.where(within(value_lane, head), part, total)
        results.append(total[:, :width])
    out[...] = jnp.concatenate(results, axis=1).astype(out.dtype)


def head_rows_kernel(index, spot, mine, other, out, outs, done):
    at = spot[index]
    copies = [(mine, outs.at[1 - at]), (other, outs.at[at])]
    finish(begin(copies, done))
    for part in range(2):
        arrange_heads(spot[2], outs.at[part], part * 4 * SLOT, out)


def middle_kernel(
    spot, own, far, side, corner, near, cross, out_mine, out_other, first, first_other,
    zero_side, zero_corner, mod, mod_base, residue, keyval, query,
    w_out, w_zero, weight, both,
):
    row, link, core = (spot[1], spot[2], spot[3])
    images, tokens, _ = own.shape
    tile = images * tokens
    width = near.shape[2] // images
    for block, at in ((out_mine, core), (out_other, 1 - core)):
        arrange_heads(link, block, at * width, w_out)
    shard = w_zero.shape[0] // 8
    kept = shard - SHARED
    for block, part, at in (
        (first, zero_side, core),
        (first_other, zero_corner, 1 - core),
    ):
        for step in range(4):
            start = (2 * (link ^ ORDER[step]) + at) * shard
            w_zero[rows_at(start + row * SHARED, kept), :] = block[step, SLOT : 2 * SLOT]
            w_zero[rows_at(start + (1 - row) * kept, SHARED), :] = part[step]
    arrange_keyvals(link, core, first, first_other, weight)
    arrange_queries(spot, first, first_other, 2, weight)

    def ordered(ref):
        parts = [
            ref[s][:, i * width : (i + 1) * width] for s in (row, 1 - row) for i in range(images)
        ]
        return jnp.concatenate(parts, axis=0)

    def stacked(one, two):
        parts = [ref[i] for ref in (one, two) for i in range(images)]
        return jnp.concatenate(parts, axis=0).astype(jnp.float32)

    projected = jnp.dot(
        ordered(near), w_out[rows_at(row * width, width), :], preferred_element_type=jnp.float32
    )
    projected += jnp.dot(
        ordered(cross),
        w_out[rows_at((1 - row) * width, width), :],
        preferred_element_type=jnp.float32,
    )
    base = stacked(own, side)
    out = (base + stacked(far, corner) + mod[2] * projected).astype(jnp.bfloat16)
    residual = dot_rows(out, w_zero[...]).astype(jnp.bfloat16)
    base = base + residual.astype(jnp.float32)
    result = modulate(base, mod_base)
    for image in range(images):
        rows = slice(image * tokens, (image + 1) * tokens)
        residue[image] = residual[rows]
        both[image, row] = result[rows]
        both[image, 1 - row] = result[tile + image * tokens : tile + (image + 1) * tokens]
    rows = both[...].reshape(2 * tile, both.shape[3])
    projected = dot_rows(rows, weight[...]).astype(keyval.dtype)
    keyval[...] = projected[:, : keyval.shape[1]]
    query[...] = projected[:, keyval.shape[1] :]


def final_kernel(spot, attended, side, head_rows, own, more, mod, out, result, done):
    row = spot[1]
    images = out.shape[0]
    width = side.shape[1] // images

    def flat(block):
        parts = [block[:, i * width : (i + 1) * width] for i in range(images)]
        return jnp.concatenate(parts, axis=0)

    near, far = (flat(attended[row]), flat(side[...]))
    projected = jnp.dot(
        near, head_rows[rows_at(row * width, width), :], preferred_element_type=jnp.float32
    )
    projected += jnp.dot(
        far, head_rows[rows_at((1 - row) * width, width), :], preferred_element_type=jnp.float32
    )
    tokens = out.shape[1]
    for image in range(images):
        rows = slice(image * tokens, (image + 1) * tokens)
        base = own[image].astype(jnp.float32) + more[image].astype(jnp.float32)
        result[image] = (base + mod[2] * projected[rows]).astype(out.dtype)
    finish(begin([(result, out)], done))


def paired_rows(sizes, latent, modulation, w_query, w_keyval, w_out, w_zero):
    branch = lax.axis_index("branch")
    row = lax.axis_index("trow")
    column = lax.axis_index("tcol")
    core = column % 2
    is_control = branch == 1
    is_query = core == row
    _, images, tile_rows, tile_cols, _ = latent.shape
    tile = tile_rows * tile_cols
    tokens = images * 2 * tile
    half = HEADS // 2 * SLOT
    lanes = half + half % 128
    spot = jnp.stack([branch, row, column // 2, core, column * tile_cols]).astype(jnp.int32)
    own = latent.reshape(images, tile, D)

    def everyone(b, r, t):
        return True

    def base_only(b, r, t):
        return b == 0

    def control_only(b, r, t):
        return b == 1

    def swap_cores(block, joins=everyone):
        return send(block, sizes, lambda b, r, t: (b, r, t ^ 1) if joins(b, r, t) else None)

    def swap_rows(block, joins=everyone):
        return send(block, sizes, lambda b, r, t: (b, 1 - r, t) if joins(b, r, t) else None)

    def swap_links(block, distance, joins=everyone):
        return send(
            block, sizes, lambda b, r, t: (b, r, t ^ (2 * distance)) if joins(b, r, t) else None
        )

    def padded_rows(block):
        return jnp.pad(block, ((0, SLOT - HD), (0, 0)))

    def joined(block, other):
        return jnp.concatenate([block, other], axis=0)

    def unset(*outs):
        return tuple(kernel_call(unset_kernel, [out], (spot,), copies=1, stay=True)[0] for out in outs)

    tile_shape = (images, tile, D)
    head_shape = ((2, tile, images * half), jnp.bfloat16)
    half_head_shape = ((tile, images * half), jnp.bfloat16)
    stack_shape = ((4, SLOT, D), jnp.bfloat16)
    shared_shape = ((4, SHARED, D), jnp.bfloat16)
    rows_shape = ((2 * half, D), jnp.bfloat16)
    projections = [((tokens, 2 * half), jnp.bfloat16), ((tokens, lanes), jnp.bfloat16)]
    shard = w_zero.shape[1]
    triple_shape = ((4, 3 * SLOT, D), jnp.bfloat16)
    half_stacks = ((2, 4, SLOT, D), jnp.bfloat16)
    both_shape = ((images, 2, tile, D), jnp.bfloat16)

    keyval_piece = padded_rows(lax.dynamic_slice_in_dim(w_keyval[0].T, row * HD, HD, axis=0))
    zero_piece = lax.dynamic_slice_in_dim(w_zero.T, row * SHARED, shard - SHARED, axis=0)
    query_or_out = padded_rows(jnp.where(is_query, w_query[0].T, w_out[0]))

    out_piece = padded_rows(w_out[0])
    piece = jnp.concatenate(
        [
            keyval_piece,
            jnp.where(is_control, query_or_out, zero_piece),
            jnp.where(is_control, out_piece, query_or_out),
        ],
        axis=0,
    )
    first = [piece, swap_links(piece, ORDER[1]), swap_links(piece, ORDER[2])]
    started = after(own, piece)
    far = send(started, sizes, lambda b, r, t: (1 - b, r, t))
    corner = send(started, sizes, lambda b, r, t: (0, 1 - r, t) if b == 1 else None)
    (normed,) = kernel_call(
        norm_kernel, [(tile_shape, jnp.bfloat16)], (spot, own, far, modulation[1]),
        near=True,
    )
    (bias,) = kernel_call(
        functools.partial(bias_kernel, 2 * tile_rows, sizes[2] * tile_cols),
        [((2 * tile, 6 * tile), jnp.float32)], (spot,), copies=1,
    )
    side = swap_rows(jnp.where(is_control, normed, own))
    side, corner, bias, *first = lax.optimization_barrier((side, corner, bias, *first))
    first.append(swap_links(first[1], ORDER[2]))
    first, head_stack, shared = kernel_call(
        stack_kernel, [triple_shape, stack_shape, shared_shape], (spot, *first),
        copies=8, stay=True,
    )
    first_other = swap_cores(first)
    out_mine = send(head_stack, sizes, lambda b, r, t: (0, r, t) if b == 1 else None)
    zero_side = swap_rows(shared, base_only)

    def halos(keyval, joins):
        def across(b, r, t):
            target = t + 1 if t % 2 else t - 1
            return (b, r, target) if joins(b, r, t) and 0 <= target < sizes[2] else None

        return send(keyval, sizes, across), swap_cores(keyval, joins)

    def neighborhood(query, keyval, outer, inner):
        (attended,) = kernel_call(
            attend_kernel, [((2 * tile, images * half), jnp.bfloat16)],
            (spot, query, outer, keyval, inner, bias),
            micros=8, near=True,
        )
        return attended.reshape(2, tile, images * half)

    def their_heads(attended, joins):
        theirs = lax.dynamic_index_in_dim(attended, 1 - row, 0, keepdims=False)
        return swap_rows(theirs, joins)

    def head_rows(index, mine, other):
        (rows,) = kernel_call(
            functools.partial(head_rows_kernel, index), [rows_shape], (spot, mine, other),
            scratch=[half_stacks], copies=2,
        )
        return rows

    def finished(attended, side_heads, rows, more, mod):
        (out,) = kernel_call(
            final_kernel, [(tile_shape, jnp.bfloat16)],
            (spot, attended, side_heads, rows, own, more, mod),
            scratch=[(tile_shape, jnp.bfloat16)], copies=1, near=True, stay=True,
        )
        return out

    def control_attention():
        keyval, query = kernel_call(
            project_kernel, projections, (spot, normed, side, first, first_other),
            scratch=[((2 * half + lanes, D), jnp.bfloat16), both_shape], micros=5, near=True, room=24,
        )
        attended = neighborhood(query, keyval, *halos(keyval, control_only))
        return attended

    attended = lax.cond(is_control, control_attention, lambda: unset(head_shape)[0])
    near = send(attended, sizes, lambda b, r, t: (0, r, t) if b == 1 else None)
    cross = send(attended, sizes, lambda b, r, t: (0, 1 - r, t) if b == 1 else None)

    def control_finish():
        rows = head_rows(3, swap_cores(head_stack, control_only), head_stack)
        side_heads = their_heads(attended, control_only)
        return unset(shared_shape, stack_shape, stack_shape) + (rows, side_heads)

    def base_prepare():
        third = jnp.where(
            is_query, first_other[:, 2 * SLOT :], after(first, attended)[:, 2 * SLOT :]
        )
        zero_corner = swap_cores(zero_side, base_only)
        out_other = swap_cores(out_mine, base_only)
        return (zero_corner, out_other, third) + unset(rows_shape, half_head_shape)

    zero_corner, out_other, third, rows, side_heads = lax.cond(
        is_control, control_finish, base_prepare
    )

    def base_finish():
        other = swap_rows(third, base_only)
        residue, keyval, query = kernel_call(
            middle_kernel,
            [(tile_shape, jnp.bfloat16)] + projections,
            (
                spot, own, far, side, corner, near, cross, out_mine, out_other, first, first_other,
                zero_side, zero_corner, modulation[1], modulation[0],
            ),
            scratch=[
                rows_shape,
                ((D, D), jnp.bfloat16),
                ((2 * half + lanes, D), jnp.bfloat16),
                both_shape,
            ],
            micros=8, near=True, room=32,
        )
        outer, inner = halos(keyval, base_only)
        attended = neighborhood(query, keyval, outer, inner)
        side_heads = their_heads(attended, base_only)
        return attended, side_heads, head_rows(1, third, other), residue

    attended, side_heads, rows, more = lax.cond(
        is_control, lambda: (attended, side_heads, rows, far), base_finish
    )
    mod = jnp.where(is_control, modulation[1], modulation[0])
    out = finished(attended, side_heads, rows, more, mod)
    return out.reshape(latent.shape)


def solution(mesh):
    placed = (
        P("branch", None, "trow", "tcol", None),
        P(),
        P("branch", None, "tcol"),
        P("branch", None, "tcol"),
        P("branch", "tcol", None),
        P(None, "tcol"),
    )
    sizes = (mesh.shape["branch"], mesh.shape["trow"], mesh.shape["tcol"])
    body = on_device
    if sizes == (2, 2, HEADS):
        body = functools.partial(paired_rows, sizes)
    return jax.shard_map(
        body,
        mesh=mesh,
        in_specs=placed,
        out_specs=P("branch", None, "trow", "tcol", None),
        check_vma=False,
    )
```

```python
import functools
import math

import jax
import jax.numpy as jnp
from jax import lax
from jax.experimental import pallas as pl
from jax.experimental.pallas import tpu as pltpu
from jax.sharding import PartitionSpec as P

D = 1152
HD = 72
HEADS = 8
WIN = 13
HW = 576


def padded(block, sides, width):
    for axis, dim in sides:
        count = lax.axis_size(axis)
        forward = [(i, i + 1) for i in range(count - 1)]
        backward = [(target, source) for source, target in forward]
        low = lax.ppermute(
            lax.slice_in_dim(block, block.shape[dim] - width, None, axis=dim), axis, forward
        )
        high = lax.ppermute(lax.slice_in_dim(block, 0, width, axis=dim), axis, backward)
        block = jnp.concatenate([low, block, high], axis=dim)
    return block


def shifted(block, axis, distance):
    devices = range(lax.axis_size(axis))
    route = [(i - distance, i) for i in devices if i - distance in devices]
    return lax.ppermute(block, axis, route)


def modulate(hidden, shift_scale):
    average = jnp.mean(hidden, axis=-1, keepdims=True)
    centred = hidden - average
    variance = jnp.mean(centred * centred, axis=-1, keepdims=True)
    return (centred * lax.rsqrt(variance + 1e-06) * (1.0 + shift_scale[1]) + shift_scale[0]).astype(
        jnp.bfloat16
    )


def block_mask(row_first, col_first, total_rows, total_cols, key_count):
    query_edge = 8
    radius = WIN // 2
    key_side = query_edge + 2 * radius
    offsets = jnp.arange(query_edge)
    reaches = jnp.arange(key_side)
    row_starts = jnp.clip(row_first + offsets - radius, 0, total_rows - WIN)
    key_rows = row_first - radius + reaches
    row_inside = (key_rows[None, :] >= row_starts[:, None]) & (
        key_rows[None, :] < row_starts[:, None] + WIN
    )
    col_starts = jnp.clip(col_first + offsets - radius, 0, total_cols - WIN)
    key_cols = col_first - radius + reaches
    col_inside = (key_cols[None, :] >= col_starts[:, None]) & (
        key_cols[None, :] < col_starts[:, None] + WIN
    )
    joined = row_inside[:, None, :, None] & col_inside[None, :, None, :]
    joined = joined.reshape(query_edge * query_edge, key_side * key_side)
    filler = jnp.zeros((query_edge * query_edge, key_count - key_side * key_side), dtype=jnp.bool_)
    return jnp.concatenate([joined, filler], axis=1)


def edge_keys(key_values):
    radius = WIN // 2
    return padded(key_values, (("trow", 1), ("tcol", 2)), radius)


def attend_tile(queries, extended, row_anchor, col_anchor, total_rows, total_cols):
    images, tile_rows, tile_cols = (queries.shape[0], queries.shape[1], queries.shape[2])
    query_edge = 8
    radius = WIN // 2
    key_side = query_edge + 2 * radius
    key_count = (key_side * key_side + 127) // 128 * 128
    across = tile_cols // query_edge
    block_count = tile_rows // query_edge * across
    scaling = 1.0 / math.sqrt(HD)

    def one_block(position):
        row_block = position // across * query_edge
        col_block = position % across * query_edge
        query_block = queries
        query_block = query_block.reshape(images, query_edge * query_edge, HEADS, HD)
        key_block = extended
        key_block = key_block.reshape(images, key_side * key_side, 2 * HW)
        key_block = jnp.pad(key_block, ((0, 0), (0, key_count - key_side * key_side), (0, 0)))
        key_heads = key_block[..., :HW].reshape(images, key_count, HEADS, HD)
        value_heads = key_block[..., HW:].reshape(images, key_count, HEADS, HD)
        allowed = block_mask(
            row_anchor + row_block, col_anchor + col_block, total_rows, total_cols, key_count
        )
        scores = (
            jnp.einsum(
                "iqhd,ikhd->ihqk", query_block, key_heads, preferred_element_type=jnp.float32
            )
            * scaling
        )
        scores = jnp.where(allowed[None, None], scores, -1e30)
        highest = jnp.max(scores, axis=-1, keepdims=True)
        raised = jnp.exp(scores - highest)
        totals = jnp.sum(raised, axis=-1, keepdims=True)
        weights = (raised / totals).astype(jnp.bfloat16)
        blended = jnp.einsum(
            "ihqk,ikhd->iqhd", weights, value_heads, preferred_element_type=jnp.float32
        )
        return blended.astype(jnp.bfloat16).reshape(images, query_edge, query_edge, HW)

    result = lax.map(one_block, jnp.arange(block_count))
    result = result.reshape(tile_rows // query_edge, across, images, query_edge, query_edge, HW)
    return result.transpose(2, 0, 3, 1, 4, 5).reshape(images, tile_rows, tile_cols, HW)


def run_block(active, hidden, shift_scale, weight_q, weight_kv, weight_o):
    images, tile_rows, tile_cols = (hidden.shape[0], hidden.shape[1], hidden.shape[2])
    tokens = images * tile_rows * tile_cols

    def project():
        flattened = modulate(hidden, shift_scale).reshape(tokens, D)
        queries = jnp.dot(flattened, weight_q, preferred_element_type=jnp.float32).astype(
            jnp.bfloat16
        )
        key_values = jnp.dot(flattened, weight_kv, preferred_element_type=jnp.float32).astype(
            jnp.bfloat16
        )
        return (queries, key_values)

    def nothing():
        return (jnp.zeros((tokens, HW), jnp.bfloat16), jnp.zeros((tokens, 2 * HW), jnp.bfloat16))

    queries, key_values = lax.cond(active, project, nothing)
    extended = edge_keys(key_values.reshape(images, tile_rows, tile_cols, 2 * HW))
    row_anchor = lax.axis_index("trow") * tile_rows
    col_anchor = lax.axis_index("tcol") * tile_cols
    total_rows = tile_rows * lax.axis_size("trow")
    total_cols = tile_cols * lax.axis_size("tcol")

    def finish():
        attended = attend_tile(
            queries.reshape(images, tile_rows, tile_cols, HW),
            extended,
            row_anchor,
            col_anchor,
            total_rows,
            total_cols,
        )
        projected = jnp.dot(
            attended.reshape(tokens, HW), weight_o, preferred_element_type=jnp.float32
        )
        return (hidden + shift_scale[2] * projected.reshape(hidden.shape)).astype(jnp.bfloat16)

    def vacant():
        return jnp.zeros(hidden.shape, jnp.bfloat16)

    return lax.cond(active, finish, vacant)


def zero_project(control_out, weight_z):
    flattened = control_out.reshape(-1, D)
    return (
        jnp.dot(flattened, weight_z, preferred_element_type=jnp.float32)
        .astype(jnp.bfloat16)
        .reshape(control_out.shape)
    )


def on_device(latent, modulation, w_query, w_keyval, w_out, w_zero):
    sources = (w_query, w_keyval, w_out)
    weight_q, weight_kv, weight_o, weight_z = (
        lax.all_gather(sources[0], "tcol", axis=2, tiled=True),
        lax.all_gather(sources[1], "tcol", axis=2, tiled=True),
        lax.all_gather(sources[2], "tcol", axis=1, tiled=True),
        lax.all_gather(w_zero, "tcol", axis=1, tiled=True),
    )
    branch_index = lax.axis_index("branch")
    is_control = branch_index == 1
    own_copy = latent[0]
    shift_scale = lax.dynamic_index_in_dim(modulation, branch_index, 0, keepdims=False)
    received = shifted(own_copy, "branch", 1)
    control_in = own_copy.astype(jnp.float32) + received.astype(jnp.float32)
    control_out = run_block(
        is_control, control_in, shift_scale, weight_q[0], weight_kv[0], weight_o[0]
    )

    def with_projection():
        return zero_project(control_out, weight_z)

    def without_projection():
        return jnp.zeros(control_out.shape, jnp.bfloat16)

    residual = lax.cond(is_control, with_projection, without_projection)
    returned = shifted(residual, "branch", -1)
    base_in = own_copy.astype(jnp.float32) + returned.astype(jnp.float32)
    base_out = run_block(
        jnp.logical_not(is_control), base_in, shift_scale, weight_q[0], weight_kv[0], weight_o[0]
    )
    return jnp.where(is_control, control_out, base_out)[None]


AXES = ("branch", "trow", "tcol")
SLOT = 80
SHARED = 64
ORDER = (0, 3, 1, 2)


def routes(sizes, move):
    found = []
    for b in range(sizes[0]):
        for r in range(sizes[1]):
            for t in range(sizes[2]):
                target = move(b, r, t)
                if target is not None:
                    found.append((place_of(sizes, b, r, t), place_of(sizes, *target)))
    return found


def place_of(sizes, b, r, t):
    return (b * sizes[1] + r) * sizes[2] + t


def send(block, sizes, move):
    return lax.ppermute(block, AXES, routes(sizes, move))


def after(block, *earlier):
    return lax.optimization_barrier((block,) + earlier)[0]


def kernel_call(body, outs, args, scratch=(), copies=0, stay=False, micros=0, near=False, room=16):
    def space(a):
        if a.dtype == jnp.int32:
            return pltpu.SMEM
        return pltpu.VMEM if near or a.dtype == jnp.float32 else pl.ANY

    buffers = [pltpu.VMEM(shape, kind) for shape, kind in scratch]
    return pl.pallas_call(
        body,
        out_shape=[jax.ShapeDtypeStruct(shape, kind) for shape, kind in outs],
        in_specs=[pl.BlockSpec(memory_space=space(a)) for a in args],
        out_specs=[pl.BlockSpec(memory_space=pl.ANY if stay else pltpu.VMEM) for _ in outs],
        scratch_shapes=buffers + ([pltpu.SemaphoreType.DMA((copies,))] if copies else []),
        compiler_params=pltpu.CompilerParams(vmem_limit_bytes=room * 1024 * 1024),
        cost_estimate=pl.CostEstimate(
            flops=0, bytes_accessed=1 + 3_700_000 * micros, transcendentals=0
        ),
    )(*args)


def begin(copies, done, first=0):
    started = []
    for n, (source, target) in enumerate(copies):
        copy = pltpu.make_async_copy(source, target, done.at[first + n])
        copy.start()
        started.append(copy)
    return started


def finish(started):
    for copy in started:
        copy.wait()


def dot_rows(left, right):
    return lax.dot_general(left, right, (((1,), (1,)), ((), ())), preferred_element_type=jnp.float32)


def rows_at(start, count):
    return pl.ds(pl.multiple_of(start, 16), count)


def stack_kernel(spot, one, two, three, four, stacked, heads, shared, done):
    pieces = (one, two, three, four)
    started = begin([(piece, stacked.at[n]) for n, piece in enumerate(pieces)], done)

    def part(first, target):
        rows = slice(first, first + target.shape[1])
        finish(begin([(piece.at[rows], target.at[n]) for n, piece in enumerate(pieces)], done, 4))

    is_control = spot[0] == 1
    is_query = spot[3] == spot[1]
    low = spot[1] == 0
    pl.when(is_control & is_query)(lambda: part(2 * SLOT, heads))
    pl.when(is_control & jnp.logical_not(is_query))(lambda: part(SLOT, heads))
    pl.when(jnp.logical_not(is_control) & low)(lambda: part(SLOT, shared))
    pl.when(jnp.logical_not(is_control | low))(lambda: part(2 * SLOT - SHARED, shared))
    finish(started)


def norm_kernel(spot, own, far, mod, normed):
    for image in range(own.shape[0]):
        hidden = own[image].astype(jnp.float32) + far[image].astype(jnp.float32)
        normed[image] = modulate(hidden, mod)


def bias_kernel(total_rows, total_cols, spot, bias, done):
    radius = WIN // 2
    query = lax.broadcasted_iota(jnp.int32, bias.shape, 0)
    key = lax.broadcasted_iota(jnp.int32, bias.shape, 1)
    base = spot[4]
    row_start = jnp.clip((query >> 3) - radius, 0, total_rows - WIN)
    col_start = jnp.clip(base + (query & 7) - radius, 0, total_cols - WIN)
    key_row = (key & 127) >> 3
    outward = 2 * spot[3] - 1
    key_col = base + (1 - (key >> 7)) * outward * 8 + (key & 7)
    inside = (
        (key_row >= row_start)
        & (key_row < row_start + WIN)
        & (key_col >= col_start)
        & (key_col < col_start + WIN)
    )
    bias[...] = jnp.where(inside, 0.0, -1e30)


def unset_kernel(*refs):
    pass


def in_order(origin):
    return (origin % 2) * 2 + origin // 2


def arrange_keyvals(link, core, mine, other, weight):
    for block, at in ((mine, core), (other, 1 - core)):
        for step in range(4):
            origin = link ^ ORDER[step]
            slot = (1 - origin // 2) * 4 + at * 2 + origin % 2
            weight[rows_at(slot * SLOT, SLOT), :] = block[step, :SLOT]


def arrange_heads(link, stack, first_row, weight):
    for step in range(4):
        start = first_row + in_order(link ^ ORDER[step]) * SLOT
        weight[rows_at(start, SLOT), :] = stack[step]


def clear_rows(weight, start, stop):
    weight[start:stop, :] = jnp.zeros((stop - start, weight.shape[1]), weight.dtype)


def arrange_queries(spot, mine, other, part, weight):
    start = weight.shape[0] - 4 * SLOT
    clear_rows(weight, 8 * SLOT, start)
    rows = slice(part * SLOT, (part + 1) * SLOT)
    own = spot[3] == spot[1]
    pl.when(own)(lambda: arrange_heads(spot[2], mine.at[:, rows], start, weight))
    pl.when(jnp.logical_not(own))(lambda: arrange_heads(spot[2], other.at[:, rows], start, weight))


def project_kernel(spot, normed, normed_other, mine, other, keyval, query, weight, both):
    row, link, core = (spot[1], spot[2], spot[3])
    arrange_keyvals(link, core, mine, other, weight)
    arrange_queries(spot, mine, other, 1, weight)
    both[:, row] = normed[...]
    both[:, 1 - row] = normed_other[...]
    tokens = both[...].reshape(-1, both.shape[3])
    projected = dot_rows(tokens, weight[...]).astype(keyval.dtype)
    keyval[...] = projected[:, : keyval.shape[1]]
    query[...] = projected[:, keyval.shape[1] :]


def attend_kernel(spot, queries, outer, here, inner, bias, out):
    scaling = math.log2(math.e) / math.sqrt(HD)
    tokens = bias.shape[0]
    images = queries.shape[0] // tokens
    parts = (outer, here, inner)
    key_lanes = queries.shape[1]
    first_key = here.shape[1] - key_lanes
    width = out.shape[1] // images
    heads = width // SLOT
    results = []
    pad = key_lanes - heads * SLOT
    value_lanes = (width + 127) // 128 * 128
    query_lane = lax.broadcasted_iota(jnp.int32, (tokens, key_lanes), 1) - pad
    value_lane = lax.broadcasted_iota(jnp.int32, (tokens, value_lanes), 1)

    def within(lane, head):
        return (lane >= head * SLOT) & (lane < (head + 1) * SLOT)

    for image in range(images):
        rows = slice(image * tokens, (image + 1) * tokens)
        keys = jnp.concatenate([part[rows, first_key:] for part in parts], axis=0)
        values = jnp.concatenate([part[rows, :value_lanes] for part in parts], axis=0)
        query = queries[rows, :].astype(jnp.float32)
        split = [jnp.where(within(query_lane, head), query, 0.0) for head in range(heads)]
        scores = dot_rows(jnp.concatenate(split, axis=0).astype(jnp.bfloat16), keys)
        raised, sums = ([], [])
        for head in range(heads):
            part = scores[head * tokens : (head + 1) * tokens] * scaling + bias[...]
            part = jnp.exp2(part - jnp.max(part, axis=-1, keepdims=True))
            sums.append(1.0 / jnp.sum(part, axis=-1, keepdims=True))
            raised.append(part.astype(jnp.bfloat16))
        blended = jnp.dot(
            jnp.concatenate(raised, axis=0), values, preferred_element_type=jnp.float32
        )
        total = jnp.zeros((tokens, value_lanes), jnp.float32)
        for head in range(heads):
            part = blended[head * tokens : (head + 1) * tokens] * sums[head]
            total = jnp.where(within(value_lane, head), part, total)
        results.append(total[:, :width])
    out[...] = jnp.concatenate(results, axis=1).astype(out.dtype)


def head_rows_kernel(index, spot, mine, other, out, outs, done):
    at = spot[index]
    copies = [(mine, outs.at[1 - at]), (other, outs.at[at])]
    finish(begin(copies, done))
    for part in range(2):
        arrange_heads(spot[2], outs.at[part], part * 4 * SLOT, out)


def middle_kernel(
    spot, own, far, side, corner, near, cross, out_mine, out_other, first, first_other,
    zero_side, zero_corner, mod, mod_base, residue, keyval, query,
    w_out, w_zero, weight, both,
):
    row, link, core = (spot[1], spot[2], spot[3])
    images, tokens, _ = own.shape
    tile = images * tokens
    width = near.shape[2] // images
    for block, at in ((out_mine, core), (out_other, 1 - core)):
        arrange_heads(link, block, at * width, w_out)
    shard = w_zero.shape[0] // 8
    kept = shard - SHARED
    for block, part, at in (
        (first, zero_side, core),
        (first_other, zero_corner, 1 - core),
    ):
        for step in range(4):
            start = (2 * (link ^ ORDER[step]) + at) * shard
            w_zero[rows_at(start + row * SHARED, kept), :] = block[step, SLOT : 2 * SLOT]
            w_zero[rows_at(start + (1 - row) * kept, SHARED), :] = part[step]
    arrange_keyvals(link, core, first, first_other, weight)
    arrange_queries(spot, first, first_other, 2, weight)

    def ordered(ref):
        parts = [
            ref[s][:, i * width : (i + 1) * width] for s in (row, 1 - row) for i in range(images)
        ]
        return jnp.concatenate(parts, axis=0)

    def stacked(one, two):
        parts = [ref[i] for ref in (one, two) for i in range(images)]
        return jnp.concatenate(parts, axis=0).astype(jnp.float32)

    projected = jnp.dot(
        ordered(near), w_out[rows_at(row * width, width), :], preferred_element_type=jnp.float32
    )
    projected += jnp.dot(
        ordered(cross),
        w_out[rows_at((1 - row) * width, width), :],
        preferred_element_type=jnp.float32,
    )
    base = stacked(own, side)
    out = (base + stacked(far, corner) + mod[2] * projected).astype(jnp.bfloat16)
    residual = dot_rows(out, w_zero[...]).astype(jnp.bfloat16)
    base = base + residual.astype(jnp.float32)
    result = modulate(base, mod_base)
    for image in range(images):
        rows = slice(image * tokens, (image + 1) * tokens)
        residue[image] = residual[rows]
        both[image, row] = result[rows]
        both[image, 1 - row] = result[tile + image * tokens : tile + (image + 1) * tokens]
    rows = both[...].reshape(2 * tile, both.shape[3])
    projected = dot_rows(rows, weight[...]).astype(keyval.dtype)
    keyval[...] = projected[:, : keyval.shape[1]]
    query[...] = projected[:, keyval.shape[1] :]


def final_kernel(spot, attended, side, head_rows, own, more, mod, out, result, done):
    row = spot[1]
    images = out.shape[0]
    width = side.shape[1] // images

    def flat(block):
        parts = [block[:, i * width : (i + 1) * width] for i in range(images)]
        return jnp.concatenate(parts, axis=0)

    near, far = (flat(attended[row]), flat(side[...]))
    projected = jnp.dot(
        near, head_rows[rows_at(row * width, width), :], preferred_element_type=jnp.float32
    )
    projected += jnp.dot(
        far, head_rows[rows_at((1 - row) * width, width), :], preferred_element_type=jnp.float32
    )
    tokens = out.shape[1]
    for image in range(images):
        rows = slice(image * tokens, (image + 1) * tokens)
        base = own[image].astype(jnp.float32) + more[image].astype(jnp.float32)
        result[image] = (base + mod[2] * projected[rows]).astype(out.dtype)
    finish(begin([(result, out)], done))


def paired_rows(sizes, latent, modulation, w_query, w_keyval, w_out, w_zero):
    branch = lax.axis_index("branch")
    row = lax.axis_index("trow")
    column = lax.axis_index("tcol")
    core = column % 2
    is_control = branch == 1
    is_query = core == row
    _, images, tile_rows, tile_cols, _ = latent.shape
    tile = tile_rows * tile_cols
    tokens = images * 2 * tile
    half = HEADS // 2 * SLOT
    lanes = half + half % 128
    spot = jnp.stack([branch, row, column // 2, core, column * tile_cols]).astype(jnp.int32)
    own = latent.reshape(images, tile, D)

    def everyone(b, r, t):
        return True

    def base_only(b, r, t):
        return b == 0

    def control_only(b, r, t):
        return b == 1

    def swap_cores(block, joins=everyone):
        return send(block, sizes, lambda b, r, t: (b, r, t ^ 1) if joins(b, r, t) else None)

    def swap_rows(block, joins=everyone):
        return send(block, sizes, lambda b, r, t: (b, 1 - r, t) if joins(b, r, t) else None)

    def swap_links(block, distance, joins=everyone):
        return send(
            block, sizes, lambda b, r, t: (b, r, t ^ (2 * distance)) if joins(b, r, t) else None
        )

    def padded_rows(block):
        return jnp.pad(block, ((0, SLOT - HD), (0, 0)))

    def joined(block, other):
        return jnp.concatenate([block, other], axis=0)

    def unset(*outs):
        return tuple(kernel_call(unset_kernel, list(outs), (spot,), copies=1, stay=True))

    tile_shape = (images, tile, D)
    head_shape = ((2, tile, images * half), jnp.bfloat16)
    half_head_shape = ((tile, images * half), jnp.bfloat16)
    stack_shape = ((4, SLOT, D), jnp.bfloat16)
    shared_shape = ((4, SHARED, D), jnp.bfloat16)
    rows_shape = ((2 * half, D), jnp.bfloat16)
    projections = [((tokens, 2 * half), jnp.bfloat16), ((tokens, lanes), jnp.bfloat16)]
    shard = w_zero.shape[1]
    triple_shape = ((4, 3 * SLOT, D), jnp.bfloat16)
    half_stacks = ((2, 4, SLOT, D), jnp.bfloat16)
    both_shape = ((images, 2, tile, D), jnp.bfloat16)

    keyval_piece = padded_rows(lax.dynamic_slice_in_dim(w_keyval[0].T, row * HD, HD, axis=0))
    zero_piece = lax.dynamic_slice_in_dim(w_zero.T, row * SHARED, shard - SHARED, axis=0)
    query_or_out = padded_rows(jnp.where(is_query, w_query[0].T, w_out[0]))

    out_piece = padded_rows(w_out[0])
    piece = jnp.concatenate(
        [
            keyval_piece,
            jnp.where(is_control, query_or_out, zero_piece),
            jnp.where(is_control, out_piece, query_or_out),
        ],
        axis=0,
    )
    first = [piece, swap_links(piece, ORDER[1]), swap_links(piece, ORDER[2])]
    (bias,) = kernel_call(
        functools.partial(bias_kernel, 2 * tile_rows, sizes[2] * tile_cols),
        [((2 * tile, 6 * tile), jnp.float32)], (spot,), copies=1,
    )
    started = after(own, piece, bias)
    far = send(started, sizes, lambda b, r, t: (1 - b, r, t))
    corner = send(started, sizes, lambda b, r, t: (0, 1 - r, t) if b == 1 else None)
    (normed,) = kernel_call(
        norm_kernel, [(tile_shape, jnp.bfloat16)], (spot, own, far, modulation[1]),
        near=True,
    )
    side = swap_rows(jnp.where(is_control, normed, own))
    first.append(swap_links(first[1], ORDER[2]))
    side, corner, bias, *first = lax.optimization_barrier((side, corner, bias, *first))
    first, head_stack, shared = kernel_call(
        stack_kernel, [triple_shape, stack_shape, shared_shape], (spot, *first),
        copies=8, stay=True,
    )
    first_other = swap_cores(first)
    out_mine = send(head_stack, sizes, lambda b, r, t: (0, r, t) if b == 1 else None)
    zero_side = swap_rows(shared, base_only)

    def halos(keyval, joins):
        def across(b, r, t):
            target = t + 1 if t % 2 else t - 1
            return (b, r, target) if joins(b, r, t) and 0 <= target < sizes[2] else None

        return send(keyval, sizes, across), swap_cores(keyval, joins)

    def neighborhood(query, keyval, outer, inner):
        (attended,) = kernel_call(
            attend_kernel, [((2 * tile, images * half), jnp.bfloat16)],
            (spot, query, outer, keyval, inner, bias),
            micros=8, near=True,
        )
        return attended.reshape(2, tile, images * half)

    def their_heads(attended, joins):
        theirs = lax.dynamic_index_in_dim(attended, 1 - row, 0, keepdims=False)
        return swap_rows(theirs, joins)

    def head_rows(index, mine, other):
        (rows,) = kernel_call(
            functools.partial(head_rows_kernel, index), [rows_shape], (spot, mine, other),
            scratch=[half_stacks], copies=2,
        )
        return rows

    def finished(attended, side_heads, rows, more, mod):
        (out,) = kernel_call(
            final_kernel, [(tile_shape, jnp.bfloat16)],
            (spot, attended, side_heads, rows, own, more, mod),
            scratch=[(tile_shape, jnp.bfloat16)], copies=1, near=True, stay=True,
        )
        return out

    def control_attention():
        keyval, query = kernel_call(
            project_kernel, projections, (spot, normed, side, first, first_other),
            scratch=[((2 * half + lanes, D), jnp.bfloat16), both_shape], micros=5, near=True, room=24,
        )
        attended = neighborhood(query, keyval, *halos(keyval, control_only))
        return (attended,) + unset(stack_shape)

    def base_third():
        third = jnp.where(is_query, first_other[:, 2 * SLOT :], first[:, 2 * SLOT :])
        return unset(head_shape) + (third,)

    attended, third = lax.cond(is_control, control_attention, base_third)
    near = send(attended, sizes, lambda b, r, t: (0, r, t) if b == 1 else None)
    cross = send(attended, sizes, lambda b, r, t: (0, 1 - r, t) if b == 1 else None)

    def control_finish():
        rows = head_rows(3, swap_cores(head_stack, control_only), head_stack)
        side_heads = their_heads(attended, control_only)
        return unset(shared_shape, stack_shape) + (rows, side_heads)

    def base_prepare():
        zero_corner = swap_cores(zero_side, base_only)
        out_other = swap_cores(out_mine, base_only)
        return (zero_corner, out_other) + unset(rows_shape, half_head_shape)

    zero_corner, out_other, rows, side_heads = lax.cond(
        is_control, control_finish, base_prepare
    )

    def base_finish():
        other = swap_rows(third, base_only)
        residue, keyval, query = kernel_call(
            middle_kernel,
            [(tile_shape, jnp.bfloat16)] + projections,
            (
                spot, own, far, side, corner, near, cross, out_mine, out_other, first, first_other,
                zero_side, zero_corner, modulation[1], modulation[0],
            ),
            scratch=[
                rows_shape,
                ((D, D), jnp.bfloat16),
                ((2 * half + lanes, D), jnp.bfloat16),
                both_shape,
            ],
            micros=8, near=True, room=32,
        )
        outer, inner = halos(keyval, base_only)
        attended = neighborhood(query, keyval, outer, inner)
        side_heads = their_heads(attended, base_only)
        return attended, side_heads, head_rows(1, third, other), residue

    attended, side_heads, rows, more = lax.cond(
        is_control, lambda: (attended, side_heads, rows, far), base_finish
    )
    mod = jnp.where(is_control, modulation[1], modulation[0])
    out = finished(attended, side_heads, rows, more, mod)
    return out.reshape(latent.shape)


def solution(mesh):
    placed = (
        P("branch", None, "trow", "tcol", None),
        P(),
        P("branch", None, "tcol"),
        P("branch", None, "tcol"),
        P("branch", "tcol", None),
        P(None, "tcol"),
    )
    sizes = (mesh.shape["branch"], mesh.shape["trow"], mesh.shape["tcol"])
    body = on_device
    if sizes == (2, 2, HEADS):
        body = functools.partial(paired_rows, sizes)
    return jax.shard_map(
        body,
        mesh=mesh,
        in_specs=placed,
        out_specs=P("branch", None, "trow", "tcol", None),
        check_vma=False,
    )
```

```python
import functools
import math

import jax
import jax.numpy as jnp
from jax import lax
from jax.experimental import pallas as pl
from jax.experimental.pallas import tpu as pltpu
from jax.sharding import PartitionSpec as P

D = 1152
HD = 72
HEADS = 8
WIN = 13
HW = 576


def padded(block, sides, width):
    for axis, dim in sides:
        count = lax.axis_size(axis)
        forward = [(i, i + 1) for i in range(count - 1)]
        backward = [(target, source) for source, target in forward]
        low = lax.ppermute(
            lax.slice_in_dim(block, block.shape[dim] - width, None, axis=dim), axis, forward
        )
        high = lax.ppermute(lax.slice_in_dim(block, 0, width, axis=dim), axis, backward)
        block = jnp.concatenate([low, block, high], axis=dim)
    return block


def shifted(block, axis, distance):
    devices = range(lax.axis_size(axis))
    route = [(i - distance, i) for i in devices if i - distance in devices]
    return lax.ppermute(block, axis, route)


def modulate(hidden, shift_scale):
    average = jnp.mean(hidden, axis=-1, keepdims=True)
    centred = hidden - average
    variance = jnp.mean(centred * centred, axis=-1, keepdims=True)
    return (centred * lax.rsqrt(variance + 1e-06) * (1.0 + shift_scale[1]) + shift_scale[0]).astype(
        jnp.bfloat16
    )


def block_mask(row_first, col_first, total_rows, total_cols, key_count):
    query_edge = 8
    radius = WIN // 2
    key_side = query_edge + 2 * radius
    offsets = jnp.arange(query_edge)
    reaches = jnp.arange(key_side)
    row_starts = jnp.clip(row_first + offsets - radius, 0, total_rows - WIN)
    key_rows = row_first - radius + reaches
    row_inside = (key_rows[None, :] >= row_starts[:, None]) & (
        key_rows[None, :] < row_starts[:, None] + WIN
    )
    col_starts = jnp.clip(col_first + offsets - radius, 0, total_cols - WIN)
    key_cols = col_first - radius + reaches
    col_inside = (key_cols[None, :] >= col_starts[:, None]) & (
        key_cols[None, :] < col_starts[:, None] + WIN
    )
    joined = row_inside[:, None, :, None] & col_inside[None, :, None, :]
    joined = joined.reshape(query_edge * query_edge, key_side * key_side)
    filler = jnp.zeros((query_edge * query_edge, key_count - key_side * key_side), dtype=jnp.bool_)
    return jnp.concatenate([joined, filler], axis=1)


def edge_keys(key_values):
    radius = WIN // 2
    return padded(key_values, (("trow", 1), ("tcol", 2)), radius)


def attend_tile(queries, extended, row_anchor, col_anchor, total_rows, total_cols):
    images, tile_rows, tile_cols = (queries.shape[0], queries.shape[1], queries.shape[2])
    query_edge = 8
    radius = WIN // 2
    key_side = query_edge + 2 * radius
    key_count = (key_side * key_side + 127) // 128 * 128
    across = tile_cols // query_edge
    block_count = tile_rows // query_edge * across
    scaling = 1.0 / math.sqrt(HD)

    def one_block(position):
        row_block = position // across * query_edge
        col_block = position % across * query_edge
        query_block = queries
        query_block = query_block.reshape(images, query_edge * query_edge, HEADS, HD)
        key_block = extended
        key_block = key_block.reshape(images, key_side * key_side, 2 * HW)
        key_block = jnp.pad(key_block, ((0, 0), (0, key_count - key_side * key_side), (0, 0)))
        key_heads = key_block[..., :HW].reshape(images, key_count, HEADS, HD)
        value_heads = key_block[..., HW:].reshape(images, key_count, HEADS, HD)
        allowed = block_mask(
            row_anchor + row_block, col_anchor + col_block, total_rows, total_cols, key_count
        )
        scores = (
            jnp.einsum(
                "iqhd,ikhd->ihqk", query_block, key_heads, preferred_element_type=jnp.float32
            )
            * scaling
        )
        scores = jnp.where(allowed[None, None], scores, -1e30)
        highest = jnp.max(scores, axis=-1, keepdims=True)
        raised = jnp.exp(scores - highest)
        totals = jnp.sum(raised, axis=-1, keepdims=True)
        weights = (raised / totals).astype(jnp.bfloat16)
        blended = jnp.einsum(
            "ihqk,ikhd->iqhd", weights, value_heads, preferred_element_type=jnp.float32
        )
        return blended.astype(jnp.bfloat16).reshape(images, query_edge, query_edge, HW)

    result = lax.map(one_block, jnp.arange(block_count))
    result = result.reshape(tile_rows // query_edge, across, images, query_edge, query_edge, HW)
    return result.transpose(2, 0, 3, 1, 4, 5).reshape(images, tile_rows, tile_cols, HW)


def run_block(active, hidden, shift_scale, weight_q, weight_kv, weight_o):
    images, tile_rows, tile_cols = (hidden.shape[0], hidden.shape[1], hidden.shape[2])
    tokens = images * tile_rows * tile_cols

    def project():
        flattened = modulate(hidden, shift_scale).reshape(tokens, D)
        queries = jnp.dot(flattened, weight_q, preferred_element_type=jnp.float32).astype(
            jnp.bfloat16
        )
        key_values = jnp.dot(flattened, weight_kv, preferred_element_type=jnp.float32).astype(
            jnp.bfloat16
        )
        return (queries, key_values)

    def nothing():
        return (jnp.zeros((tokens, HW), jnp.bfloat16), jnp.zeros((tokens, 2 * HW), jnp.bfloat16))

    queries, key_values = lax.cond(active, project, nothing)
    extended = edge_keys(key_values.reshape(images, tile_rows, tile_cols, 2 * HW))
    row_anchor = lax.axis_index("trow") * tile_rows
    col_anchor = lax.axis_index("tcol") * tile_cols
    total_rows = tile_rows * lax.axis_size("trow")
    total_cols = tile_cols * lax.axis_size("tcol")

    def finish():
        attended = attend_tile(
            queries.reshape(images, tile_rows, tile_cols, HW),
            extended,
            row_anchor,
            col_anchor,
            total_rows,
            total_cols,
        )
        projected = jnp.dot(
            attended.reshape(tokens, HW), weight_o, preferred_element_type=jnp.float32
        )
        return (hidden + shift_scale[2] * projected.reshape(hidden.shape)).astype(jnp.bfloat16)

    def vacant():
        return jnp.zeros(hidden.shape, jnp.bfloat16)

    return lax.cond(active, finish, vacant)


def zero_project(control_out, weight_z):
    flattened = control_out.reshape(-1, D)
    return (
        jnp.dot(flattened, weight_z, preferred_element_type=jnp.float32)
        .astype(jnp.bfloat16)
        .reshape(control_out.shape)
    )


def on_device(latent, modulation, w_query, w_keyval, w_out, w_zero):
    sources = (w_query, w_keyval, w_out)
    weight_q, weight_kv, weight_o, weight_z = (
        lax.all_gather(sources[0], "tcol", axis=2, tiled=True),
        lax.all_gather(sources[1], "tcol", axis=2, tiled=True),
        lax.all_gather(sources[2], "tcol", axis=1, tiled=True),
        lax.all_gather(w_zero, "tcol", axis=1, tiled=True),
    )
    branch_index = lax.axis_index("branch")
    is_control = branch_index == 1
    own_copy = latent[0]
    shift_scale = lax.dynamic_index_in_dim(modulation, branch_index, 0, keepdims=False)
    received = shifted(own_copy, "branch", 1)
    control_in = own_copy.astype(jnp.float32) + received.astype(jnp.float32)
    control_out = run_block(
        is_control, control_in, shift_scale, weight_q[0], weight_kv[0], weight_o[0]
    )

    def with_projection():
        return zero_project(control_out, weight_z)

    def without_projection():
        return jnp.zeros(control_out.shape, jnp.bfloat16)

    residual = lax.cond(is_control, with_projection, without_projection)
    returned = shifted(residual, "branch", -1)
    base_in = own_copy.astype(jnp.float32) + returned.astype(jnp.float32)
    base_out = run_block(
        jnp.logical_not(is_control), base_in, shift_scale, weight_q[0], weight_kv[0], weight_o[0]
    )
    return jnp.where(is_control, control_out, base_out)[None]


AXES = ("branch", "trow", "tcol")
SLOT = 80
SHARED = 64
ORDER = (0, 3, 1, 2)


def routes(sizes, move):
    found = []
    for b in range(sizes[0]):
        for r in range(sizes[1]):
            for t in range(sizes[2]):
                target = move(b, r, t)
                if target is not None:
                    found.append((place_of(sizes, b, r, t), place_of(sizes, *target)))
    return found


def place_of(sizes, b, r, t):
    return (b * sizes[1] + r) * sizes[2] + t


def send(block, sizes, move):
    return lax.ppermute(block, AXES, routes(sizes, move))


def after(block, *earlier):
    return lax.optimization_barrier((block,) + earlier)[0]


def kernel_call(body, outs, args, scratch=(), copies=0, stay=False, micros=0, near=False, room=16, keep=()):
    def space(a):
        if a.dtype == jnp.int32:
            return pltpu.SMEM
        return pltpu.VMEM if near or a.dtype == jnp.float32 else pl.ANY

    buffers = [pltpu.VMEM(shape, kind) for shape, kind in scratch]
    return pl.pallas_call(
        body,
        out_shape=[jax.ShapeDtypeStruct(shape, kind) for shape, kind in outs],
        in_specs=[pl.BlockSpec(memory_space=space(a)) for a in args],
        out_specs=[pl.BlockSpec(memory_space=pl.ANY if stay else pltpu.VMEM) for _ in outs],
        input_output_aliases=dict(keep),
        scratch_shapes=buffers + ([pltpu.SemaphoreType.DMA((copies,))] if copies else []),
        compiler_params=pltpu.CompilerParams(vmem_limit_bytes=room * 1024 * 1024),
        cost_estimate=pl.CostEstimate(
            flops=0, bytes_accessed=1 + 3_700_000 * micros, transcendentals=0
        ),
    )(*args)


def begin(copies, done, first=0):
    started = []
    for n, (source, target) in enumerate(copies):
        copy = pltpu.make_async_copy(source, target, done.at[first + n])
        copy.start()
        started.append(copy)
    return started


def finish(started):
    for copy in started:
        copy.wait()


def dot_rows(left, right):
    return lax.dot_general(left, right, (((1,), (1,)), ((), ())), preferred_element_type=jnp.float32)


def rows_at(start, count):
    return pl.ds(pl.multiple_of(start, 16), count)


def stack_kernel(first_index, count, spot, *refs):
    pieces = list(enumerate(refs[:count], first_index))
    stacked, heads, shared, done = refs[-4:]
    started = begin([(piece, stacked.at[n]) for n, piece in pieces], done)

    def part(first, target):
        rows = slice(first, first + target.shape[1])
        finish(begin([(piece.at[rows], target.at[n]) for n, piece in pieces], done, count))

    is_control = spot[0] == 1
    is_query = spot[3] == spot[1]
    low = spot[1] == 0
    pl.when(is_control & is_query)(lambda: part(2 * SLOT, heads))
    pl.when(is_control & jnp.logical_not(is_query))(lambda: part(SLOT, heads))
    pl.when(jnp.logical_not(is_control) & low)(lambda: part(SLOT, shared))
    pl.when(jnp.logical_not(is_control | low))(lambda: part(2 * SLOT - SHARED, shared))
    finish(started)


def norm_kernel(spot, own, far, mod, normed):
    for image in range(own.shape[0]):
        hidden = own[image].astype(jnp.float32) + far[image].astype(jnp.float32)
        normed[image] = modulate(hidden, mod)


def bias_kernel(total_rows, total_cols, spot, bias, done):
    radius = WIN // 2
    query = lax.broadcasted_iota(jnp.int32, bias.shape, 0)
    key = lax.broadcasted_iota(jnp.int32, bias.shape, 1)
    base = spot[4]
    row_start = jnp.clip((query >> 3) - radius, 0, total_rows - WIN)
    col_start = jnp.clip(base + (query & 7) - radius, 0, total_cols - WIN)
    key_row = (key & 127) >> 3
    outward = 2 * spot[3] - 1
    key_col = base + (1 - (key >> 7)) * outward * 8 + (key & 7)
    inside = (
        (key_row >= row_start)
        & (key_row < row_start + WIN)
        & (key_col >= col_start)
        & (key_col < col_start + WIN)
    )
    bias[...] = jnp.where(inside, 0.0, -1e30)


def unset_kernel(*refs):
    pass


def in_order(origin):
    return (origin % 2) * 2 + origin // 2


def arrange_keyvals(link, core, mine, other, weight):
    for block, at in ((mine, core), (other, 1 - core)):
        for step in range(4):
            origin = link ^ ORDER[step]
            slot = (1 - origin // 2) * 4 + at * 2 + origin % 2
            weight[rows_at(slot * SLOT, SLOT), :] = block[step, :SLOT]


def arrange_heads(link, stack, first_row, weight):
    for step in range(4):
        start = first_row + in_order(link ^ ORDER[step]) * SLOT
        weight[rows_at(start, SLOT), :] = stack[step]


def clear_rows(weight, start, stop):
    weight[start:stop, :] = jnp.zeros((stop - start, weight.shape[1]), weight.dtype)


def arrange_queries(spot, mine, other, part, weight):
    start = weight.shape[0] - 4 * SLOT
    clear_rows(weight, 8 * SLOT, start)
    rows = slice(part * SLOT, (part + 1) * SLOT)
    own = spot[3] == spot[1]
    pl.when(own)(lambda: arrange_heads(spot[2], mine.at[:, rows], start, weight))
    pl.when(jnp.logical_not(own))(lambda: arrange_heads(spot[2], other.at[:, rows], start, weight))


def project_kernel(spot, normed, normed_other, mine, other, keyval, query, weight, both):
    row, link, core = (spot[1], spot[2], spot[3])
    arrange_keyvals(link, core, mine, other, weight)
    arrange_queries(spot, mine, other, 1, weight)
    both[:, row] = normed[...]
    both[:, 1 - row] = normed_other[...]
    tokens = both[...].reshape(-1, both.shape[3])
    projected = dot_rows(tokens, weight[...]).astype(keyval.dtype)
    keyval[...] = projected[:, : keyval.shape[1]]
    query[...] = projected[:, keyval.shape[1] :]


def attend_kernel(spot, queries, outer, here, inner, bias, out):
    scaling = math.log2(math.e) / math.sqrt(HD)
    tokens = bias.shape[0]
    images = queries.shape[0] // tokens
    parts = (outer, here, inner)
    key_lanes = queries.shape[1]
    first_key = here.shape[1] - key_lanes
    width = out.shape[1] // images
    heads = width // SLOT
    results = []
    pad = key_lanes - heads * SLOT
    value_lanes = (width + 127) // 128 * 128
    query_lane = lax.broadcasted_iota(jnp.int32, (tokens, key_lanes), 1) - pad
    value_lane = lax.broadcasted_iota(jnp.int32, (tokens, value_lanes), 1)

    def within(lane, head):
        return (lane >= head * SLOT) & (lane < (head + 1) * SLOT)

    for image in range(images):
        rows = slice(image * tokens, (image + 1) * tokens)
        keys = jnp.concatenate([part[rows, first_key:] for part in parts], axis=0)
        values = jnp.concatenate([part[rows, :value_lanes] for part in parts], axis=0)
        query = queries[rows, :].astype(jnp.float32)
        split = [jnp.where(within(query_lane, head), query, 0.0) for head in range(heads)]
        scores = dot_rows(jnp.concatenate(split, axis=0).astype(jnp.bfloat16), keys)
        raised, sums = ([], [])
        for head in range(heads):
            part = scores[head * tokens : (head + 1) * tokens] * scaling + bias[...]
            part = jnp.exp2(part - jnp.max(part, axis=-1, keepdims=True))
            sums.append(1.0 / jnp.sum(part, axis=-1, keepdims=True))
            raised.append(part.astype(jnp.bfloat16))
        blended = jnp.dot(
            jnp.concatenate(raised, axis=0), values, preferred_element_type=jnp.float32
        )
        total = jnp.zeros((tokens, value_lanes), jnp.float32)
        for head in range(heads):
            part = blended[head * tokens : (head + 1) * tokens] * sums[head]
            total = jnp.where(within(value_lane, head), part, total)
        results.append(total[:, :width])
    out[...] = jnp.concatenate(results, axis=1).astype(out.dtype)


def head_rows_kernel(index, spot, mine, other, out, outs, done):
    at = spot[index]
    copies = [(mine, outs.at[1 - at]), (other, outs.at[at])]
    finish(begin(copies, done))
    for part in range(2):
        arrange_heads(spot[2], outs.at[part], part * 4 * SLOT, out)


def middle_kernel(
    spot, own, far, side, corner, near, cross, out_mine, out_other, first, first_other,
    zero_side, zero_corner, mod, mod_base, residue, keyval, query,
    w_out, w_zero, weight, both,
):
    row, link, core = (spot[1], spot[2], spot[3])
    images, tokens, _ = own.shape
    tile = images * tokens
    width = near.shape[2] // images
    for block, at in ((out_mine, core), (out_other, 1 - core)):
        arrange_heads(link, block, at * width, w_out)
    shard = w_zero.shape[0] // 8
    kept = shard - SHARED
    for block, part, at in (
        (first, zero_side, core),
        (first_other, zero_corner, 1 - core),
    ):
        for step in range(4):
            start = (2 * (link ^ ORDER[step]) + at) * shard
            w_zero[rows_at(start + row * SHARED, kept), :] = block[step, SLOT : 2 * SLOT]
            w_zero[rows_at(start + (1 - row) * kept, SHARED), :] = part[step]
    arrange_keyvals(link, core, first, first_other, weight)
    arrange_queries(spot, first, first_other, 2, weight)

    def ordered(ref):
        parts = [
            ref[s][:, i * width : (i + 1) * width] for s in (row, 1 - row) for i in range(images)
        ]
        return jnp.concatenate(parts, axis=0)

    def stacked(one, two):
        parts = [ref[i] for ref in (one, two) for i in range(images)]
        return jnp.concatenate(parts, axis=0).astype(jnp.float32)

    projected = jnp.dot(
        ordered(near), w_out[rows_at(row * width, width), :], preferred_element_type=jnp.float32
    )
    projected += jnp.dot(
        ordered(cross),
        w_out[rows_at((1 - row) * width, width), :],
        preferred_element_type=jnp.float32,
    )
    base = stacked(own, side)
    out = (base + stacked(far, corner) + mod[2] * projected).astype(jnp.bfloat16)
    residual = dot_rows(out, w_zero[...]).astype(jnp.bfloat16)
    base = base + residual.astype(jnp.float32)
    result = modulate(base, mod_base)
    for image in range(images):
        rows = slice(image * tokens, (image + 1) * tokens)
        residue[image] = residual[rows]
        both[image, row] = result[rows]
        both[image, 1 - row] = result[tile + image * tokens : tile + (image + 1) * tokens]
    rows = both[...].reshape(2 * tile, both.shape[3])
    projected = dot_rows(rows, weight[...]).astype(keyval.dtype)
    keyval[...] = projected[:, : keyval.shape[1]]
    query[...] = projected[:, keyval.shape[1] :]


def final_kernel(spot, attended, side, head_rows, own, more, mod, out, result, done):
    row = spot[1]
    images = out.shape[0]
    width = side.shape[1] // images

    def flat(block):
        parts = [block[:, i * width : (i + 1) * width] for i in range(images)]
        return jnp.concatenate(parts, axis=0)

    near, far = (flat(attended[row]), flat(side[...]))
    projected = jnp.dot(
        near, head_rows[rows_at(row * width, width), :], preferred_element_type=jnp.float32
    )
    projected += jnp.dot(
        far, head_rows[rows_at((1 - row) * width, width), :], preferred_element_type=jnp.float32
    )
    tokens = out.shape[1]
    for image in range(images):
        rows = slice(image * tokens, (image + 1) * tokens)
        base = own[image].astype(jnp.float32) + more[image].astype(jnp.float32)
        result[image] = (base + mod[2] * projected[rows]).astype(out.dtype)
    finish(begin([(result, out)], done))


def paired_rows(sizes, latent, modulation, w_query, w_keyval, w_out, w_zero):
    branch = lax.axis_index("branch")
    row = lax.axis_index("trow")
    column = lax.axis_index("tcol")
    core = column % 2
    is_control = branch == 1
    is_query = core == row
    _, images, tile_rows, tile_cols, _ = latent.shape
    tile = tile_rows * tile_cols
    tokens = images * 2 * tile
    half = HEADS // 2 * SLOT
    lanes = half + half % 128
    spot = jnp.stack([branch, row, column // 2, core, column * tile_cols]).astype(jnp.int32)
    own = latent.reshape(images, tile, D)

    def everyone(b, r, t):
        return True

    def base_only(b, r, t):
        return b == 0

    def control_only(b, r, t):
        return b == 1

    def swap_cores(block, joins=everyone):
        return send(block, sizes, lambda b, r, t: (b, r, t ^ 1) if joins(b, r, t) else None)

    def swap_rows(block, joins=everyone):
        return send(block, sizes, lambda b, r, t: (b, 1 - r, t) if joins(b, r, t) else None)

    def swap_links(block, distance, joins=everyone):
        return send(
            block, sizes, lambda b, r, t: (b, r, t ^ (2 * distance)) if joins(b, r, t) else None
        )

    def padded_rows(block):
        return jnp.pad(block, ((0, SLOT - HD), (0, 0)))

    def joined(block, other):
        return jnp.concatenate([block, other], axis=0)

    def unset(*outs):
        return tuple(kernel_call(unset_kernel, list(outs), (spot,), copies=1, stay=True))

    tile_shape = (images, tile, D)
    head_shape = ((2, tile, images * half), jnp.bfloat16)
    half_head_shape = ((tile, images * half), jnp.bfloat16)
    stack_shape = ((4, SLOT, D), jnp.bfloat16)
    shared_shape = ((4, SHARED, D), jnp.bfloat16)
    rows_shape = ((2 * half, D), jnp.bfloat16)
    projections = [((tokens, 2 * half), jnp.bfloat16), ((tokens, lanes), jnp.bfloat16)]
    shard = w_zero.shape[1]
    triple_shape = ((4, 3 * SLOT, D), jnp.bfloat16)
    half_stacks = ((2, 4, SLOT, D), jnp.bfloat16)
    both_shape = ((images, 2, tile, D), jnp.bfloat16)

    keyval_piece = padded_rows(lax.dynamic_slice_in_dim(w_keyval[0].T, row * HD, HD, axis=0))
    zero_piece = lax.dynamic_slice_in_dim(w_zero.T, row * SHARED, shard - SHARED, axis=0)
    query_or_out = padded_rows(jnp.where(is_query, w_query[0].T, w_out[0]))

    out_piece = padded_rows(w_out[0])
    piece = jnp.concatenate(
        [
            keyval_piece,
            jnp.where(is_control, query_or_out, zero_piece),
            jnp.where(is_control, out_piece, query_or_out),
        ],
        axis=0,
    )
    first = [piece, swap_links(piece, ORDER[1]), swap_links(piece, ORDER[2])]
    (bias,) = kernel_call(
        functools.partial(bias_kernel, 2 * tile_rows, sizes[2] * tile_cols),
        [((2 * tile, 6 * tile), jnp.float32)], (spot,), copies=1,
    )
    started = after(own, piece, bias)
    far = send(started, sizes, lambda b, r, t: (1 - b, r, t))
    corner = send(started, sizes, lambda b, r, t: (0, 1 - r, t) if b == 1 else None)
    (normed,) = kernel_call(
        norm_kernel, [(tile_shape, jnp.bfloat16)], (spot, own, far, modulation[1]),
        near=True,
    )
    side = swap_rows(jnp.where(is_control, normed, own))
    last = swap_links(first[1], ORDER[2])
    parts = [triple_shape, stack_shape, shared_shape]
    begun = kernel_call(
        functools.partial(stack_kernel, 0, 3), parts, (spot, *first), copies=6, stay=True
    )
    side, corner, bias, last, *begun = lax.optimization_barrier((side, corner, bias, last, *begun))
    first, head_stack, shared = kernel_call(
        functools.partial(stack_kernel, 3, 1), parts, (spot, last, *begun),
        copies=2, stay=True, keep=((2, 0), (3, 1), (4, 2)),
    )
    first_other = swap_cores(first)
    out_mine = send(head_stack, sizes, lambda b, r, t: (0, r, t) if b == 1 else None)
    zero_side = swap_rows(shared, base_only)

    def halos(keyval, joins):
        def across(b, r, t):
            target = t + 1 if t % 2 else t - 1
            return (b, r, target) if joins(b, r, t) and 0 <= target < sizes[2] else None

        return send(keyval, sizes, across), swap_cores(keyval, joins)

    def neighborhood(query, keyval, outer, inner):
        (attended,) = kernel_call(
            attend_kernel, [((2 * tile, images * half), jnp.bfloat16)],
            (spot, query, outer, keyval, inner, bias),
            micros=8, near=True,
        )
        return attended.reshape(2, tile, images * half)

    def their_heads(attended, joins):
        theirs = lax.dynamic_index_in_dim(attended, 1 - row, 0, keepdims=False)
        return swap_rows(theirs, joins)

    def head_rows(index, mine, other):
        (rows,) = kernel_call(
            functools.partial(head_rows_kernel, index), [rows_shape], (spot, mine, other),
            scratch=[half_stacks], copies=2,
        )
        return rows

    def finished(attended, side_heads, rows, more, mod):
        (out,) = kernel_call(
            final_kernel, [(tile_shape, jnp.bfloat16)],
            (spot, attended, side_heads, rows, own, more, mod),
            scratch=[(tile_shape, jnp.bfloat16)], copies=1, near=True, stay=True,
        )
        return out

    def control_attention():
        keyval, query = kernel_call(
            project_kernel, projections, (spot, normed, side, first, first_other),
            scratch=[((2 * half + lanes, D), jnp.bfloat16), both_shape], micros=5, near=True, room=24,
        )
        attended = neighborhood(query, keyval, *halos(keyval, control_only))
        return (attended,) + unset(stack_shape)

    def base_third():
        third = jnp.where(is_query, first_other[:, 2 * SLOT :], first[:, 2 * SLOT :])
        return unset(head_shape) + (third,)

    attended, third = lax.cond(is_control, control_attention, base_third)
    near = send(attended, sizes, lambda b, r, t: (0, r, t) if b == 1 else None)
    cross = send(attended, sizes, lambda b, r, t: (0, 1 - r, t) if b == 1 else None)

    def control_finish():
        rows = head_rows(3, swap_cores(head_stack, control_only), head_stack)
        side_heads = their_heads(attended, control_only)
        return unset(shared_shape, stack_shape) + (rows, side_heads)

    def base_prepare():
        zero_corner = swap_cores(zero_side, base_only)
        out_other = swap_cores(out_mine, base_only)
        return (zero_corner, out_other) + unset(rows_shape, half_head_shape)

    zero_corner, out_other, rows, side_heads = lax.cond(
        is_control, control_finish, base_prepare
    )

    def base_finish():
        other = swap_rows(third, base_only)
        residue, keyval, query = kernel_call(
            middle_kernel,
            [(tile_shape, jnp.bfloat16)] + projections,
            (
                spot, own, far, side, corner, near, cross, out_mine, out_other, first, first_other,
                zero_side, zero_corner, modulation[1], modulation[0],
            ),
            scratch=[
                rows_shape,
                ((D, D), jnp.bfloat16),
                ((2 * half + lanes, D), jnp.bfloat16),
                both_shape,
            ],
            micros=8, near=True, room=32,
        )
        outer, inner = halos(keyval, base_only)
        attended = neighborhood(query, keyval, outer, inner)
        side_heads = their_heads(attended, base_only)
        return attended, side_heads, head_rows(1, third, other), residue

    attended, side_heads, rows, more = lax.cond(
        is_control, lambda: (attended, side_heads, rows, far), base_finish
    )
    mod = jnp.where(is_control, modulation[1], modulation[0])
    out = finished(attended, side_heads, rows, more, mod)
    return out.reshape(latent.shape)


def solution(mesh):
    placed = (
        P("branch", None, "trow", "tcol", None),
        P(),
        P("branch", None, "tcol"),
        P("branch", None, "tcol"),
        P("branch", "tcol", None),
        P(None, "tcol"),
    )
    sizes = (mesh.shape["branch"], mesh.shape["trow"], mesh.shape["tcol"])
    body = on_device
    if sizes == (2, 2, HEADS):
        body = functools.partial(paired_rows, sizes)
    return jax.shard_map(
        body,
        mesh=mesh,
        in_specs=placed,
        out_specs=P("branch", None, "trow", "tcol", None),
        check_vma=False,
    )
```
